32 devices in a mesh: section: 2 (over core), dp: 16 (over z, y, x).
Axes of the slice: x: 2, y: 2, z: 4, core: 2. Of those that a mesh axis runs over, the one named last changes fastest.
Arguments:
- captions: bfloat16 [1024, 16, 768], P('dp'), may hold values from -6 to 6
- caption_lengths: int32 [1024], P('dp'), may hold values from 1 to 16
- caption_cotangent: bfloat16 [1024, 16, 768], P('dp'), may hold values from -6 to 6
- first_gain: bfloat16 [768], replicated, may hold values from 0.5 to 1.5
- first_shift: bfloat16 [768], replicated, may hold values from -1.75 to 1.75
- project_in: bfloat16 [768, 2304], replicated, may hold values from -0.21875 to 0.21875
- inward_bias: bfloat16 [1536], replicated, may hold values from -1.75 to 1.75
- project_out: bfloat16 [768, 768], replicated, may hold values from -0.625 to 0.625
- outward_bias: bfloat16 [768], replicated, may hold values from -1.75 to 1.75
- second_gain: bfloat16 [768], replicated, may hold values from 0.5 to 1.5
- second_shift: bfloat16 [768], replicated, may hold values from -1.75 to 1.75
- expand_weight: bfloat16 [768, 3072], replicated, may hold values from -0.21875 to 0.21875
- expand_bias: bfloat16 [3072], replicated, may hold values from -1.75 to 1.75
- reduce_weight: bfloat16 [3072, 768], replicated, may hold values from -0.109375 to 0.109375
- reduce_bias: bfloat16 [768], replicated, may hold values from -1.75 to 1.75
- patches: bfloat16 [512, 50, 768], P(('section', 'dp')), may hold values from -6 to 6
- vision_first_gain: bfloat16 [768], replicated, may hold values from 0.5 to 1.5
- vision_first_shift: bfloat16 [768], replicated, may hold values from -1.75 to 1.75
- vision_project_in: bfloat16 [768, 2304], replicated, may hold values from -0.21875 to 0.21875
- vision_inward_bias: bfloat16 [1536], replicated, may hold values from -1.75 to 1.75
- vision_project_out: bfloat16 [768, 768], replicated, may hold values from -0.625 to 0.625
- vision_outward_bias: bfloat16 [768], replicated, may hold values from -1.75 to 1.75
- vision_second_gain: bfloat16 [768], replicated, may hold values from 0.5 to 1.5
- vision_second_shift: bfloat16 [768], replicated, may hold values from -1.75 to 1.75
- vision_expand_weight: bfloat16 [768, 3072], replicated, may hold values from -0.21875 to 0.21875
- vision_expand_bias: bfloat16 [3072], replicated, may hold values from -1.75 to 1.75
- vision_reduce_weight: bfloat16 [3072, 768], replicated, may hold values from -0.109375 to 0.109375
- vision_reduce_bias: bfloat16 [768], replicated, may hold values from -1.75 to 1.75
Outputs:
- vision_output: bfloat16 [512, 50, 768], P(('section', 'dp'))
- caption_output: bfloat16 [1024, 16, 768], P('dp', None, 'section')
- captions_gradient: bfloat16 [1024, 16, 768], P('dp', None, 'section')
- first_gain_gradient: float32 [768], P('dp')
- first_shift_gradient: float32 [768], P('dp')
- project_in_gradient: float32 [768, 2304], P('dp')
- inward_bias_gradient: float32 [1536], P('dp')
- project_out_gradient: float32 [768, 768], P('dp')
- outward_bias_gradient: float32 [768], P('dp')
- second_gain_gradient: float32 [768], P('dp')
- second_shift_gradient: float32 [768], P('dp')
- expand_weight_gradient: float32 [768, 3072], P('dp')
- expand_bias_gradient: float32 [3072], P('dp')
- reduce_weight_gradient: float32 [3072, 768], P('dp')
- reduce_bias_gradient: float32 [768], P('dp')
The draws below stay inside these ranges and needn't reach their ends.
Inputs may be any that keep to these rules, and one draw needn't show every extreme that they name: `caption_lengths`: each caption's used slots are its first ones.
All inputs are finite; a program needn't handle non-finite values.
Results may differ from the reference program's by a relative error of at most 0.01.
Values may be sent and summed in bfloat16 or wider, within the bound.
No kernel may reach another device: no remote copies, remote signals or barrier semaphores. Data moves between devices by JAX's collectives and lax.ppermute only.
A program may use at most 256 MiB of HBM per device.

```python
import math
import jax
import jax.numpy as jnp
from jax import lax

D = 768
FF = 3072
HEAD_DIM = 64
SEQ = 16
PATCHES = 50
CAPTIONS = 1024
IMAGES = 512


def with_ends(drawn, stream_key, smallest, top_value):
    longest = drawn.shape.index(max(drawn.shape))
    spots = []
    for shift in (0, 1):
        where = [jax.random.randint(jax.random.fold_in(stream_key, axis), (), 0, length) for axis, length in enumerate(drawn.shape)]
        where[longest] = (where[longest] + shift) % drawn.shape[longest]
        spots.append(tuple(where))
    return drawn.at[spots[0]].set(smallest).at[spots[1]].set(top_value)


def level_of(own_key, shape, cuts, low, top_value):
    def one(position, parts):
        heights = jax.random.uniform(jax.random.fold_in(jax.random.fold_in(own_key, 6), position), (parts,), jnp.float32, low / len(cuts), top_value / len(cuts))
        return jnp.repeat(jnp.exp(heights), shape[position] // parts).reshape((-1,) + (1,) * (len(shape) - position - 1))

    level = one(*cuts[0])
    for cut in cuts[1:]:
        level = level * one(*cut)
    return level


def noise(key, dims, spread, reach, shards=(), held_as=jnp.bfloat16):
    factor_of = level_of(key, dims, shards, -0.22, 0.18) if shards else 1.0
    entries = jax.random.normal(key, dims, jnp.float32) * spread * factor_of
    return jnp.minimum(jnp.maximum(entries, -reach), reach).astype(held_as)


def setup_inputs(seed: int = 0) -> dict:
    key_list = jax.random.split(jax.random.key(seed), 29)
    captions = noise(key_list[0], (CAPTIONS, SEQ, D), 1.0, 6.0, ((0, 16),))
    caption_lengths = with_ends(jax.random.randint(key_list[1], (CAPTIONS,), 1, SEQ + 1), jax.random.fold_in(key_list[1], 1), 1, SEQ).astype(jnp.int32)
    caption_cotangent = noise(key_list[2], (CAPTIONS, SEQ, D), 1.0, 6.0, ((0, 16),))
    first_gain = jnp.clip(1.0 + 0.1 * jax.random.normal(key_list[3], (D,), jnp.float32), 0.5, 1.5).astype(jnp.bfloat16)
    first_shift = noise(key_list[4], (D,), 0.3, 1.75)
    project_in = noise(key_list[5], (D, 3 * D), D ** -0.5, 0.21875)
    inward_bias = noise(key_list[6], (2 * D,), 0.3, 1.75)
    project_out = noise(key_list[7], (D, D), (D // 8) ** -0.5, 0.625)
    outward_bias = noise(key_list[8], (D,), 0.3, 1.75)
    second_gain = jnp.clip(1.0 + 0.1 * jax.random.normal(key_list[9], (D,), jnp.float32), 0.5, 1.5).astype(jnp.bfloat16)
    second_shift = noise(key_list[10], (D,), 0.3, 1.75)
    expand_weight = noise(key_list[11], (D, FF), D ** -0.5, 0.21875)
    expand_bias = noise(key_list[12], (FF,), 0.3, 1.75)
    reduce_weight = noise(key_list[13], (FF, D), FF ** -0.5, 0.109375)
    reduce_bias = noise(key_list[14], (D,), 0.3, 1.75)
    patches = noise(key_list[15], (IMAGES, PATCHES, D), 1.0, 6.0, ((0, 32),))
    vision_first_gain = jnp.clip(1.0 + 0.1 * jax.random.normal(key_list[16], (D,), jnp.float32), 0.5, 1.5).astype(jnp.bfloat16)
    vision_first_shift = noise(key_list[17], (D,), 0.3, 1.75)
    vision_project_in = noise(key_list[18], (D, 3 * D), D ** -0.5, 0.21875)
    vision_inward_bias = noise(key_list[19], (2 * D,), 0.3, 1.75)
    vision_project_out = noise(key_list[20], (D, D), (D // 8) ** -0.5, 0.625)
    vision_outward_bias = noise(key_list[21], (D,), 0.3, 1.75)
    vision_second_gain = jnp.clip(1.0 + 0.1 * jax.random.normal(key_list[22], (D,), jnp.float32), 0.5, 1.5).astype(jnp.bfloat16)
    vision_second_shift = noise(key_list[23], (D,), 0.3, 1.75)
    vision_expand_weight = noise(key_list[24], (D, FF), D ** -0.5, 0.21875)
    vision_expand_bias = noise(key_list[25], (FF,), 0.3, 1.75)
    vision_reduce_weight = noise(key_list[26], (FF, D), FF ** -0.5, 0.109375)
    vision_reduce_bias = noise(key_list[27], (D,), 0.3, 1.75)
    return {"captions": captions, "caption_lengths": caption_lengths, "caption_cotangent": caption_cotangent, "first_gain": first_gain, "first_shift": first_shift, "project_in": project_in, "inward_bias": inward_bias, "project_out": project_out, "outward_bias": outward_bias, "second_gain": second_gain, "second_shift": second_shift, "expand_weight": expand_weight, "expand_bias": expand_bias, "reduce_weight": reduce_weight, "reduce_bias": reduce_bias, "patches": patches, "vision_first_gain": vision_first_gain, "vision_first_shift": vision_first_shift, "vision_project_in": vision_project_in, "vision_inward_bias": vision_inward_bias, "vision_project_out": vision_project_out, "vision_outward_bias": vision_outward_bias, "vision_second_gain": vision_second_gain, "vision_second_shift": vision_second_shift, "vision_expand_weight": vision_expand_weight, "vision_expand_bias": vision_expand_bias, "vision_reduce_weight": vision_reduce_weight, "vision_reduce_bias": vision_reduce_bias}


EPSILON = 1e-06
MASKED = -1000000000.0
HIGHEST = lax.Precision.HIGHEST

@jax.custom_vjp
def low(v):
    return lax.optimization_barrier(v.astype(jnp.bfloat16)).astype(jnp.float32)

@jax.custom_vjp
def low_back(v):
    return v

def low_keep(v):
    return (low(v), None)

def low_pass(kept, grad):
    return (grad,)

def back_keep(v):
    return (v, None)

def back_low(kept, grad):
    return (low(grad),)
low.defvjp(low_keep, low_pass)
low_back.defvjp(back_keep, back_low)

def unchanged(value):
    return value

def normalize(source, gain, shift):
    average = lax.optimization_barrier(jnp.mean(source, axis=-1, keepdims=True))
    centred = source - average
    variance = lax.optimization_barrier(jnp.mean(centred * centred, axis=-1, keepdims=True))
    return centred * lax.rsqrt(variance + EPSILON) * gain + shift

def attend_part(block, allowed, weights, back):
    gain, shift, project_in, inward_bias, project_out, outward_bias = weights
    count, length, width = block.shape
    scale = HEAD_DIM ** (-0.5)
    normed = low(normalize(block, gain, shift))
    full_bias = jnp.concatenate([inward_bias[:width], jnp.zeros((width,), jnp.float32), inward_bias[width:]])
    packed = low(back(jnp.dot(normed, project_in, precision=HIGHEST) + full_bias))
    split = packed.reshape(count, length, 3, width // HEAD_DIM, HEAD_DIM)
    scores = back(jnp.einsum('bqhd,bkhd->bhqk', split[:, :, 0], split[:, :, 1], precision=HIGHEST) * scale)
    scores = jnp.where(allowed[:, None, None, :], scores, MASKED)
    peak = lax.optimization_barrier(jnp.max(scores, axis=-1, keepdims=True))
    powered = jnp.exp(scores - peak)
    probs = low(powered / lax.optimization_barrier(jnp.sum(powered, axis=-1, keepdims=True)))
    context = jnp.einsum('bhqk,bkhd->bqhd', probs, split[:, :, 2], precision=HIGHEST)
    context = low(back(context.reshape(count, length, width)))
    return block + back(jnp.dot(context, project_out, precision=HIGHEST) + outward_bias)

def expand_part(middle, weights, back):
    gain, shift, expand_weight, expand_bias, reduce_weight, reduce_bias = weights
    normed = low(normalize(middle, gain, shift))
    hidden = back(jnp.dot(normed, expand_weight, precision=HIGHEST) + expand_bias)
    active = low(jax.nn.gelu(hidden, approximate=True))
    return middle + back(jnp.dot(active, reduce_weight, precision=HIGHEST) + reduce_bias)

def text_forward(block, lengths, weights):
    positions = jnp.arange(SEQ)
    allowed = positions[None, :] < lengths[:, None]
    middle = attend_part(block, allowed, weights[:6], low_back)
    middle = low(low_back(middle))
    return expand_part(middle, weights[6:], low_back)

def reference(captions, caption_lengths, caption_cotangent, first_gain, first_shift, project_in, inward_bias, project_out, outward_bias, second_gain, second_shift, expand_weight, expand_bias, reduce_weight, reduce_bias, patches, vision_first_gain, vision_first_shift, vision_project_in, vision_inward_bias, vision_project_out, vision_outward_bias, vision_second_gain, vision_second_shift, vision_expand_weight, vision_expand_bias, vision_reduce_weight, vision_reduce_bias):
    text_weights = tuple((value.astype(jnp.float32) for value in (first_gain, first_shift, project_in, inward_bias, project_out, outward_bias, second_gain, second_shift, expand_weight, expand_bias, reduce_weight, reduce_bias)))
    block_count = math.gcd(CAPTIONS, 256)
    step_count = CAPTIONS // block_count
    sources = captions.astype(jnp.float32).reshape(step_count, block_count, SEQ, D)
    lengths_all = caption_lengths.reshape(step_count, block_count)
    cotangents = caption_cotangent.astype(jnp.float32).reshape(step_count, block_count, SEQ, D)

    def advance(totals, pieces):
        block, lengths, cotangent = pieces

        def closed(source, weights):
            return text_forward(source, lengths, weights)
        result, pullback = jax.vjp(closed, block, text_weights)
        block_gradient, weight_gradients = pullback(cotangent)
        totals = tuple((a + b for a, b in zip(totals, weight_gradients)))
        return (totals, (result.astype(jnp.bfloat16), block_gradient.astype(jnp.bfloat16)))
    starting = tuple((jnp.zeros(value.shape, jnp.float32) for value in text_weights))
    totals, (results, gradients) = lax.scan(advance, starting, (sources, lengths_all, cotangents))
    caption_output = results.reshape(CAPTIONS, SEQ, D)
    captions_gradient = gradients.reshape(CAPTIONS, SEQ, D)
    vision_weights = tuple((value.astype(jnp.float32) for value in (vision_first_gain, vision_first_shift, vision_project_in, vision_inward_bias, vision_project_out, vision_outward_bias, vision_second_gain, vision_second_shift, vision_expand_weight, vision_expand_bias, vision_reduce_weight, vision_reduce_bias)))
    image_count = math.gcd(IMAGES, 64)
    vision_sources = patches.astype(jnp.float32).reshape(IMAGES // image_count, image_count, PATCHES, D)

    def vision_step(block):
        allowed = jnp.ones((image_count, PATCHES), jnp.bool_)
        middle = attend_part(block, allowed, vision_weights[:6], unchanged)
        return expand_part(middle, vision_weights[6:], unchanged).astype(jnp.bfloat16)
    vision_output = lax.map(vision_step, vision_sources).reshape(IMAGES, PATCHES, D)
    return (vision_output, caption_output, captions_gradient, totals[0], totals[1], totals[2], totals[3], totals[4], totals[5], totals[6], totals[7], totals[8], totals[9], totals[10], totals[11])
```

```python
from functools import partial

import jax
import jax.experimental.pallas as pl
import jax.numpy as jnp
from jax import lax
from jax.experimental.pallas import tpu as pltpu
from jax.sharding import PartitionSpec as P

HEAD_DIM = 64
GROUP = 128
EPSILON = 1e-06
MASKED = -1000000000.0
ROOT = 0.7978845608028654
CUBIC = 0.044715
F32 = jnp.float32
BF16 = jnp.bfloat16
MIB = 1024 * 1024


def nn(a, b):
    return lax.dot_general(a, b, (((1,), (0,)), ((), ())), preferred_element_type=F32)


def nt(a, b):
    return lax.dot_general(a, b, (((1,), (1,)), ((), ())), preferred_element_type=F32)


def tn(a, b):
    return lax.dot_general(a, b, (((0,), (0,)), ((), ())), preferred_element_type=F32)


def row(ref):
    return ref[...].astype(F32).reshape(1, -1)


def units(x):
    average = jnp.mean(x, axis=-1, keepdims=True)
    centred = x - average
    variance = jnp.mean(centred * centred, axis=-1, keepdims=True)
    inverse = lax.rsqrt(variance + EPSILON)
    return centred * inverse, inverse


def norm_back(unit, inverse, gain, dy):
    du = dy * gain
    first = jnp.mean(du, axis=-1, keepdims=True)
    second = jnp.mean(du * unit, axis=-1, keepdims=True)
    return (du - first - unit * second) * inverse


def lane_block(slots, rows):
    return lax.broadcasted_iota(jnp.int32, (rows, GROUP), 1) // slots


def two_heads(a):
    lanes = lax.broadcasted_iota(jnp.int32, a.shape, 1)
    low = (lanes < HEAD_DIM).astype(F32).astype(BF16)
    high = (lanes >= HEAD_DIM).astype(F32).astype(BF16)
    return jnp.concatenate([a * low, a * high], axis=0)


def compact(full, slots):
    block = lane_block(slots, slots)
    out = full[:slots]
    for b in range(1, GROUP // slots):
        out = jnp.where(block == b, full[b * slots : (b + 1) * slots], out)
    return out


def spread(part, slots):
    block = lane_block(slots, slots)
    return jnp.concatenate(
        [part * (block == b).astype(F32).astype(BF16) for b in range(GROUP // slots)], axis=0
    )


def attention(q, k, v, allowed, slots):
    scores = nt(two_heads(k), q)
    probs = []
    for a in range(2):
        s = compact(scores[a * GROUP : (a + 1) * GROUP], slots) * (HEAD_DIM**-0.5)
        s = jnp.where(allowed, s, MASKED)
        powered = jnp.exp(s - jnp.max(s, axis=0, keepdims=True))
        probs.append(powered / jnp.sum(powered, axis=0, keepdims=True))
    wide = jnp.concatenate([spread(p.astype(BF16), slots) for p in probs], axis=0)
    return tn(wide, two_heads(v)).astype(BF16), probs


def attention_back(q, k, v, probs, dc, slots):
    vv, kk, qq, dd = two_heads(v), two_heads(k), two_heads(q), two_heads(dc)
    dprobs = nt(vv, dc)
    wide_p, wide_s = [], []
    for a in range(2):
        dp = compact(dprobs[a * GROUP : (a + 1) * GROUP], slots)
        p = probs[a]
        ds = p * (dp - jnp.sum(p * dp, axis=0, keepdims=True))
        wide_p.append(spread(p.astype(BF16), slots))
        wide_s.append(spread(ds.astype(BF16), slots))
    dv = nn(jnp.concatenate(wide_p, axis=1), dd)
    dk = nn(jnp.concatenate(wide_s, axis=1), qq)
    dq = tn(jnp.concatenate(wide_s, axis=0), kk)
    scale = HEAD_DIM**-0.5
    return (dq * scale).astype(BF16), (dk * scale).astype(BF16), dv.astype(BF16)


def project(n1, win_ref, bias, packed_ref):
    width = n1.shape[1]
    for t in range(3):
        part = nn(n1, win_ref[:, t * width : (t + 1) * width])
        if t != 1:
            half = 0 if t == 0 else width
            part = part + bias[:, half : half + width]
        packed_ref[:, t * width : (t + 1) * width] = part.astype(BF16)


def attend_forward(
    info, lens, x_ref, g_ref, s_ref, win_ref, bi_ref, wo_ref, bo_ref,
    mid_ref, ctx_ref, n1_ref, pk_ref, pc_ref, *, slots,
):
    rows, width = x_ref.shape
    x = x_ref[...].astype(F32)
    unit, _ = units(x)
    n1 = (unit * row(g_ref) + row(s_ref)).astype(BF16)
    n1_ref[...] = n1
    project(n1, win_ref, row(bi_ref), pk_ref)
    block = lane_block(slots, 1)
    slot = lax.broadcasted_iota(jnp.int32, (slots, GROUP), 0)
    start = (info[0] * pl.num_programs(0) + pl.program_id(0)) * (rows // slots)
    for g in range(rows // GROUP):
        used = jnp.zeros((1, GROUP), jnp.int32)
        for b in range(GROUP // slots):
            used = jnp.where(block == b, lens[start + g * (GROUP // slots) + b], used)
        allowed = slot < used
        tokens = slice(g * GROUP, (g + 1) * GROUP)
        for p in range(width // 128):
            q, k, v = (pk_ref[tokens, t * width + p * 128 : t * width + (p + 1) * 128] for t in range(3))
            ctx, probs = attention(q, k, v, allowed, slots)
            ctx_ref[tokens, p * 128 : (p + 1) * 128] = ctx
            for a in range(2):
                pc_ref[(2 * p + a) * slots : (2 * p + a + 1) * slots, tokens] = probs[a]
    mid_ref[...] = (x + (nn(ctx_ref[...], wo_ref[...]) + row(bo_ref))).astype(BF16)


def expand_forward(
    info, own_ref, oth_ref, cot_ref, g_ref, s_ref, we_ref, be_ref, wr_ref, br_ref,
    n2_ref, slope_ref, keep_ref, send_ref, outk_ref, outs_ref, mid, acc, act, *, chunk,
):
    step = pl.program_id(0)
    tokens, width = cot_ref.shape
    half = own_ref.shape[0]
    c = info[0]

    @pl.when(step == 0)
    def _():
        mid[pl.ds(pl.multiple_of(c * half, half), half), :] = own_ref[...]
        mid[pl.ds(pl.multiple_of((1 - c) * half, half), half), :] = oth_ref[...]
        for t in range(0, tokens, chunk):
            unit, _ = units(mid[t : t + chunk].astype(F32))
            n2_ref[t : t + chunk] = (unit * row(g_ref) + row(s_ref)).astype(BF16)
            acc[t : t + chunk] = jnp.zeros((chunk, width), F32)

    for t in range(0, tokens, chunk):
        h = nn(n2_ref[t : t + chunk], we_ref[...]) + row(be_ref)
        square = h * h
        th = jnp.tanh(ROOT * (h + CUBIC * (square * h)))
        gate = 0.5 * (1.0 + th)
        active = (h * gate).astype(BF16)
        slope = gate + (0.5 * h) * (1.0 - th * th) * (ROOT + (3.0 * CUBIC * ROOT) * square)
        act[t : t + chunk] = active
        slope_ref[t : t + chunk] = slope.astype(BF16)
        acc[t : t + chunk] += nn(active, wr_ref[...])
    grad = tn(act[...], cot_ref[...]).astype(BF16)
    short = grad.shape[0] // 2

    @pl.when(info[1] == 0)
    def _():
        keep_ref[0] = grad[:short]
        send_ref[0] = grad[short:]

    @pl.when(info[1] == 1)
    def _():
        keep_ref[0] = grad[short:]
        send_ref[0] = grad[:short]

    def finish(mine, others):
        bias = row(br_ref)
        outk_ref[...] = mid[:, mine].astype(F32) + (acc[:, mine] + bias[:, mine])
        outs_ref[...] = acc[:, others].astype(BF16)

    @pl.when((step == pl.num_programs(0) - 1) & (c == 0))
    def _():
        finish(slice(0, width // 2), slice(width // 2, width))

    @pl.when((step == pl.num_programs(0) - 1) & (c == 1))
    def _():
        finish(slice(width // 2, width), slice(0, width // 2))


def split_rows(grad, first, second, bit):
    short = grad.shape[0] // (2 * first.shape[0])

    def store(at, take):
        for z in range(first.shape[0]):
            begin = (2 * z + take) * short
            at[z] = grad[begin : begin + short]

    @pl.when(bit == 0)
    def _():
        store(first, 0)
        store(second, 1)

    @pl.when(bit == 1)
    def _():
        store(first, 1)
        store(second, 0)


def expand_backward(
    info, n2_ref, slope_ref, cot_ref, we_ref, wr_ref,
    keep_ref, send_ref, db_ref, dk_ref, ds_ref, acc, dh, *, chunk,
):
    step = pl.program_id(0)
    tokens, width = cot_ref.shape
    half = dk_ref.shape[0]
    c = info[0]

    @pl.when(step == 0)
    def _():
        acc[...] = jnp.zeros(acc.shape, F32)

    total = jnp.zeros((1, slope_ref.shape[1]), F32)
    for t in range(0, tokens, chunk):
        da = nt(cot_ref[t : t + chunk], wr_ref[...])
        low = (da * slope_ref[t : t + chunk].astype(F32)).astype(BF16)
        dh[t : t + chunk] = low
        total = total + jnp.sum(low.astype(F32), axis=0, keepdims=True)
        acc[t : t + chunk] += nt(low, we_ref[...])
    db_ref[0] = total
    split_rows(tn(n2_ref[...], dh[...]).astype(BF16), keep_ref, send_ref, info[2])

    @pl.when(step == pl.num_programs(0) - 1)
    def _():
        dk_ref[...] = acc[pl.ds(pl.multiple_of(c * half, half), half), :]
        ds_ref[...] = acc[pl.ds(pl.multiple_of((1 - c) * half, half), half), :].astype(BF16)


def attend_backward(
    info, dn_ref, da_ref, mid_ref, cot_ref, g_ref, wo_ref, pk_ref, pc_ref,
    mgk_ref, mgs_ref, dpk_ref, dps_ref, sums_ref, dctx, dpk, *, slots,
):
    rows, width = mid_ref.shape
    cot = cot_ref[...].astype(F32)
    unit, inverse = units(mid_ref[...].astype(F32))
    dn = dn_ref[...] + da_ref[...].astype(F32)
    mg = (cot + norm_back(unit, inverse, row(g_ref), dn)).astype(BF16)
    dctx[...] = nt(mg, wo_ref[...]).astype(BF16)
    for g in range(rows // GROUP):
        tokens = slice(g * GROUP, (g + 1) * GROUP)
        for p in range(width // 128):
            q, k, v = (pk_ref[tokens, t * width + p * 128 : t * width + (p + 1) * 128] for t in range(3))
            probs = [pc_ref[(2 * p + a) * slots : (2 * p + a + 1) * slots, tokens] for a in range(2)]
            grads = attention_back(q, k, v, probs, dctx[tokens, p * 128 : (p + 1) * 128], slots)
            for t in range(3):
                dpk[tokens, t * width + p * 128 : t * width + (p + 1) * 128] = grads[t]

    def total(a):
        return jnp.sum(a, axis=0, keepdims=True)

    sums = [
        total(dn * unit),
        total(dn),
        total(mg.astype(F32)),
        total(cot),
        total(dpk[:, :width].astype(F32)),
        total(dpk[:, 2 * width :].astype(F32)),
    ]
    sums = jnp.concatenate(sums + [jnp.zeros((2, width), F32)], axis=0)

    @pl.when(pl.program_id(0) == 0)
    def _():
        sums_ref[...] = sums

    @pl.when(pl.program_id(0) > 0)
    def _():
        sums_ref[...] += sums

    wide = 3 * width // 2

    @pl.when(info[0] == 0)
    def _():
        mgk_ref[...] = mg[:, : width // 2]
        mgs_ref[...] = mg[:, width // 2 :]
        dpk_ref[...] = dpk[:, :wide]
        dps_ref[...] = dpk[:, wide:]

    @pl.when(info[0] == 1)
    def _():
        mgk_ref[...] = mg[:, width // 2 :]
        mgs_ref[...] = mg[:, : width // 2]
        dpk_ref[...] = dpk[:, wide:]
        dps_ref[...] = dpk[:, :wide]


def attend_weights(
    info, n1k, n1o, dpk, dpo, ctk, cto, mgk, mgo, k1, s1, k2, s2,
):
    block = mgk.shape[1]
    per = k1.shape[2] // block
    for j in range(4):
        cols = slice(j * block, (j + 1) * block)
        if j < 3:
            grad = tn(n1k[...], dpk[:, cols]) + tn(n1o[...], dpo[:, cols])
        else:
            grad = tn(ctk[...], mgk[...]) + tn(cto[...], mgo[...])
        place = slice((j % per) * block, (j % per + 1) * block)
        first, second, bit = (k1, s1, info[1]) if j < per else (k2, s2, info[2])
        split_rows(grad.astype(BF16), first.at[:, :, place], second.at[:, :, place], bit)


def input_backward(
    info, x_ref, g_ref, winc_ref, wino_ref, dpk, dps, mgk, mgs,
    cgk_ref, cgs_ref, sums_ref,
):
    width = x_ref.shape[1]
    unit, inverse = units(x_ref[...].astype(F32))
    dn = nt(dpk[...], winc_ref[...]) + nt(dps[...], wino_ref[...])
    dv = norm_back(unit, inverse, row(g_ref), dn)
    sums = jnp.concatenate(
        [
            jnp.sum(dn * unit, axis=0, keepdims=True),
            jnp.sum(dn, axis=0, keepdims=True),
            jnp.zeros((6, width), F32),
        ],
        axis=0,
    )

    @pl.when(pl.program_id(0) == 0)
    def _():
        sums_ref[...] = sums

    @pl.when(pl.program_id(0) > 0)
    def _():
        sums_ref[...] += sums

    half = width // 2

    def store(mine, others):
        cgk_ref[...] = (dv[:, mine] + mgk[...].astype(F32)).astype(BF16)
        cgs_ref[...] = (dv[:, others] + mgs[...].astype(F32)).astype(BF16)

    @pl.when(info[0] == 0)
    def _():
        store(slice(0, half), slice(half, width))

    @pl.when(info[0] == 1)
    def _():
        store(slice(half, width), slice(0, half))


def vision_attend(
    x_ref, g_ref, s_ref, win_ref, bi_ref, wo_ref, bo_ref, mid_ref, xs, pk, ctx, *, slots
):
    images, used, width = x_ref.shape
    xs[...] = jnp.zeros(xs.shape, F32)
    for i in range(images):
        xs[i * slots : i * slots + used] = x_ref[i].astype(F32)
    x = xs[...]
    unit, _ = units(x)
    n1 = (unit * row(g_ref) + row(s_ref)).astype(BF16)
    project(n1, win_ref, row(bi_ref), pk)
    allowed = lax.broadcasted_iota(jnp.int32, (slots, GROUP), 0) < used
    for g in range(images * slots // GROUP):
        tokens = slice(g * GROUP, (g + 1) * GROUP)
        for p in range(width // 128):
            q, k, v = (pk[tokens, t * width + p * 128 : t * width + (p + 1) * 128] for t in range(3))
            out, _ = attention(q, k, v, allowed, slots)
            ctx[tokens, p * 128 : (p + 1) * 128] = out
    mid_ref[...] = x + (nn(ctx[...], wo_ref[...]) + row(bo_ref))


def vision_expand(*refs, chunk, slots):
    mid_ref, g_ref, s_ref, we_ref, be_ref, wr_ref, br_ref = refs[:7]
    out_ref, n2, acc = refs[-3:]
    step = pl.program_id(0)
    tokens = mid_ref.shape[0]

    @pl.when(step == 0)
    def _():
        for t in range(0, tokens, chunk):
            m = mid_ref[t : t + chunk]
            unit, _ = units(m)
            n2[t : t + chunk] = (unit * row(g_ref) + row(s_ref)).astype(BF16)
            acc[t : t + chunk] = m + row(br_ref)

    for t in range(0, tokens, chunk):
        h = nn(n2[t : t + chunk], we_ref[...]) + row(be_ref)
        th = jnp.tanh(ROOT * (h + CUBIC * (h * h * h)))
        active = (0.5 * h * (1.0 + th)).astype(BF16)
        acc[t : t + chunk] += nn(active, wr_ref[...])

    @pl.when(step == pl.num_programs(0) - 1)
    def _():
        used = out_ref.shape[1]
        for i in range(out_ref.shape[0]):
            out_ref[i] = acc[i * slots : i * slots + used].astype(BF16)


def shape(dims, dtype=BF16):
    return jax.ShapeDtypeStruct(dims, dtype)


def whole(dims):
    return pl.BlockSpec(dims, lambda *_: (0,) * len(dims))


def kernel(body, name, grid, ins, outs, scratch, flops, args, scalars=(), aliases=None):
    specs = pltpu.PrefetchScalarGridSpec(
        num_scalar_prefetch=len(scalars),
        grid=grid,
        in_specs=ins,
        out_specs=[o[0] for o in outs],
        scratch_shapes=scratch,
    )
    moved = sum(a.size * a.dtype.itemsize for a in args)
    moved += sum(o[1].size * o[1].dtype.itemsize for o in outs)
    return pl.pallas_call(
        body,
        name=name,
        grid_spec=specs,
        out_shape=[o[1] for o in outs],
        compiler_params=pltpu.CompilerParams(
            vmem_limit_bytes=52 * MIB, dimension_semantics=("arbitrary",) * len(grid)
        ),
        cost_estimate=pl.CostEstimate(flops=int(flops), bytes_accessed=moved, transcendentals=0),
        input_output_aliases=aliases or {},
    )(*scalars, *args)


def on_device(
    captions, caption_lengths, caption_cotangent,
    first_gain, first_shift, project_in, inward_bias, project_out, outward_bias,
    second_gain, second_shift, expand_weight, expand_bias, reduce_weight, reduce_bias,
    patches,
    vision_first_gain, vision_first_shift, vision_project_in, vision_inward_bias, vision_project_out, vision_outward_bias,
    vision_second_gain, vision_second_shift, vision_expand_weight, vision_expand_bias, vision_reduce_weight, vision_reduce_bias,
):
    count, slots, width = captions.shape
    hidden = expand_weight.shape[1]
    tokens = count * slots
    own = tokens // 2
    half = width // 2
    piece = hidden // 8
    wide = 3 * half
    heads = width // HEAD_DIM
    ranks = lax.axis_size("dp")
    low = (ranks // 16).bit_length() - 1
    core = lax.axis_index("section")
    place = lax.axis_index("dp")
    bits = [(place >> (low + b)) & 1 for b in range(4)]
    info = jnp.stack([core, bits[0], bits[1]]).astype(jnp.int32)
    x = captions.reshape(tokens, width)
    cot = caption_cotangent.reshape(tokens, width)

    def hop(value, bit, only=None):
        step = 1 << (low + bit)
        pairs = []
        for k in range(2):
            for d in range(ranks):
                if only is None or only(k, (d >> (low + 1)) & 1):
                    pairs.append((k * ranks + d, k * ranks + (d ^ step)))
        return lax.ppermute(value, ("section", "dp"), pairs)

    def swap(value):
        return lax.ppermute(value, "section", [(0, 1), (1, 0)])

    block = 256
    steps = own // block
    mine = lambda i, info, *_: (info[0] * steps + i, 0)
    at = lambda i, *_: (i, 0)
    middle, context, normed, packed, probs = kernel(
        partial(attend_forward, slots=slots), "caption_attention", (steps,),
        [pl.BlockSpec((block, width), mine), whole((width,)), whole((width,)), whole(project_in.shape),
         whole(inward_bias.shape), whole(project_out.shape), whole((width,))],
        [(pl.BlockSpec((block, width), at), shape((own, width))),
         (pl.BlockSpec((block, width), at), shape((own, width))),
         (pl.BlockSpec((block, width), at), shape((own, width))),
         (pl.BlockSpec((block, 3 * width), at), shape((own, 3 * width))),
         (pl.BlockSpec((heads * slots, block), lambda i, *_: (0, i)), shape((heads * slots, own), F32))],
        [], 2 * own * width * width * 4 * 1.3,
        (x, first_gain, first_shift, project_in, inward_bias, project_out, outward_bias),
        (info, caption_lengths),
    )
    middle_far = swap(middle)

    unit_block = lambda j, info: (0, 2 * j + info[0])
    unit_rows = lambda j, info: (2 * j + info[0], 0)
    zrow = lambda j, info: (j, 0, 0)
    n2, slope, a_keep, a_send, out_keep, out_send = kernel(
        partial(expand_forward, chunk=256), "caption_mlp_forward", (4,),
        [whole((own, width)), whole((own, width)), whole((tokens, width)), whole((width,)), whole((width,)),
         pl.BlockSpec((width, piece), unit_block), pl.BlockSpec((1, 1, piece), lambda j, info: (2 * j + info[0], 0, 0)),
         pl.BlockSpec((piece, width), unit_rows), whole((width,))],
        [(whole((tokens, width)), shape((tokens, width))),
         (pl.BlockSpec((tokens, piece), lambda j, info: (0, j)), shape((tokens, 4 * piece))),
         (pl.BlockSpec((1, piece // 2, width), zrow), shape((4, piece // 2, width))),
         (pl.BlockSpec((1, piece // 2, width), zrow), shape((4, piece // 2, width))),
         (whole((tokens, half)), shape((tokens, half), F32)),
         (whole((tokens, half)), shape((tokens, half)))],
        [pltpu.VMEM((tokens, width), BF16), pltpu.VMEM((tokens, width), F32), pltpu.VMEM((tokens, piece), BF16)],
        2 * tokens * width * hidden // 2 * 3,
        (middle, middle_far, cot, second_gain, second_shift, expand_weight, expand_bias.reshape(8, 1, piece), reduce_weight, reduce_bias),
        (info,),
    )
    context_far = swap(context)
    normed_far = swap(normed)
    out_far = swap(out_send)
    a_far = hop(a_send, 0)

    rows = width // 8
    b_keep, b_send, bias_part, dn_keep, dn_send = kernel(
        partial(expand_backward, chunk=256), "caption_mlp_backward", (4,),
        [whole((tokens, width)), pl.BlockSpec((tokens, piece), lambda j, info: (0, j)), whole((tokens, width)),
         pl.BlockSpec((width, piece), unit_block), pl.BlockSpec((piece, width), unit_rows)],
        [(pl.BlockSpec((4, rows, piece), lambda j, info: (0, 0, j)), shape((4, rows, 4 * piece))),
         (pl.BlockSpec((4, rows, piece), lambda j, info: (0, 0, j)), shape((4, rows, 4 * piece))),
         (pl.BlockSpec((1, 1, piece), zrow), shape((4, 1, piece), F32)),
         (whole((own, width)), shape((own, width), F32)),
         (whole((own, width)), shape((own, width)))],
        [pltpu.VMEM((tokens, width), F32), pltpu.VMEM((tokens, piece), BF16)],
        2 * tokens * width * hidden // 2 * 3,
        (n2, slope, cot, expand_weight, reduce_weight),
        (info,),
    )
    dn_far = swap(dn_send)
    b_far = hop(b_send, 1)

    mg_keep, mg_send, dp_keep, dp_send, sums = kernel(
        partial(attend_backward, slots=slots), "caption_attention_backward", (steps,),
        [pl.BlockSpec((block, width), at), pl.BlockSpec((block, width), at), pl.BlockSpec((block, width), at),
         pl.BlockSpec((block, width), mine), whole((width,)), whole(project_out.shape),
         pl.BlockSpec((block, 3 * width), at), pl.BlockSpec((heads * slots, block), lambda i, *_: (0, i))],
        [(pl.BlockSpec((block, half), at), shape((own, half))),
         (pl.BlockSpec((block, half), at), shape((own, half))),
         (pl.BlockSpec((block, wide), at), shape((own, wide))),
         (pl.BlockSpec((block, wide), at), shape((own, wide))),
         (whole((8, width)), shape((8, width), F32))],
        [pltpu.VMEM((block, width), BF16), pltpu.VMEM((block, 3 * width), BF16)],
        2 * own * width * width * 3,
        (dn_keep, dn_far, middle, cot, second_gain, project_out, packed, probs),
        (info,),
    )
    dp_far = swap(dp_send)
    mg_far = swap(mg_send)

    c1_keep, c1_send, c2_keep, c2_send = kernel(
        attend_weights, "caption_attention_weights", (1,),
        [whole((own, width)), whole((own, width)), whole((own, wide)), whole((own, wide)),
         whole((own, width)), whole((own, width)), whole((own, half)), whole((own, half))],
        [(whole((8, rows // 2, width)), shape((8, rows // 2, width))),
         (whole((8, rows // 2, width)), shape((8, rows // 2, width))),
         (whole((4, rows, width)), shape((4, rows, width))),
         (whole((4, rows, width)), shape((4, rows, width)))],
        [], 2 * tokens * width * width * 2,
        (normed, normed_far, dp_keep, dp_far, context, context_far, mg_keep, mg_far),
        (info,),
    )
    c1_far = hop(c1_send, 0)
    c2_far = hop(c2_send, 1)

    cg_keep, cg_send, sums_in = kernel(
        input_backward, "caption_input_backward", (steps,),
        [pl.BlockSpec((block, width), mine), whole((width,)),
         pl.BlockSpec((width, wide), lambda i, info: (0, info[0])),
         pl.BlockSpec((width, wide), lambda i, info: (0, 1 - info[0])),
         pl.BlockSpec((block, wide), at), pl.BlockSpec((block, wide), at),
         pl.BlockSpec((block, half), at), pl.BlockSpec((block, half), at)],
        [(pl.BlockSpec((block, half), at), shape((own, half))),
         (pl.BlockSpec((block, half), at), shape((own, half))),
         (whole((8, width)), shape((8, width), F32))],
        [], 2 * own * width * width * 3,
        (x, first_gain, project_in, project_in, dp_keep, dp_send, mg_keep, mg_send),
        (info,),
    )
    cg_far = swap(cg_send)

    bias_part = bias_part.reshape(4, 1, piece)
    blank = jnp.zeros_like(bias_part)
    bias_full = jnp.where(
        core == 0,
        jnp.concatenate([bias_part, blank], axis=1),
        jnp.concatenate([blank, bias_part], axis=1),
    )
    vectors = jnp.concatenate([sums_in[:2], sums[:6], bias_full.reshape(4, width)], axis=0)
    vectors = lax.psum(vectors, ("section", "dp"))

    def add(a, b):
        return (a.astype(F32) + b.astype(F32)).astype(BF16)

    def pick(value, bit, axis):
        return lax.dynamic_index_in_dim(value, bit, axis, keepdims=False)

    def fold(keep, far, bit, axis, only=None):
        keep, far = keep, far
        b = bits[bit]
        sending = add(pick(keep, 1 - b, axis), pick(far, 1 - b, axis))
        return add(pick(keep, b, axis), pick(far, b, axis)), hop(sending, bit, only)

    def finish(total):
        if low:
            groups = [list(range(i, i + (1 << low))) for i in range(0, ranks, 1 << low)]
            total = lax.psum_scatter(
                total, "dp", scatter_dimension=0, tiled=True, axis_index_groups=groups
            )
        return total

    on_core = lambda k, y: k == y
    a_sum = add(a_keep, a_far)
    a_sum = add(a_sum, hop(a_sum, 1, lambda k, y: k != y)).reshape(2, 2, piece // 2, width)
    sending = pick(a_sum, 1 - bits[2], 1)
    a_keep, a_far = pick(a_sum, bits[2], 1), hop(sending, 2, on_core)
    a_keep, a_far = fold(a_keep, a_far, 3, 0, on_core)
    a_own = finish(add(a_keep, a_far))
    a_away = swap(a_own)
    reduce_grad = jnp.where(core == bits[1], a_own, a_away).astype(F32)

    def rest(keep, far, second):
        columns = keep.shape[-1]
        dims = (2, 2, 2, rows // 2, columns)
        keep, far = fold(keep.reshape(dims), far.reshape(dims), second, 2)
        keep, far = fold(keep, far, 2, 1)
        keep, far = fold(keep, far, 3, 0)
        return finish(add(keep, far))

    b_own = rest(b_keep, b_far, 0)
    b_away = swap(b_own)
    c_own = jnp.concatenate([rest(c1_keep, c1_far, 1), rest(c2_keep, c2_far, 0)], axis=1)
    c_away = swap(c_own)

    def both(mine_part, far_part, axis):
        return jnp.where(
            core == 0,
            jnp.concatenate([mine_part, far_part], axis=axis),
            jnp.concatenate([far_part, mine_part], axis=axis),
        )

    share = width // ranks
    expand_grad = both(
        b_own.reshape(share, 4, 1, piece), b_away.reshape(share, 4, 1, piece), 2
    ).reshape(share, hidden).astype(F32)
    in_grad = both(c_own[:, :wide], c_away[:, :wide], 1).astype(F32)
    out_grad = both(c_own[:, wide:], c_away[:, wide:], 1).astype(F32)

    def vector(first, number=1):
        size = number * width // ranks
        flat = vectors[first : first + number].reshape(-1)
        return lax.dynamic_slice_in_dim(flat, place * size, size, 0)

    caption_output = (out_keep + out_far.astype(F32)).astype(BF16).reshape(count, slots, half)
    captions_gradient = both(cg_keep, cg_far, 0).reshape(count, slots, half)

    images, used, _ = patches.shape
    padded = 64
    parts = 2
    span = images // parts
    four = 4
    vision_output = None
    for part in range(parts):
        (vision_middle,) = kernel(
            partial(vision_attend, slots=padded), "vision_attention", (span // four,),
            [pl.BlockSpec((four, used, width), lambda i, part=part: (part * (span // four) + i, 0, 0)),
             whole((width,)), whole((width,)), whole(vision_project_in.shape), whole(vision_inward_bias.shape),
             whole(vision_project_out.shape), whole((width,))],
            [(pl.BlockSpec((four * padded, width), lambda i: (i, 0)), shape((span * padded, width), F32))],
            [pltpu.VMEM((four * padded, width), F32), pltpu.VMEM((four * padded, 3 * width), BF16),
             pltpu.VMEM((four * padded, width), BF16)],
            2 * span * padded * width * width * 4 * 1.3,
            (patches, vision_first_gain, vision_first_shift, vision_project_in, vision_inward_bias,
             vision_project_out, vision_outward_bias),
        )
        more = () if vision_output is None else (vision_output,)
        (vision_output,) = kernel(
            partial(vision_expand, chunk=256, slots=padded), "vision_mlp", (hidden // 1024,),
            [whole((span * padded, width)), whole((width,)), whole((width,)),
             pl.BlockSpec((width, 1024), lambda j: (0, j)), pl.BlockSpec((1024,), lambda j: (j,)),
             pl.BlockSpec((1024, width), lambda j: (j, 0)), whole((width,))]
            + [pl.BlockSpec(memory_space=pl.ANY)] * len(more),
            [(pl.BlockSpec((span, used, width), lambda j, part=part: (part, 0, 0)), shape(patches.shape))],
            [pltpu.VMEM((span * padded, width), BF16), pltpu.VMEM((span * padded, width), F32)],
            2 * span * padded * width * hidden * 2,
            (vision_middle, vision_second_gain, vision_second_shift, vision_expand_weight, vision_expand_bias,
             vision_reduce_weight, vision_reduce_bias) + more,
            aliases={7: 0} if more else None,
        )

    return (
        vision_output, caption_output, captions_gradient,
        vector(0), vector(1), in_grad, vector(6, 2),
        out_grad, vector(4), vector(2), vector(3), expand_grad, vector(8, 4), reduce_grad, vector(5),
    )


def solution(mesh):
    spread_all = P(("section", "dp"), None, None)
    placed = (P("dp", None, None), P("dp"), P("dp", None, None)) + (P(),) * 12 + (spread_all,) + (P(),) * 12
    features = P("dp", None, "section")
    return jax.shard_map(
        on_device,
        mesh=mesh,
        in_specs=placed,
        out_specs=(
            spread_all, features, features,
            P("dp"), P("dp"), P("dp", None), P("dp"), P("dp", None), P("dp"),
            P("dp"), P("dp"), P("dp", None), P("dp"), P("dp", None), P("dp"),
        ),
        check_vma=False,
    )
```

```python
from functools import partial

import jax
import jax.experimental.pallas as pl
import jax.numpy as jnp
from jax import lax
from jax.experimental.pallas import tpu as pltpu
from jax.sharding import PartitionSpec as P

HEAD_DIM = 64
GROUP = 128
EPSILON = 1e-06
MASKED = -1000000000.0
ROOT = 0.7978845608028654
CUBIC = 0.044715
F32 = jnp.float32
BF16 = jnp.bfloat16
MIB = 1024 * 1024
COST = 1e6


def nn(a, b):
    return lax.dot_general(a, b, (((1,), (0,)), ((), ())), preferred_element_type=F32)


def nt(a, b):
    return lax.dot_general(a, b, (((1,), (1,)), ((), ())), preferred_element_type=F32)


def tn(a, b):
    return lax.dot_general(a, b, (((0,), (0,)), ((), ())), preferred_element_type=F32)


def row(ref):
    return ref[...].astype(F32).reshape(1, -1)


def units(x):
    average = jnp.mean(x, axis=-1, keepdims=True)
    centred = x - average
    variance = jnp.mean(centred * centred, axis=-1, keepdims=True)
    inverse = lax.rsqrt(variance + EPSILON)
    return centred * inverse, inverse


def norm_back(unit, inverse, gain, dy):
    du = dy * gain
    first = jnp.mean(du, axis=-1, keepdims=True)
    second = jnp.mean(du * unit, axis=-1, keepdims=True)
    return (du - first - unit * second) * inverse


def lane_block(slots, rows):
    return lax.broadcasted_iota(jnp.int32, (rows, GROUP), 1) // slots


def two_heads(a):
    lanes = lax.broadcasted_iota(jnp.int32, a.shape, 1)
    low = (lanes < HEAD_DIM).astype(F32).astype(BF16)
    high = (lanes >= HEAD_DIM).astype(F32).astype(BF16)
    return jnp.concatenate([a * low, a * high], axis=0)


def compact(full, slots):
    block = lane_block(slots, slots)
    out = full[:slots]
    for b in range(1, GROUP // slots):
        out = jnp.where(block == b, full[b * slots : (b + 1) * slots], out)
    return out


def spread(part, slots):
    block = lane_block(slots, slots)
    return jnp.concatenate(
        [part * (block == b).astype(F32).astype(BF16) for b in range(GROUP // slots)], axis=0
    )


def attention(q, k, v, allowed, slots):
    scores = nt(two_heads(k), q)
    probs = []
    for a in range(2):
        s = compact(scores[a * GROUP : (a + 1) * GROUP], slots) * (HEAD_DIM**-0.5)
        s = jnp.where(allowed, s, MASKED)
        powered = jnp.exp(s - jnp.max(s, axis=0, keepdims=True))
        probs.append(powered / jnp.sum(powered, axis=0, keepdims=True))
    wide = jnp.concatenate([spread(p.astype(BF16), slots) for p in probs], axis=0)
    return tn(wide, two_heads(v)), probs


def attention_back(q, k, v, probs, dc, slots):
    vv, kk, qq, dd = two_heads(v), two_heads(k), two_heads(q), two_heads(dc)
    dprobs = nt(vv, dc)
    wide_p, wide_s = [], []
    for a in range(2):
        dp = compact(dprobs[a * GROUP : (a + 1) * GROUP], slots)
        p = probs[a]
        ds = p * (dp - jnp.sum(p * dp, axis=0, keepdims=True))
        wide_p.append(spread(p.astype(BF16), slots))
        wide_s.append(spread(ds.astype(BF16), slots))
    dv = nn(jnp.concatenate(wide_p, axis=1), dd)
    dk = nn(jnp.concatenate(wide_s, axis=1), qq)
    dq = tn(jnp.concatenate(wide_s, axis=0), kk)
    scale = HEAD_DIM**-0.5
    return (dq * scale).astype(BF16), (dk * scale).astype(BF16), dv.astype(BF16)


def fetch(pairs, sems):
    copies = [pltpu.make_async_copy(a, b, sems.at[i]) for i, (a, b) in enumerate(pairs)]
    for copy in copies:
        copy.start()
    return copies


def thirds(win, held, width):
    return [(win.at[:, t * width : (t + 1) * width], held.at[:, t * width : (t + 1) * width]) for t in range(3)]


def inward(n1, t, win, bias):
    width = n1.shape[1]
    part = nn(n1, win[:, t * width : (t + 1) * width])
    if t != 1:
        part = part + bias[:, t // 2 * width : (t // 2 + 1) * width]
    return part.astype(BF16)


def attend_forward(
    info, lens, x_hbm, g_ref, s_ref, win_hbm, bi_ref, wo_hbm, bo_ref,
    mid_ref, ctx_ref, n1_ref, pk_ref, pc_ref, xs, win, wo, sems, *, slots,
):
    rows, width = xs.shape
    begin = pl.multiple_of(info[0] * rows, rows)
    copies = fetch(
        [(x_hbm.at[pl.ds(begin, rows)], xs), *thirds(win_hbm, win, width), (wo_hbm, wo)], sems
    )
    copies[0].wait()
    unit, _ = units(xs[...].astype(F32))
    n1_ref[...] = (unit * row(g_ref) + row(s_ref)).astype(BF16)
    for t in range(3):
        copies[1 + t].wait()
        pk_ref[:, t * width : (t + 1) * width] = inward(n1_ref[...], t, win, row(bi_ref))
    block = lane_block(slots, 1)
    slot = lax.broadcasted_iota(jnp.int32, (slots, GROUP), 0)
    per = GROUP // slots
    start = info[0] * (rows // slots)
    for g in range(rows // GROUP):
        used = jnp.zeros((1, GROUP), jnp.int32)
        for b in range(per):
            used = jnp.where(block == b, lens[start + g * per + b], used)
        allowed = slot < used
        tokens = slice(g * GROUP, (g + 1) * GROUP)
        for p in range(width // 128):
            q, k, v = (pk_ref[tokens, t * width + p * 128 : t * width + (p + 1) * 128] for t in range(3))
            ctx, probs = attention(q, k, v, allowed, slots)
            ctx_ref[tokens, p * 128 : (p + 1) * 128] = ctx.astype(BF16)
            for a in range(2):
                pc_ref[(2 * p + a) * slots : (2 * p + a + 1) * slots, tokens] = probs[a]
    copies[4].wait()
    mid_ref[...] = (xs[...].astype(F32) + (nn(ctx_ref[...], wo[...]) + row(bo_ref))).astype(BF16)


def unit_parts(info, we_hbm, wr_hbm, we, wr):
    piece = we.shape[1] // 4
    pairs = []
    for z in range(4):
        held = slice(z * piece, (z + 1) * piece)
        begin = pl.ds(pl.multiple_of((2 * z + info[0]) * piece, piece), piece)
        pairs += [(we_hbm.at[:, begin], we.at[:, held]), (wr_hbm.at[begin], wr.at[held])]
    return pairs


def choose(flag, a, b):
    return jnp.where(flag == 0, a, b)


def expand_forward(
    info, own_ref, oth_ref, cot_ref, g_ref, s_ref, be_ref, br_ref, we_hbm, wr_hbm,
    n2_ref, slope_ref, keep_ref, send_ref, outk_ref, outs_ref, we, wr, act, sems, *, chunk,
):
    tokens, width = cot_ref.shape
    count, half = own_ref.shape[0], width // 2
    c = info[0]
    copies = fetch(unit_parts(info, we_hbm, wr_hbm, we, wr), sems)
    bias = jnp.concatenate([be_ref[2 * z + c] for z in range(4)], axis=1).astype(F32)
    last = row(br_ref)
    last = choose(c, last[:, :half], last[:, half:])
    begins = []
    for k in range(tokens // chunk):
        source, first = (own_ref, k * chunk) if k * chunk < count else (oth_ref, k * chunk - count)
        at = pl.ds(pl.multiple_of((c if source is own_ref else 1 - c) * count + first, chunk), chunk)
        begins.append((source, first, at))
        unit, _ = units(source[first : first + chunk].astype(F32))
        n2_ref[at] = (unit * row(g_ref) + row(s_ref)).astype(BF16)
    for copy in copies:
        copy.wait()
    for source, first, at in begins:
        h = nn(n2_ref[at], we[...]) + bias
        square = h * h
        gate = 0.5 + 0.5 * jnp.tanh(h * (ROOT + (ROOT * CUBIC) * square))
        active = h * gate
        slope = gate + active * (1.0 - gate) * (2.0 * ROOT + (6.0 * CUBIC * ROOT) * square)
        act[at] = active.astype(BF16)
        slope_ref[at] = slope.astype(BF16)
        out = nn(act[at], wr[...])
        mid = source[first : first + chunk].astype(F32)
        outk_ref[at] = choose(c, mid[:, :half], mid[:, half:]) + (choose(c, out[:, :half], out[:, half:]) + last)
        outs_ref[at] = choose(c, out[:, half:], out[:, :half]).astype(BF16)
    span = act.shape[1] // 4
    for z in range(4):
        grad = tn(act[:, z * span : (z + 1) * span], cot_ref[...])
        keep_ref[z] = choose(info[1], grad[: span // 2], grad[span // 2 :]).astype(BF16)
        send_ref[z] = choose(info[1], grad[span // 2 :], grad[: span // 2]).astype(BF16)


def expand_backward(
    info, slope_ref, cot_ref, we_hbm, wr_hbm, dh_ref, db_ref, dk_ref, ds_ref, we, wr, sems, *, chunk,
):
    tokens, width = cot_ref.shape
    count = dk_ref.shape[0]
    c = info[0]
    copies = fetch(unit_parts(info, we_hbm, wr_hbm, we, wr), sems)
    for copy in copies:
        copy.wait()
    total = jnp.zeros((1, slope_ref.shape[1]), F32)
    for k in range(tokens // chunk):
        mine = k * chunk < count
        first = k * chunk if mine else k * chunk - count
        at = pl.ds(pl.multiple_of((c if mine else 1 - c) * count + first, chunk), chunk)
        da = nt(cot_ref[at], wr[...])
        dh = (da * slope_ref[at].astype(F32)).astype(BF16)
        dh_ref[at] = dh
        total = total + jnp.sum(dh.astype(F32), axis=0, keepdims=True)
        dn = nt(dh_ref[at], we[...])
        if mine:
            dk_ref[first : first + chunk] = dn
        else:
            ds_ref[first : first + chunk] = dn.astype(BF16)
    db_ref[...] = total


def split_rows(grad, first, second, bit):
    short = grad.shape[0] // (2 * first.shape[0])
    for z in range(first.shape[0]):
        low = grad[2 * z * short : (2 * z + 1) * short]
        high = grad[(2 * z + 1) * short : (2 * z + 2) * short]
        first[z] = choose(bit, low, high).astype(BF16)
        second[z] = choose(bit, high, low).astype(BF16)


def expand_weights(info, n2_ref, dh_ref, keep_ref, send_ref):
    span = dh_ref.shape[1] // 2
    for j in range(2):
        cols = slice(j * span, (j + 1) * span)
        grad = tn(n2_ref[...], dh_ref[:, cols])
        split_rows(grad, keep_ref.at[:, :, cols], send_ref.at[:, :, cols], info[2])


def attend_backward(
    info, dn_ref, da_ref, mid_ref, cot_ref, g_ref, wo_ref, pk_ref, pc_ref, *refs, slots,
):
    keeps, sends, (sums_ref, dctx, dpk) = refs[:4], refs[4:8], refs[8:]
    rows, width = mid_ref.shape
    half, wide = width // 2, 3 * width // 2
    c = info[0]
    cot = cot_ref[...].astype(F32)
    unit, inverse = units(mid_ref[...].astype(F32))
    dn = dn_ref[...] + da_ref[...].astype(F32)
    mg = (cot + norm_back(unit, inverse, row(g_ref), dn)).astype(BF16)
    dctx[...] = nt(mg, wo_ref[...]).astype(BF16)
    for g in range(rows // GROUP):
        tokens = slice(g * GROUP, (g + 1) * GROUP)
        for p in range(width // 128):
            q, k, v = (pk_ref[tokens, t * width + p * 128 : t * width + (p + 1) * 128] for t in range(3))
            probs = [pc_ref[(2 * p + a) * slots : (2 * p + a + 1) * slots, tokens] for a in range(2)]
            grads = attention_back(q, k, v, probs, dctx[tokens, p * 128 : (p + 1) * 128], slots)
            for t in range(3):
                dpk[tokens, t * width + p * 128 : t * width + (p + 1) * 128] = grads[t]

    def total(a):
        return jnp.sum(a, axis=0, keepdims=True)

    mf = mg.astype(F32)
    sums = [
        total(dn * unit),
        total(dn),
        total(mf),
        total(cot),
        total(dpk[:, :width].astype(F32)),
        total(dpk[:, 2 * width :].astype(F32)),
    ]
    sums = jnp.concatenate(sums + [jnp.zeros((2, width), F32)], axis=0)

    @pl.when(pl.program_id(0) == 0)
    def _():
        sums_ref[...] = sums

    @pl.when(pl.program_id(0) > 0)
    def _():
        sums_ref[...] += sums

    keeps[3][...] = choose(c, mf[:, :half], mf[:, half:]).astype(BF16)
    sends[3][...] = choose(c, mf[:, half:], mf[:, :half]).astype(BF16)

    def store(mine, others):
        for j in range(3):
            keeps[j][...] = dpk[:, mine + j * half : mine + (j + 1) * half]
            sends[j][...] = dpk[:, others + j * half : others + (j + 1) * half]

    @pl.when(c == 0)
    def _():
        store(0, wide)

    @pl.when(c == 1)
    def _():
        store(wide, 0)


def attend_weights(info, n1k, n1o, ctk, cto, *refs):
    keeps, fars, (k1, s1, k2, s2) = refs[:4], refs[4:8], refs[8:]
    block = keeps[0].shape[1]
    for j in range(4):
        left, right = (n1k, n1o) if j < 3 else (ctk, cto)
        grad = tn(left[...], keeps[j][...]) + tn(right[...], fars[j][...])
        place = slice((j % 2) * block, (j % 2 + 1) * block)
        first, second, bit = (k1, s1, info[1]) if j < 2 else (k2, s2, info[2])
        split_rows(grad, first.at[:, :, place], second.at[:, :, place], bit)


def input_backward(
    info, x_ref, g_ref, winc_ref, wino_ref, *refs,
):
    (*dpk, mgk), (*dps, mgs), (sums_ref, db_ref, cgk_ref, cgs_ref, vec_ref) = refs[:4], refs[4:8], refs[8:]
    width = x_ref.shape[1]
    half = width // 2
    c = info[0]
    unit, inverse = units(x_ref[...].astype(F32))
    dn = nt(jnp.concatenate([r[...] for r in dpk], axis=1), winc_ref[...])
    dn = dn + nt(jnp.concatenate([r[...] for r in dps], axis=1), wino_ref[...])
    dv = norm_back(unit, inverse, row(g_ref), dn)
    sums = jnp.concatenate(
        [jnp.sum(dn * unit, axis=0, keepdims=True), jnp.sum(dn, axis=0, keepdims=True)], axis=0
    )

    @pl.when(pl.program_id(0) == 0)
    def _():
        vec_ref[:2] = sums
        vec_ref[2:8] = sums_ref[:6]
        for z in range(4):
            part = db_ref[:, z * half : (z + 1) * half]
            vec_ref[8 + z : 9 + z, :half] = part * (1 - c).astype(F32)
            vec_ref[8 + z : 9 + z, half:] = part * c.astype(F32)
        vec_ref[12:] = jnp.zeros((4, width), F32)

    @pl.when(pl.program_id(0) > 0)
    def _():
        vec_ref[:2] += sums

    cgk_ref[...] = (choose(c, dv[:, :half], dv[:, half:]) + mgk[...].astype(F32)).astype(BF16)
    cgs_ref[...] = (choose(c, dv[:, half:], dv[:, :half]) + mgs[...].astype(F32)).astype(BF16)


def vision_attend(
    x_ref, g_ref, s_ref, win_hbm, bi_ref, wo_hbm, bo_ref, mid_ref, win, wo, n1, pk, ctx, sems,
    *, images, slots,
):
    rows, width = x_ref.shape
    copies = fetch([*thirds(win_hbm, win, width), (wo_hbm, wo)], sems)
    unit, _ = units(x_ref[...].astype(F32))
    n1[...] = (unit * row(g_ref) + row(s_ref)).astype(BF16)
    across = width // 128
    pk[:, rows:] = jnp.zeros((pk.shape[0], pk.shape[1] - rows, 128), F32)
    for t in range(3):
        copies[t].wait()
        part = inward(n1[...], t, win, row(bi_ref)).astype(F32)
        for p in range(across):
            pk[t * across + p, :rows] = part[:, p * 128 : (p + 1) * 128]
    allowed = lax.broadcasted_iota(jnp.int32, (slots, GROUP), 0) < rows // images
    per = GROUP // slots
    for i in range(0, images, per):
        for p in range(across):

            def load(t):
                parts = [pk[t * across + p, pl.ds(i + b, slots, stride=images)] for b in range(per)]
                return jnp.concatenate(parts, axis=0).astype(BF16)

            out, _ = attention(load(0), load(1), load(2), allowed, slots)
            for b in range(per):
                ctx[p, pl.ds(i + b, slots, stride=images)] = out[b * slots : (b + 1) * slots]
    copies[3].wait()
    context = jnp.concatenate([ctx[p, :rows].astype(BF16) for p in range(across)], axis=1)
    mid_ref[...] = x_ref[...].astype(F32) + (nn(context, wo[...]) + row(bo_ref))


def vision_expand(
    mid_ref, g_ref, s_ref, be_ref, br_ref, we_hbm, wr_hbm, *refs,
):
    out_ref, we, wr, n2, act, sems = refs[-6:]
    rows, width = mid_ref.shape
    blocks = we.shape[1] // width
    cut = [slice(f * width, (f + 1) * width) for f in range(blocks)]
    copies = fetch([(we_hbm.at[:, f], we.at[:, f]) for f in cut] + [(wr_hbm.at[f], wr.at[f]) for f in cut], sems)
    unit, _ = units(mid_ref[...])
    n2[...] = (unit * row(g_ref) + row(s_ref)).astype(BF16)
    bias = row(be_ref)
    for f, cols in enumerate(cut):
        copies[f].wait()
        h = nn(n2[...], we[:, cols]) + bias[:, cols]
        gate = 0.5 + 0.5 * jnp.tanh(h * (ROOT + (ROOT * CUBIC) * (h * h)))
        act[:, cols] = (h * gate).astype(BF16)
    for f in range(blocks):
        copies[blocks + f].wait()
    result = mid_ref[...] + (nn(act[...], wr[...]) + row(br_ref))
    out_ref[...] = result.astype(BF16).reshape(out_ref.shape)


def shape(dims, dtype=BF16):
    return jax.ShapeDtypeStruct(dims, dtype)


def whole(dims):
    return pl.BlockSpec(dims, lambda *_: (0,) * len(dims))


FAR = pl.BlockSpec(memory_space=pl.ANY)


def kernel(body, name, grid, ins, outs, scratch, args, scalars=(), aliases=None, after=(), cost=1, limit=40):
    first, extra = len(scalars) + len(args), len(after)

    def run(*refs):
        return body(*refs[:first], *refs[first + extra :])

    specs = pltpu.PrefetchScalarGridSpec(
        num_scalar_prefetch=len(scalars),
        grid=grid,
        in_specs=list(ins) + [FAR] * extra,
        out_specs=[o[0] for o in outs],
        scratch_shapes=scratch,
    )
    return pl.pallas_call(
        run,
        name=name,
        grid_spec=specs,
        out_shape=[o[1] for o in outs],
        compiler_params=pltpu.CompilerParams(
            vmem_limit_bytes=limit * MIB, dimension_semantics=("arbitrary",) * len(grid)
        ),
        cost_estimate=pl.CostEstimate(
            flops=int(cost * COST), bytes_accessed=1000, transcendentals=0
        ),
        input_output_aliases=aliases or {},
    )(*scalars, *args, *after)


class Parts:
    def __init__(self, arrays, dims, own=()):
        self.arrays, self.dims, self.own = list(arrays), list(dims), tuple(own)

    def left(self):
        return [d for d in self.dims[0] if d not in self.own]


BITS = {"x": 1, "y": 2, "zl": 3, "zh": 4}


def fold(jobs, info, after, name):
    args, ins, outs, counts = [], [], [], []
    for parts, bit in jobs:
        keep = [d for d in parts.left() if d != bit]
        counts.append(len(parts.arrays))
        for array, dims in zip(parts.arrays, parts.dims):
            payload = array.shape[len(dims) :]

            def at(i, info, dims=dims, bit=bit, own=parts.own, payload=payload):
                places = []
                for d in dims:
                    if d == bit:
                        places.append(1 - info[BITS[d]])
                    elif d in own:
                        places.append(info[BITS[d]])
                    else:
                        places.append(0)
                return (*places, *(0 for _ in payload))

            block = tuple(None if d == bit or d in parts.own else 2 for d in dims)
            args.append(array)
            ins.append(pl.BlockSpec((*block, *payload), at))
        dims = (2,) * len(keep) + payload
        outs.append((whole(dims), shape(dims, parts.arrays[0].dtype)))

    def body(info, *refs):
        at = 0
        for n, (number, out) in enumerate(zip(counts, refs[sum(counts) :])):
            total = refs[at][...].astype(F32)
            for r in refs[at + 1 : at + number]:
                total = total + r[...].astype(F32)
            out[...] = total.astype(out.dtype)
            at += number

    return kernel(body, name, (1,), ins, outs, [], args, (info,), after=after, cost=1, limit=24)


def assemble(
    info, a_own, a_far, b_own, b_far, c_own, c_far, v_own, v_far,
    a_ref, b_ref, in_ref, out_ref, v_ref, *, ranks,
):
    c = info[0]
    a_ref[...] = choose(c ^ info[2], a_own[...].astype(F32), a_far[...].astype(F32))
    piece = b_ref.shape[1] // 8
    wide, half = in_ref.shape[1] // 2, out_ref.shape[1] // 2

    def store(low, high, c_low, c_high):
        for z in range(4):
            held = slice(z * piece, (z + 1) * piece)
            b_ref[:, 2 * z * piece : (2 * z + 1) * piece] = low[:, held].astype(F32)
            b_ref[:, (2 * z + 1) * piece : (2 * z + 2) * piece] = high[:, held].astype(F32)
        in_ref[:, :wide] = c_low[:, :wide].astype(F32)
        in_ref[:, wide:] = c_high[:, :wide].astype(F32)
        out_ref[:, :half] = c_low[:, wide:].astype(F32)
        out_ref[:, half:] = c_high[:, wide:].astype(F32)

    @pl.when(c == 0)
    def _():
        store(b_own, b_far, c_own, c_far)

    @pl.when(c == 1)
    def _():
        store(b_far, b_own, c_far, c_own)

    total = v_own[...] + v_far[...]
    width = total.shape[1]
    place = info[5]

    def part(rows, size):
        offset = place * size
        which = offset // width
        taken = rows[:1]
        for k in range(1, rows.shape[0]):
            taken = jnp.where(which == k, rows[k : k + 1], taken)
        taken = jnp.concatenate([taken] * 8, axis=0)
        turn = lax.rem(width - lax.rem(offset, width), width)
        return pltpu.roll(taken, turn, 1)[:1]

    one = width // ranks
    lanes = v_ref.shape[1]
    for k in range(6):
        v_ref[k : k + 1] = part(total[k : k + 1], one)[:, :lanes]
    v_ref[6:7] = part(total[6:8], 2 * one)[:, :lanes]
    v_ref[7:8] = part(total[8:12], 4 * one)[:, :lanes]


def on_device(
    captions, caption_lengths, caption_cotangent,
    first_gain, first_shift, project_in, inward_bias, project_out, outward_bias,
    second_gain, second_shift, expand_weight, expand_bias, reduce_weight, reduce_bias,
    patches,
    vision_first_gain, vision_first_shift, vision_project_in, vision_inward_bias, vision_project_out, vision_outward_bias,
    vision_second_gain, vision_second_shift, vision_expand_weight, vision_expand_bias, vision_reduce_weight, vision_reduce_bias,
):
    count, slots, width = captions.shape
    hidden = expand_weight.shape[1]
    tokens = count * slots
    own = tokens // 2
    half = width // 2
    units_own = hidden // 2
    piece = hidden // 8
    wide = 3 * half
    heads = width // HEAD_DIM
    rows = width // 16
    ranks = lax.axis_size("dp")
    low = (ranks // 16).bit_length() - 1
    core = lax.axis_index("section")
    place = lax.axis_index("dp")
    info = jnp.stack([core] + [(place >> (low + b)) & 1 for b in range(4)] + [place]).astype(jnp.int32)
    x = captions.reshape(tokens, width)
    cot = caption_cotangent.reshape(tokens, width)
    dma = pltpu.SemaphoreType.DMA

    def hop(value, bit, only=None):
        step = 1 << (low + BITS[bit] - 1)
        pairs = []
        for k in range(2):
            for d in range(ranks):
                if only is None or only(k, (d >> (low + 1)) & 1):
                    pairs.append((k * ranks + d, k * ranks + (d ^ step)))
        return lax.ppermute(value, ("section", "dp"), pairs)

    def swap(value):
        return lax.ppermute(value, "section", [(0, 1), (1, 0)])

    def advance(jobs, after, name, only=None):
        sums = fold(jobs, info, after, name)
        for (parts, bit), value in zip(jobs, sums):
            if bit is not None:
                left = [d for d in parts.left() if d != bit]
                parts.own += (bit,)
                parts.arrays.append(hop(value, bit, only))
                parts.dims.append(left)
        return sums

    def low_sum(value):
        if low:
            groups = [list(range(i, i + (1 << low))) for i in range(0, ranks, 1 << low)]
            value = lax.psum_scatter(
                value, "dp", scatter_dimension=0, tiled=True, axis_index_groups=groups
            )
        return value

    vector = whole((width,))
    middle, context, normed, packed, probs = kernel(
        partial(attend_forward, slots=slots), "caption_attention", (1,),
        [FAR, vector, vector, FAR, whole(inward_bias.shape), FAR, vector],
        [(whole((own, width)), shape((own, width)))] * 3
        + [(whole((own, 3 * width)), shape((own, 3 * width))),
           (whole((heads * slots, own)), shape((heads * slots, own), F32))],
        [pltpu.VMEM((own, width), BF16), pltpu.VMEM(project_in.shape, BF16), pltpu.VMEM(project_out.shape, BF16), dma((5,))],
        (x, first_gain, first_shift, project_in, inward_bias, project_out, outward_bias),
        (info, caption_lengths), cost=7,
    )
    middle_far = swap(middle)

    held = [pltpu.VMEM((width, units_own), BF16), pltpu.VMEM((units_own, width), BF16)]
    n2, slope, a_keep, a_send, out_keep, out_send = kernel(
        partial(expand_forward, chunk=256), "caption_mlp_forward", (1,),
        [whole((own, width)), whole((own, width)), whole((tokens, width)), vector, vector,
         whole((8, 1, piece)), vector, FAR, FAR],
        [(whole((tokens, width)), shape((tokens, width))),
         (whole((tokens, units_own)), shape((tokens, units_own))),
         (whole((4, piece // 2, width)), shape((4, piece // 2, width))),
         (whole((4, piece // 2, width)), shape((4, piece // 2, width))),
         (whole((tokens, half)), shape((tokens, half), F32)),
         (whole((tokens, half)), shape((tokens, half)))],
        [*held, pltpu.VMEM((tokens, units_own), BF16), dma((8,))],
        (middle, middle_far, cot, second_gain, second_shift, expand_bias.reshape(8, 1, piece), reduce_bias, expand_weight, reduce_weight),
        (info,), cost=13,
    )
    a_far = hop(a_send, "x")
    context_far = swap(context)
    normed_far = swap(normed)
    out_far = swap(out_send)

    dh, db, dn_keep, dn_send = kernel(
        partial(expand_backward, chunk=256), "caption_mlp_backward", (1,),
        [whole((tokens, units_own)), whole((tokens, width)), FAR, FAR],
        [(whole((tokens, units_own)), shape((tokens, units_own))),
         (whole((1, units_own)), shape((1, units_own), F32)),
         (whole((own, width)), shape((own, width), F32)),
         (whole((own, width)), shape((own, width)))],
        [*held, dma((8,))],
        (slope, cot, expand_weight, reduce_weight),
        (info,), cost=8,
    )
    dn_far = swap(dn_send)
    b_keep, b_send = kernel(
        expand_weights, "caption_mlp_weights", (1,),
        [whole((tokens, width)), whole((tokens, units_own))],
        [(whole((4, 2 * rows, units_own)), shape((4, 2 * rows, units_own)))] * 2,
        [], (n2, dh), (info,), cost=4, after=(dn_keep,),
    )
    b_far = hop(b_send, "y")

    block = 256
    steps = own // block
    mine = lambda i, info: (info[0] * steps + i, 0)
    at = lambda i, *_: (i, 0)
    *pieces, sums = kernel(
        partial(attend_backward, slots=slots), "caption_attention_backward", (steps,),
        [pl.BlockSpec((block, width), at), pl.BlockSpec((block, width), at), pl.BlockSpec((block, width), at),
         pl.BlockSpec((block, width), mine), vector, whole(project_out.shape),
         pl.BlockSpec((block, 3 * width), at), pl.BlockSpec((heads * slots, block), lambda i, *_: (0, i))],
        [(pl.BlockSpec((block, half), at), shape((own, half)))] * 8
        + [(whole((8, width)), shape((8, width), F32))],
        [pltpu.VMEM((block, width), BF16), pltpu.VMEM((block, 3 * width), BF16)],
        (dn_keep, dn_far, middle, cot, second_gain, project_out, packed, probs),
        (info,), cost=9, after=(b_keep,),
    )
    keeps, sends = pieces[:4], pieces[4:]
    fars = [swap(p) for p in sends]

    cg_keep, cg_send, vectors = kernel(
        input_backward, "caption_input_backward", (steps,),
        [pl.BlockSpec((block, width), mine), vector,
         pl.BlockSpec((width, wide), lambda i, info: (0, info[0])),
         pl.BlockSpec((width, wide), lambda i, info: (0, 1 - info[0])),
         *[pl.BlockSpec((block, half), at)] * 8, whole((8, width)), whole((1, units_own))],
        [(pl.BlockSpec((block, half), at), shape((own, half)))] * 2
        + [(whole((16, width)), shape((16, width), F32))],
        [],
        (x, first_gain, project_in, project_in, *keeps, *sends, sums, db),
        (info,), cost=5,
    )
    cg_far = swap(cg_send)

    c1_keep, c1_send, c2_keep, c2_send = kernel(
        attend_weights, "caption_attention_weights", (1,),
        [whole((own, width))] * 4 + [whole((own, half))] * 8,
        [(whole((8, rows, width)), shape((8, rows, width)))] * 2
        + [(whole((4, 2 * rows, width)), shape((4, 2 * rows, width)))] * 2,
        [],
        (normed, normed_far, context, context_far, *keeps, *fars),
        (info,), after=(cg_keep,), cost=5,
    )

    a = Parts([a_keep.reshape(2, 2, piece // 2, width), a_far.reshape(2, 2, piece // 2, width)], [("zh", "zl")] * 2)
    b_shape = (2, 2, 2, rows, units_own)
    b = Parts([b_keep.reshape(b_shape), b_far.reshape(b_shape)], [("zh", "zl", "x")] * 2)
    c_shape = (2, 2, 2, rows, width)
    c1 = Parts([c1_keep.reshape(c_shape), hop(c1_send, "x").reshape(c_shape)], [("zh", "zl", "y")] * 2)
    v_far = hop(vectors, "x")
    c2 = Parts([c2_keep.reshape(c_shape), hop(c2_send, "y").reshape(c_shape)], [("zh", "zl", "x")] * 2)

    def doubled(v):
        return Parts(v, [()] * len(v))

    images, used, _ = patches.shape
    flat = jnp.transpose(patches, (1, 0, 2)).reshape(used * images, width)
    padded = 64
    span = used // 2
    sums = advance([(a, "zl")], (c1_keep,), "fold_one")
    (vision_middle,) = kernel(
        partial(vision_attend, images=images, slots=padded), "vision_attention", (1,),
        [whole(flat.shape), vector, vector, FAR, whole(vision_inward_bias.shape), FAR, vector],
        [(whole(flat.shape), shape(flat.shape, F32))],
        [pltpu.VMEM(vision_project_in.shape, BF16), pltpu.VMEM(vision_project_out.shape, BF16),
         pltpu.VMEM(flat.shape, BF16), pltpu.VMEM((3 * width // 128, padded * images, 128), F32),
         pltpu.VMEM((width // 128, padded * images, 128), F32), dma((4,))],
        (flat, vision_first_gain, vision_first_shift, vision_project_in, vision_inward_bias,
         vision_project_out, vision_outward_bias),
        after=(sums[0],), cost=10,
    )

    def vision_second(part, before, after):
        (out,) = kernel(
            vision_expand, "vision_mlp", (1,),
            [pl.BlockSpec((span * images, width), lambda i: (part, 0)), vector, vector,
             whole((hidden,)), vector, FAR, FAR] + [FAR] * len(before),
            [(pl.BlockSpec((span, images, width), lambda i: (part, 0, 0)), shape((used, images, width)))],
            [pltpu.VMEM((width, hidden), BF16), pltpu.VMEM((hidden, width), BF16),
             pltpu.VMEM((span * images, width), BF16), pltpu.VMEM((span * images, hidden), BF16), dma((8,))],
            (vision_middle, vision_second_gain, vision_second_shift, vision_expand_bias,
             vision_reduce_bias, vision_expand_weight, vision_reduce_weight) + before,
            aliases={7: 0} if before else None, after=after, cost=6,
        )
        return out

    v = doubled([vectors, v_far])
    sums = advance([(a, "zh"), (b, "zl"), (c1, "y"), (c2, "x"), (v, None)], (vision_middle,), "fold_two")
    v = doubled([sums[-1], hop(sums[-1], "y")])
    vision_output = vision_second(0, (), (sums[0],))

    c_dims = ("zh", "zl")
    sums = advance([(a, None), (b, "zh"), (c1, "zl"), (c2, "zl"), (v, None)], (vision_output,), "fold_three")
    a = Parts([sums[0], hop(sums[0], "y", lambda k, y: k != y)], [()] * 2)
    v = doubled([sums[-1], hop(sums[-1], "zl")])
    vision_output = vision_second(1, (vision_output,), (sums[1],))

    sums = advance([(a, None), (b, "x"), (c1, "zh"), (c2, "zh"), (v, None)], (vision_output,), "fold_four")
    a_own = low_sum(sums[0])
    a_away = swap(a_own)
    v = doubled([sums[-1], hop(sums[-1], "zh")])
    sums = advance([(b, None), (c1, None), (c2, None), (v, None)], (), "fold_five")
    b_own = low_sum(sums[0])
    c_own = low_sum(jnp.concatenate([sums[1], sums[2]], axis=1))
    v_own = sums[3]
    if low:
        groups = [list(range(i, i + (1 << low))) for i in range(0, ranks, 1 << low)]
        v_own = lax.psum(v_own, "dp", axis_index_groups=groups)
    b_away, c_away, v_away = swap(b_own), swap(c_own), swap(v_own)
    share = width // ranks
    reduce_grad, expand_grad, in_grad, out_grad, shares = kernel(
        partial(assemble, ranks=ranks), "assemble", (1,),
        [whole(t.shape) for t in (a_own, a_away, b_own, b_away, c_own, c_away, v_own, v_away)],
        [(whole((4 * share, width)), shape((4 * share, width), F32)),
         (whole((share, hidden)), shape((share, hidden), F32)),
         (whole((share, 3 * width)), shape((share, 3 * width), F32)),
         (whole((share, width)), shape((share, width), F32)),
         (whole((8, 256)), shape((8, 256), F32))],
        [], (a_own, a_away, b_own, b_away, c_own, c_away, v_own, v_away), (info,), cost=1,
    )

    def both(mine_part, far_part, axis):
        return jnp.where(
            core == 0,
            jnp.concatenate([mine_part, far_part], axis=axis),
            jnp.concatenate([far_part, mine_part], axis=axis),
        )

    caption_output = (out_keep + out_far.astype(F32)).astype(BF16).reshape(count, slots, half)
    captions_gradient = both(cg_keep, cg_far, 0).reshape(count, slots, half)
    return (
        jnp.transpose(vision_output, (1, 0, 2)), caption_output, captions_gradient,
        shares[0, :share], shares[1, :share], in_grad, shares[6, : 2 * share], out_grad, shares[4, :share],
        shares[2, :share], shares[3, :share], expand_grad, shares[7, : 4 * share], reduce_grad, shares[5, :share],
    )


def solution(mesh):
    spread_all = P(("section", "dp"), None, None)
    placed = (P("dp", None, None), P("dp"), P("dp", None, None)) + (P(),) * 12 + (spread_all,) + (P(),) * 12
    features = P("dp", None, "section")
    return jax.shard_map(
        on_device,
        mesh=mesh,
        in_specs=placed,
        out_specs=(
            spread_all, features, features,
            P("dp"), P("dp"), P("dp", None), P("dp"), P("dp", None), P("dp"),
            P("dp"), P("dp"), P("dp", None), P("dp"), P("dp", None), P("dp"),
        ),
        check_vma=False,
    )
```

```python
from functools import partial

import jax
import jax.experimental.pallas as pl
import jax.numpy as jnp
from jax import lax
from jax.experimental.pallas import tpu as pltpu
from jax.sharding import PartitionSpec as P

HEAD_DIM = 64
GROUP = 128
EPSILON = 1e-06
MASKED = -1000000000.0
ROOT = 0.7978845608028654
CUBIC = 0.044715
F32 = jnp.float32
BF16 = jnp.bfloat16
MIB = 1024 * 1024
COST = 1000000
LIMITS = {
    "caption_attention": 30,
    "caption_mlp_forward": 40,
    "caption_mlp_backward": 36,
    "caption_mlp_weights": 28,
    "caption_attention_backward": 32,
    "caption_input_backward": 24,
    "caption_attention_weights": 28,
    "vision_attention": 36,
    "vision_attention_rest": 32,
    "vision_mlp": 28,
}


def nn(a, b):
    return lax.dot_general(a, b, (((1,), (0,)), ((), ())), preferred_element_type=F32)


def nt(a, b):
    return lax.dot_general(a, b, (((1,), (1,)), ((), ())), preferred_element_type=F32)


def tn(a, b):
    return lax.dot_general(a, b, (((0,), (0,)), ((), ())), preferred_element_type=F32)


def row(ref):
    return ref[...].astype(F32).reshape(1, -1)


def units(x):
    average = jnp.mean(x, axis=-1, keepdims=True)
    centred = x - average
    variance = jnp.mean(centred * centred, axis=-1, keepdims=True)
    inverse = lax.rsqrt(variance + EPSILON)
    return centred * inverse, inverse


def norm_back(unit, inverse, gain, dy):
    du = dy * gain
    first = jnp.mean(du, axis=-1, keepdims=True)
    second = jnp.mean(du * unit, axis=-1, keepdims=True)
    return (du - first - unit * second) * inverse


def lane_block(slots, rows):
    return lax.broadcasted_iota(jnp.int32, (rows, GROUP), 1) // slots


def two_heads(a):
    lanes = lax.broadcasted_iota(jnp.int32, a.shape, 1)
    low = (lanes < HEAD_DIM).astype(F32).astype(BF16)
    high = (lanes >= HEAD_DIM).astype(F32).astype(BF16)
    return jnp.concatenate([a * low, a * high], axis=0)


def compact(full, slots):
    block = lane_block(slots, slots)
    out = full[:slots]
    for b in range(1, GROUP // slots):
        out = jnp.where(block == b, full[b * slots : (b + 1) * slots], out)
    return out


def spread(part, slots):
    block = lane_block(slots, slots)
    return jnp.concatenate(
        [part * (block == b).astype(F32).astype(BF16) for b in range(GROUP // slots)], axis=0
    )


def attention(q, k, v, allowed, slots):
    scores = nt(two_heads(k), q)
    probs = []
    for a in range(2):
        s = compact(scores[a * GROUP : (a + 1) * GROUP], slots) * (HEAD_DIM**-0.5)
        s = jnp.where(allowed, s, MASKED)
        powered = jnp.exp(s - jnp.max(s, axis=0, keepdims=True))
        probs.append(powered / jnp.sum(powered, axis=0, keepdims=True))
    wide = jnp.concatenate([spread(p.astype(BF16), slots) for p in probs], axis=0)
    return tn(wide, two_heads(v)), probs


def attention_back(q, k, v, probs, dc, slots):
    vv, kk, qq, dd = two_heads(v), two_heads(k), two_heads(q), two_heads(dc)
    dprobs = nt(vv, dc)
    wide_p, wide_s = [], []
    for a in range(2):
        dp = compact(dprobs[a * GROUP : (a + 1) * GROUP], slots)
        p = probs[a]
        ds = p * (dp - jnp.sum(p * dp, axis=0, keepdims=True))
        wide_p.append(spread(p.astype(BF16), slots))
        wide_s.append(spread(ds.astype(BF16), slots))
    dv = nn(jnp.concatenate(wide_p, axis=1), dd)
    dk = nn(jnp.concatenate(wide_s, axis=1), qq)
    dq = tn(jnp.concatenate(wide_s, axis=0), kk)
    scale = HEAD_DIM**-0.5
    return (dq * scale).astype(BF16), (dk * scale).astype(BF16), dv.astype(BF16)


def fetch(pairs, sems, first=0):
    copies = [pltpu.make_async_copy(a, b, sems.at[first + i]) for i, (a, b) in enumerate(pairs)]
    for copy in copies:
        copy.start()
    return copies


def wait(copies):
    for copy in copies:
        copy.wait()


def part(number, size):
    return pl.ds(pl.multiple_of(number * size, size), size)


def thirds(win, held, width):
    return [(win.at[:, t * width : (t + 1) * width], held.at[:, t * width : (t + 1) * width]) for t in range(3)]


def choose(flag, a, b):
    return jnp.where(flag == 0, a, b)


def inward(n1, t, win, bias):
    width = n1.shape[1]
    out = nn(n1, win[:, t * width : (t + 1) * width])
    if t != 1:
        out = out + bias[:, t // 2 * width : (t // 2 + 1) * width]
    return out.astype(BF16)


def attend_forward(
    info, lens, x_hbm, g_hbm, s_hbm, win_hbm, bi_hbm, wo_hbm, bo_hbm,
    mid_ref, ctx_hbm, pk_hbm, pc_hbm, xs, win, wo, g, s, bi, bo, ctx, pk, pc, sems, *, slots,
):
    rows, width = xs.shape
    small = fetch([(g_hbm, g), (s_hbm, s), (bi_hbm, bi), (bo_hbm, bo)], sems)
    copies = fetch([(x_hbm.at[part(info[0], rows)], xs), *thirds(win_hbm, win, width), (wo_hbm, wo)], sems, 4)
    wait(small)
    copies[0].wait()
    unit, _ = units(xs[...].astype(F32))
    n1 = (unit * row(g) + row(s)).astype(BF16)
    for t in range(3):
        copies[1 + t].wait()
        pk[:, t * width : (t + 1) * width] = inward(n1, t, win, row(bi))
    leaving = fetch([(pk, pk_hbm)], sems, 9)
    block = lane_block(slots, 1)
    slot = lax.broadcasted_iota(jnp.int32, (slots, GROUP), 0)
    per = GROUP // slots
    start = info[0] * (rows // slots)
    for n in range(rows // GROUP):
        used = jnp.zeros((1, GROUP), jnp.int32)
        for b in range(per):
            used = jnp.where(block == b, lens[start + n * per + b], used)
        allowed = slot < used
        tokens = slice(n * GROUP, (n + 1) * GROUP)
        for p in range(width // 128):
            q, k, v = (pk[tokens, t * width + p * 128 : t * width + (p + 1) * 128] for t in range(3))
            out, probs = attention(q, k, v, allowed, slots)
            ctx[tokens, p * 128 : (p + 1) * 128] = out.astype(BF16)
            for a in range(2):
                pc[(2 * p + a) * slots : (2 * p + a + 1) * slots, tokens] = probs[a]
    leaving += fetch([(ctx, ctx_hbm), (pc, pc_hbm)], sems, 10)
    copies[4].wait()
    mid_ref[...] = (xs[...].astype(F32) + (nn(ctx[...], wo[...]) + row(bo))).astype(BF16)
    wait(leaving)


def unit_parts(info, we_hbm, wr_hbm, we, wr):
    piece = we.shape[1] // 4
    first, second = [], []
    for z in range(4):
        held = slice(z * piece, (z + 1) * piece)
        begin = part(2 * z + info[0], piece)
        first.append((we_hbm.at[:, begin], we.at[:, held]))
        second.append((wr_hbm.at[begin], wr.at[held]))
    return first, second


def expand_forward(
    info, own_ref, oth_ref, ctx_hbm, cot_hbm, g_hbm, s_hbm, be_hbm, br_hbm, we_hbm, wr_hbm,
    n2_ref, slope_ref, keep_ref, send_ref, outk_ref, outs_ref,
    mid, cot, we, wr, act, g, s, be, br, sems, *, chunk,
):
    tokens, width = mid.shape
    count, half = own_ref.shape[0], width // 2
    c = info[0]
    small = fetch([(g_hbm, g), (s_hbm, s), (be_hbm, be), (br_hbm, br)], sems)
    first, second = unit_parts(info, we_hbm, wr_hbm, we, wr)
    into, out_of = fetch(first, sems, 4), fetch(second, sems, 8)
    last = fetch([(cot_hbm, cot)], sems, 12)
    for k in range(2):
        held = outs_ref.at[tokens + k * count : tokens + (k + 1) * count]
        last += fetch([(ctx_hbm.at[:, k * half : (k + 1) * half], held)], sems, 13 + k)
    mid[part(c, count)] = own_ref[...]
    mid[part(1 - c, count)] = oth_ref[...]
    wait(small)
    for t in range(0, tokens, chunk):
        unit, _ = units(mid[t : t + chunk].astype(F32))
        n2_ref[t : t + chunk] = (unit * row(g) + row(s)).astype(BF16)
    piece = we.shape[1] // 4
    every = row(be)
    bias = jnp.concatenate(
        [choose(c, every[:, 2 * z * piece : (2 * z + 1) * piece], every[:, (2 * z + 1) * piece : (2 * z + 2) * piece]) for z in range(4)],
        axis=1,
    )
    over = row(br)
    over = choose(c, over[:, :half], over[:, half:])
    wait(into)
    wait(out_of)
    for t in range(0, tokens, chunk):
        h = nn(n2_ref[t : t + chunk], we[...]) + bias
        square = h * h
        gate = 0.5 + 0.5 * jnp.tanh(h * (ROOT + (ROOT * CUBIC) * square))
        active = h * gate
        slope = gate + active * (1.0 - gate) * (2.0 * ROOT + (6.0 * CUBIC * ROOT) * square)
        act[t : t + chunk] = active.astype(BF16)
        slope_ref[t : t + chunk] = slope.astype(BF16)
        out = nn(act[t : t + chunk], wr[...])
        old = mid[t : t + chunk].astype(F32)
        outk_ref[t : t + chunk] = choose(c, old[:, :half], old[:, half:]) + (choose(c, out[:, :half], out[:, half:]) + over)
        outs_ref[t : t + chunk] = choose(c, out[:, half:], out[:, :half]).astype(BF16)
    wait(last)
    short = piece // 2
    for z in range(4):
        grad = tn(act[:, z * piece : (z + 1) * piece], cot[...])
        held = slice(z * short, (z + 1) * short)
        keep_ref[held] = choose(info[1], grad[:short], grad[short:]).astype(BF16)
        send_ref[held] = choose(info[1], grad[short:], grad[:short]).astype(BF16)


def expand_backward(
    info, slope_ref, cot_hbm, we_hbm, wr_hbm, dh_ref, db_ref, dk_ref, ds_one, ds_two, cot, we, wr, acc, sems, *, chunk,
):
    tokens, width = cot.shape
    count = dk_ref.shape[0]
    c = info[0]
    first, second = unit_parts(info, we_hbm, wr_hbm, we, wr)
    copies = fetch([(cot_hbm, cot)], sems) + fetch(second, sems, 1)
    later = fetch(first, sems, 5)
    wait(copies)
    total = jnp.zeros((1, slope_ref.shape[1]), F32)
    for t in range(0, tokens, chunk):
        da = nt(cot[t : t + chunk], wr[...])
        dh = (da * slope_ref[t : t + chunk].astype(F32)).astype(BF16)
        dh_ref[t : t + chunk] = dh
        total = total + jnp.sum(dh.astype(F32), axis=0, keepdims=True)
        if t == 0:
            wait(later)
        acc[t : t + chunk] = nt(dh_ref[t : t + chunk], we[...])
    db_ref[...] = total
    dk_ref[...] = acc[part(c, count)]
    ds_one[...] = acc[part(2 * (1 - c), count // 2)].astype(BF16)
    ds_two[...] = acc[part(2 * (1 - c) + 1, count // 2)].astype(BF16)


def split_rows(grad, first, second, bit, cols, short):
    for n in range(grad.shape[0] // (2 * short)):
        low = grad[2 * n * short : (2 * n + 1) * short]
        high = grad[(2 * n + 1) * short : (2 * n + 2) * short]
        first[n * short : (n + 1) * short, cols] = choose(bit, low, high).astype(BF16)
        second[n * short : (n + 1) * short, cols] = choose(bit, high, low).astype(BF16)


def expand_weights(info, n2_ref, dh_ref, outk_ref, far_ref, keep_ref, send_ref, out_ref):
    span = dh_ref.shape[1] // 2
    for j in range(2):
        cols = slice(j * span, (j + 1) * span)
        grad = tn(n2_ref[...], dh_ref[:, cols])
        split_rows(grad, keep_ref, send_ref, info[2], cols, grad.shape[0] // 8)
    out_ref[...] = (outk_ref[...] + far_ref[: out_ref.shape[0]].astype(F32)).astype(BF16)


def attend_backward(
    info, dn_ref, da_one, da_two, mid_ref, cot_hbm, g_hbm, wo_hbm, pk_hbm, pc_hbm,
    dpk, mg_ref, s1, s2, s3, s4, sums_ref, cot, g, wo, pk, pc, dctx, sems, *, slots,
):
    rows, width = mid_ref.shape
    half, wide = width // 2, 3 * width // 2
    c = info[0]
    copies = fetch([(cot_hbm.at[part(c, rows)], cot), (g_hbm, g), (wo_hbm, wo), (pk_hbm, pk), (pc_hbm, pc)], sems)
    wait(copies[:2])
    cotf = cot[...].astype(F32)
    unit, inverse = units(mid_ref[...].astype(F32))
    dn = dn_ref[...] + jnp.concatenate([da_one[...], da_two[...]], axis=0).astype(F32)
    mf = (cotf + norm_back(unit, inverse, row(g), dn)).astype(BF16)
    mg_ref[...] = mf

    def total(a):
        return jnp.sum(a, axis=0, keepdims=True)

    sums = [total(dn * unit), total(dn), total(mf.astype(F32)), total(cotf)]
    copies[2].wait()
    dctx[...] = nt(mf, wo[...]).astype(BF16)
    wait(copies[3:])
    for n in range(rows // GROUP):
        tokens = slice(n * GROUP, (n + 1) * GROUP)
        for p in range(width // 128):
            q, k, v = (pk[tokens, t * width + p * 128 : t * width + (p + 1) * 128] for t in range(3))
            probs = [pc[(2 * p + a) * slots : (2 * p + a + 1) * slots, tokens] for a in range(2)]
            grads = attention_back(q, k, v, probs, dctx[tokens, p * 128 : (p + 1) * 128], slots)
            for t in range(3):
                dpk[tokens, t * width + p * 128 : t * width + (p + 1) * 128] = grads[t]
    sums += [total(dpk[:, :width].astype(F32)), total(dpk[:, 2 * width :].astype(F32))]
    sums_ref[...] = jnp.concatenate(sums + [jnp.zeros((2, width), F32)], axis=0)

    def store(mine):
        s1[...] = dpk[:, mine : mine + half]
        s2[...] = dpk[:, mine + half : mine + width]
        s3[...] = dpk[:, mine + width : mine + wide]
        s4[...] = mg_ref[:, mine // 3 : mine // 3 + half]

    @pl.when(c == 0)
    def _():
        store(wide)

    @pl.when(c == 1)
    def _():
        store(0)


def high_low(v):
    high = v.astype(BF16)
    return high, (v - high.astype(F32)).astype(BF16)


def attend_weights(
    info, x_hbm, g_hbm, s_hbm, dpk, mg, ctx_hbm, far, f1, f2, f3, f4, vec,
    k1, t1, k2, t2, x, g, s, ctx, sems,
):
    rows, half = dpk.shape[0], mg.shape[1] // 2
    c = info[0]
    copies = fetch([(g_hbm, g), (s_hbm, s), (x_hbm.at[part(c, rows)], x.at[:rows]), (x_hbm.at[part(1 - c, rows)], x.at[rows:]), (ctx_hbm, ctx)], sems)
    wait(copies[:4])
    unit, _ = units(x[...].astype(F32))
    x[...] = (unit * row(g) + row(s)).astype(BF16)
    short = k1.shape[0] // 8
    fars = (f1, f2, f3, f4)
    for j in range(4):
        if j < 3:
            left, right = x[:rows], x[rows:]
            mine = dpk[:, pl.ds(pl.multiple_of(c * 3 * half + j * half, 128), half)]
        else:
            copies[4].wait()
            left, right = ctx[...], jnp.concatenate([far[2 * rows : 3 * rows], far[3 * rows :]], axis=1)
            mine = mg[:, pl.ds(pl.multiple_of(c * half, 128), half)]
        grad = tn(left, mine) + tn(right, fars[j][...])
        cols = slice((j % 2) * half, (j % 2 + 1) * half)
        if j < 2:
            split_rows(grad, k1, t1, info[1], cols, short)
        else:
            split_rows(grad, k2, t2, info[2], cols, 2 * short)
    high, low = high_low(vec[...])
    t1[8 * short : 8 * short + 16] = high
    t1[8 * short + 16 :] = low


def input_backward(
    info, x_hbm, g_hbm, win_hbm, dpk, mg, sums_ref, db_ref, cg_hbm, cgs_ref, vec_ref, x, g, win, cgk, sems,
):
    rows, width = x.shape
    half = width // 2
    c = info[0]
    copies = fetch([(x_hbm.at[part(c, rows)], x), (g_hbm, g), (win_hbm, win)], sems)
    wait(copies[:2])
    unit, inverse = units(x[...].astype(F32))
    copies[2].wait()
    dn = nt(dpk[...], win[...])
    out = norm_back(unit, inverse, row(g), dn) + mg[...].astype(F32)
    cgk[...] = choose(c, out[:, :half], out[:, half:]).astype(BF16)
    leaving = fetch([(cgk, cg_hbm.at[part(c, rows)])], sems, 3)
    cgs_ref[...] = choose(c, out[:, half:], out[:, :half]).astype(BF16)
    vec_ref[0:1] = jnp.sum(dn * unit, axis=0, keepdims=True)
    vec_ref[1:2] = jnp.sum(dn, axis=0, keepdims=True)
    vec_ref[2:8] = sums_ref[:6]
    flag = c.astype(F32)
    for z in range(4):
        one = db_ref[:, z * half : (z + 1) * half]
        vec_ref[8 + z : 9 + z, :half] = one * (1.0 - flag)
        vec_ref[8 + z : 9 + z, half:] = one * flag
    vec_ref[12:] = jnp.zeros((4, width), F32)
    wait(leaving)


def vision_heads(n1, win, bias, pk, ctx, images, slots):
    rows = n1.shape[0]
    some = win.shape[1] // 3
    across = some // 128
    pk[:, rows:] = jnp.zeros((pk.shape[0], pk.shape[1] - rows, 128), F32)
    for t in range(3):
        out = nn(n1[...], win[:, t * some : (t + 1) * some])
        if bias[t] is not None:
            out = out + bias[t]
        out = out.astype(BF16).astype(F32)
        for p in range(across):
            pk[t * across + p, :rows] = out[:, p * 128 : (p + 1) * 128]
    allowed = lax.broadcasted_iota(jnp.int32, (slots, GROUP), 0) < rows // images
    per = GROUP // slots
    for i in range(0, images, per):
        for p in range(across):

            def load(t):
                parts = [pk[t * across + p, pl.ds(i + b, slots, stride=images)] for b in range(per)]
                return jnp.concatenate(parts, axis=0).astype(BF16)

            out, _ = attention(load(0), load(1), load(2), allowed, slots)
            for b in range(per):
                ctx[p, pl.ds(i + b, slots, stride=images)] = out[b * slots : (b + 1) * slots]
    return jnp.concatenate([ctx[p, :rows].astype(BF16) for p in range(across)], axis=1)


def some_columns(win_hbm, win, begin, width):
    some = win.shape[1] // 3
    return [(win_hbm.at[:, t * width + begin : t * width + begin + some], win.at[:, t * some : (t + 1) * some]) for t in range(3)]


def vision_attend_one(
    x_hbm, g_hbm, s_hbm, win_hbm, bi_hbm, n1_ref, ctx_ref, token, x, win, g, s, bi, pk, ctx, sems, *, images, slots,
):
    rows, width = x.shape
    copies = fetch([(x_hbm, x), (g_hbm, g), (s_hbm, s), (bi_hbm, bi)], sems)
    later = fetch(some_columns(win_hbm, win, 0, width), sems, 4)
    wait(copies)
    unit, _ = units(x[...].astype(F32))
    n1_ref[...] = (unit * row(g) + row(s)).astype(BF16)
    wait(later)
    some = win.shape[1] // 3
    every = row(bi)
    bias = (every[:, :some], None, every[:, width : width + some])
    ctx_ref[...] = vision_heads(n1_ref, win, bias, pk, ctx, images, slots)
    token[...] = jnp.zeros(token.shape, F32)


def vision_attend_two(
    n1_ref, ctx_ref, x_hbm, win_hbm, bi_hbm, wo_hbm, bo_hbm, mid_ref, token,
    x, win, wo, bi, bo, pk, ctx, sems, *, images, slots,
):
    rows, width = x.shape
    some = win.shape[1] // 3
    later = fetch([(bi_hbm, bi), *some_columns(win_hbm, win, width - some, width)], sems)
    last = fetch([(x_hbm, x), (bo_hbm, bo), (wo_hbm, wo)], sems, 4)
    wait(later)
    every = row(bi)
    bias = (every[:, width - some : width], None, every[:, 2 * width - some :])
    context = vision_heads(n1_ref, win, bias, pk, ctx, images, slots)
    context = jnp.concatenate([ctx_ref[...], context], axis=1)
    wait(last)
    mid_ref[...] = x[...].astype(F32) + (nn(context, wo[...]) + row(bo))
    token[...] = jnp.zeros(token.shape, F32)


def vision_expand(mid_hbm, g_hbm, s_hbm, be_hbm, br_hbm, we, wr, *refs, begin):
    out_hbm, token, mid, g, s, be, br, n2, act, out, sems = refs[-11:]
    rows, width = mid.shape
    images = out.shape[1]
    copies = fetch([(mid_hbm.at[begin : begin + rows], mid), (g_hbm, g), (s_hbm, s), (be_hbm, be), (br_hbm, br)], sems)
    wait(copies)
    unit, _ = units(mid[...])
    n2[...] = (unit * row(g) + row(s)).astype(BF16)
    bias = row(be)
    for f in range(we.shape[1] // width):
        cols = slice(f * width, (f + 1) * width)
        h = nn(n2[...], we[:, cols]) + bias[:, cols]
        gate = 0.5 + 0.5 * jnp.tanh(h * (ROOT + (ROOT * CUBIC) * (h * h)))
        act[:, cols] = (h * gate).astype(BF16)
    result = mid[...] + (nn(act[...], wr[...]) + row(br))
    out[...] = result.astype(BF16).reshape(out.shape)
    token[...] = jnp.zeros(token.shape, F32)
    wait(fetch([(out, out_hbm.at[begin // images : (begin + rows) // images])], sems, 5))


def summed(parts, size, cols=slice(None)):
    total = None
    for ref, begin in parts:
        if not isinstance(begin, int):
            begin = pl.multiple_of(begin, 16)
        one = ref[pl.ds(begin, size), cols].astype(F32)
        total = one if total is None else total + one
    return total


def places(info):
    return info[1], info[2], info[3], info[4]


def fold_a_zl(info, a0, a1, a_out):
    x, y, zl, zh = places(info)
    size = a_out.shape[0] // 2
    for h in range(2):
        at = (2 * h + 1 - zl) * size
        a_out[h * size : (h + 1) * size] = summed([(a0, at), (a1, at)], size).astype(BF16)


def fold_a_zh_b_x(info, a0, a1, a2, b0, b1, a_out, b_out):
    x, y, zl, zh = places(info)
    size, unit = a_out.shape[0], b_out.shape[0] // 4
    at = (2 * (1 - zh) + zl) * size
    a_out[...] = summed([(a0, at), (a1, at), (a2, (1 - zh) * size)], size).astype(BF16)
    for z in range(4):
        at = (2 * z + 1 - x) * unit
        b_out[z * unit : (z + 1) * unit] = summed([(b0, at), (b1, at)], unit).astype(BF16)


def fold_c(info, c0, c1, d0, d1, vec, c_out, d_out, v_out):
    x, y, zl, zh = places(info)
    unit = d_out.shape[0] // 4
    for q in range(4):
        held = slice(q * unit, (q + 1) * unit)
        at = (2 * q + 1 - y) * unit
        c_out[held] = summed([(c0, at), (c1, at)], unit).astype(BF16)
        at = (2 * q + 1 - x) * unit
        d_out[held] = summed([(d0, at), (d1, at)], unit).astype(BF16)
    v = vec[...] + (c1[8 * unit : 8 * unit + 16].astype(F32) + c1[8 * unit + 16 :].astype(F32))
    v_out[...] = v
    c_out[4 * unit : 4 * unit + 16], c_out[4 * unit + 16 :] = high_low(v)


def fold_a_y_b_zl(info, a0, a1, a2, a3, b0, b1, b2, a_out, b_out):
    x, y, zl, zh = places(info)
    size, unit = a_out.shape[0], b_out.shape[0] // 2
    at = (2 * zh + zl) * size
    a_out[...] = summed([(a0, at), (a1, at), (a2, zh * size), (a3, 0)], size).astype(BF16)
    for h in range(2):
        z = 2 * h + 1 - zl
        at = (2 * z + x) * unit
        b_out[h * unit : (h + 1) * unit] = summed([(b0, at), (b1, at), (b2, z * unit)], unit).astype(BF16)


def fold_a_b_zh_c_zl(
    info, a4, a5, b0, b1, b2, b3, c0, c1, c2, d0, d1, d2, vec, a_out, b_out, e_out, v_out
):
    x, y, zl, zh = places(info)
    unit, width = b_out.shape[0], a_out.shape[1]
    a_out[...] = (a4[...].astype(F32) + a5[...].astype(F32)).astype(BF16)
    z = 2 * (1 - zh) + zl
    at = (2 * z + x) * unit
    b_out[...] = summed([(b0, at), (b1, at), (b2, z * unit), (b3, (1 - zh) * unit)], unit).astype(BF16)
    for h in range(2):
        held = slice(h * unit, (h + 1) * unit)
        q = 2 * h + 1 - zl
        at = (2 * q + y) * unit
        e_out[held, :width] = summed([(c0, at), (c1, at), (c2, q * unit)], unit).astype(BF16)
        at = (2 * q + x) * unit
        e_out[held, width:] = summed([(d0, at), (d1, at), (d2, q * unit)], unit).astype(BF16)
    v = vec[...] + (c2[4 * unit : 4 * unit + 16].astype(F32) + c2[4 * unit + 16 :].astype(F32))
    v_out[...] = v
    e_out[2 * unit :, :width], e_out[2 * unit :, width:] = high_low(v)


def fold_b_c_zh(info, b0, b1, b2, b3, b4, c0, c1, c2, d0, d1, d2, e3, vec, b_out, e_out, v_out):
    x, y, zl, zh = places(info)
    unit, width = b_out.shape[0], vec.shape[1]
    z = 2 * zh + zl
    at = (2 * z + x) * unit
    parts = [(b0, at), (b1, at), (b2, z * unit), (b3, zh * unit), (b4, 0)]
    b_out[...] = summed(parts, unit).astype(BF16)
    settle(info, 1 - zh, c0, c1, c2, d0, d1, d2, [(e3, (1 - zh) * unit)], e_out, 0, unit)
    v = vec[...] + (e3[2 * unit :, :width].astype(F32) + e3[2 * unit :, width:].astype(F32))
    v_out[...] = v
    e_out[unit:, :width], e_out[unit:, width:] = high_low(v)


def settle(info, zh, c0, c1, c2, d0, d1, d2, more, out, begin, unit):
    x, y, zl, _ = places(info)
    width = out.shape[1] // 2
    q = 2 * zh + zl
    at = (2 * q + y) * unit
    first = summed([(c0, at), (c1, at), (c2, q * unit)], unit) + summed(more, unit, slice(0, width))
    at = (2 * q + x) * unit
    second = summed([(d0, at), (d1, at), (d2, q * unit)], unit) + summed(more, unit, slice(width, 2 * width))
    out[begin : begin + unit, :width] = first.astype(BF16)
    out[begin : begin + unit, width:] = second.astype(BF16)


def fold_last(info, b_own, c0, c1, c2, d0, d1, d2, e3, e4, vec, out):
    x, y, zl, zh = places(info)
    unit, width = b_own.shape[0], vec.shape[1]
    out[:unit] = b_own[...]
    settle(info, zh, c0, c1, c2, d0, d1, d2, [(e3, zh * unit), (e4, 0)], out, unit, unit)
    v = vec[...] + (e4[unit:, :width].astype(F32) + e4[unit:, width:].astype(F32))
    out[2 * unit :, :width], out[2 * unit :, width:] = high_low(v)


def assemble(
    info, a_own, a_far, f_own, f_far, cg_far, cg_in, a_ref, b_ref, in_ref, out_ref, *refs, ranks
):
    vectors, (cg_hbm, sems) = refs[:8], refs[8:]
    c = info[0]
    rows = cg_far.shape[0]
    leaving = fetch([(cg_far, cg_hbm.at[part(1 - c, rows)])], sems)
    a_ref[...] = choose(c ^ info[2], a_own[...].astype(F32), a_far[...].astype(F32))
    share, hidden = b_ref.shape
    piece = hidden // 8
    wide, half = in_ref.shape[1] // 2, out_ref.shape[1] // 2
    mine, far = f_own[...].astype(F32), f_far[...].astype(F32)
    low, high = choose(c, mine, far), choose(c, far, mine)
    for z in range(4):
        held = slice(z * piece, (z + 1) * piece)
        b_ref[:, 2 * z * piece : (2 * z + 1) * piece] = low[:share, held]
        b_ref[:, (2 * z + 1) * piece : (2 * z + 2) * piece] = high[:share, held]
    in_ref[:, :wide] = low[share : 2 * share, :wide]
    in_ref[:, wide:] = high[share : 2 * share, :wide]
    out_ref[:, :half] = low[share : 2 * share, wide:]
    out_ref[:, half:] = high[share : 2 * share, wide:]
    width = out_ref.shape[1]
    one, two = f_own[2 * share :].astype(F32), f_far[2 * share :].astype(F32)
    total = (one[:, :width] + one[:, width:]) + (two[:, :width] + two[:, width:])
    place = info[5]
    first = 0
    for ref, number in zip(vectors, (1, 1, 1, 1, 1, 1, 2, 4)):
        size = number * width // ranks
        offset = place * size
        which = offset // width
        taken = total[first : first + 1]
        for k in range(1, number):
            taken = jnp.where(which == k, total[first + k : first + k + 1], taken)
        turn = lax.rem(width - lax.rem(offset, width), width)
        turned = pltpu.roll(jnp.concatenate([taken] * 8, axis=0), turn, 1)
        ref[...] = turned[:1, :size].reshape(size)
        first += number
    wait(leaving)


def shape(dims, dtype=BF16):
    return jax.ShapeDtypeStruct(dims, dtype)


def whole(dims):
    return pl.BlockSpec(dims, lambda *_: (0,) * len(dims))


HBM = pl.BlockSpec(memory_space=pltpu.HBM)
FAR = pl.BlockSpec(memory_space=pl.ANY)


def kernel(body, name, ins, outs, scratch, args, scalars=(), aliases=None, after=()):
    first, extra = len(scalars) + len(args), len(after)

    def run(*refs):
        return body(*refs[:first], *refs[first + extra :])

    specs = pltpu.PrefetchScalarGridSpec(
        num_scalar_prefetch=len(scalars),
        grid=(1,),
        in_specs=[HBM if far else whole(a.shape) for far, a in zip(ins, args, strict=True)] + [FAR] * extra,
        out_specs=[HBM if far else whole(s.shape) for far, s in outs],
        scratch_shapes=scratch,
    )
    return pl.pallas_call(
        run,
        name=name,
        grid_spec=specs,
        out_shape=[pltpu.HBM(s.shape, s.dtype) if far is True else s for far, s in outs],
        compiler_params=pltpu.CompilerParams(
            vmem_limit_bytes=LIMITS.get(name, 16) * MIB, dimension_semantics=("arbitrary",)
        ),
        cost_estimate=pl.CostEstimate(flops=COST, bytes_accessed=1000, transcendentals=0),
        input_output_aliases=aliases or {},
    )(*scalars, *(pltpu.with_memory_space_constraint(a, pltpu.HBM) if far is True else a for far, a in zip(ins, args)), *after)


BITS = {"x": 0, "y": 1, "zl": 2, "zh": 3}


def on_device(
    captions, caption_lengths, caption_cotangent,
    first_gain, first_shift, project_in, inward_bias, project_out, outward_bias,
    second_gain, second_shift, expand_weight, expand_bias, reduce_weight, reduce_bias,
    patches,
    vision_first_gain, vision_first_shift, vision_project_in, vision_inward_bias, vision_project_out, vision_outward_bias,
    vision_second_gain, vision_second_shift, vision_expand_weight, vision_expand_bias, vision_reduce_weight, vision_reduce_bias,
):
    count, slots, width = captions.shape
    hidden = expand_weight.shape[1]
    tokens = count * slots
    own = tokens // 2
    half = width // 2
    units_own = hidden // 2
    heads = width // HEAD_DIM
    unit = width // 16
    quarter = hidden // 16
    ranks = lax.axis_size("dp")
    low = (ranks // 16).bit_length() - 1
    core = lax.axis_index("section")
    place = lax.axis_index("dp")
    info = jnp.stack([core] + [(place >> (low + b)) & 1 for b in range(4)] + [place]).astype(jnp.int32)
    x = captions.reshape(tokens, width)
    cot = caption_cotangent.reshape(tokens, width)
    dma = pltpu.SemaphoreType.DMA

    def hop(value, bit, only=None):
        step = 1 << (low + BITS[bit])
        pairs = []
        for k in range(2):
            for d in range(ranks):
                if only is None or only(k, (d >> (low + 1)) & 1):
                    pairs.append((k * ranks + d, k * ranks + (d ^ step)))
        return lax.ppermute(value, ("section", "dp"), pairs)

    def swap(value):
        return lax.ppermute(value, "section", [(0, 1), (1, 0)])

    def vmem(dims, dtype=BF16):
        return pltpu.VMEM(dims, dtype)

    line = vmem((width,))

    def fold(body, args, outs, after):
        return kernel(body, body.__name__, [False] * len(args), [(False, s) for s in outs], [], args, (info,), after=after)

    middle, context, packed, probs = kernel(
        partial(attend_forward, slots=slots), "caption_attention",
        [True] * 7,
        [(False, shape((own, width))), (True, shape((own, width))), (True, shape((own, 3 * width))),
         (True, shape((heads * slots, own), F32))],
        [vmem((own, width)), vmem(project_in.shape), vmem(project_out.shape), line, line, vmem(inward_bias.shape), line,
         vmem((own, width)), vmem((own, 3 * width)), vmem((heads * slots, own), F32), dma((12,))],
        (x, first_gain, first_shift, project_in, inward_bias, project_out, outward_bias),
        (info, caption_lengths),
    )
    middle_far = swap(middle)

    held = [vmem((width, units_own)), vmem((units_own, width))]
    n2, slope, a0, a_send, out_keep, out_send = kernel(
        partial(expand_forward, chunk=256), "caption_mlp_forward",
        [False, False] + [True] * 8,
        [(False, shape((tokens, width))), (False, shape((tokens, units_own))),
         (False, shape((4 * quarter, width))), (False, shape((4 * quarter, width))),
         (False, shape((tokens, half), F32)), (False, shape((2 * tokens, half)))],
        [vmem((tokens, width)), vmem((tokens, width)), *held, vmem((tokens, units_own)),
         line, line, vmem((hidden,)), line, dma((15,))],
        (middle, middle_far, context, cot, second_gain, second_shift, expand_bias, reduce_bias, expand_weight, reduce_weight),
        (info,),
    )
    a1 = hop(a_send, "x")
    out_far = swap(out_send)

    dh, db, dn_keep, dn_one, dn_two = kernel(
        partial(expand_backward, chunk=256), "caption_mlp_backward",
        [False, True, True, True],
        [(False, shape((tokens, units_own))), (False, shape((1, units_own), F32)),
         (False, shape((own, width), F32)), (False, shape((own // 2, width))), (False, shape((own // 2, width)))],
        [vmem((tokens, width)), *held, vmem((tokens, width), F32), dma((9,))],
        (slope, cot, expand_weight, reduce_weight), (info,),
    )
    dn_one, dn_two = swap(dn_one), swap(dn_two)
    b0, b_send, caption_output = kernel(
        expand_weights, "caption_mlp_weights", [False] * 4,
        [(False, shape((8 * unit, units_own)))] * 2 + [(False, shape((tokens, half)))],
        [], (n2, dh, out_keep, out_far), (info,), after=(dn_keep,),
    )
    b1 = hop(b_send, "y")

    dpk, mg, p1, p2, p3, p4, sums = kernel(
        partial(attend_backward, slots=slots), "caption_attention_backward",
        [False] * 4 + [2] * 3 + [True, True],
        [(False, shape((own, 3 * width))), (False, shape((own, width)))]
        + [(False, shape((own, half)))] * 4 + [(False, shape((8, width), F32))],
        [vmem((own, width)), line, vmem(project_out.shape), vmem((own, 3 * width)), vmem((heads * slots, own), F32),
         vmem((own, width)), dma((5,))],
        (dn_keep, dn_one, dn_two, middle, cot, second_gain, project_out, packed, probs),
        (info,), after=(b0,),
    )
    f1, f2, f3, f4 = swap(p1), swap(p2), swap(p3), swap(p4)

    cg_half, cg_send, vectors = kernel(
        input_backward, "caption_input_backward",
        [True] * 3 + [False] * 4,
        [(True, shape((tokens, half))), (False, shape((own, half))), (False, shape((16, width), F32))],
        [vmem((own, width)), line, vmem(project_in.shape), vmem((own, half)), dma((4,))],
        (x, first_gain, project_in, dpk, mg, sums, db), (info,),
    )
    cg_far = swap(cg_send)
    (a_send,) = fold(fold_a_zl, (a0, a1), [shape((2 * quarter, width))], (vectors,))
    a2 = hop(a_send, "zl")

    c0, c_send, d0, d_send = kernel(
        attend_weights, "caption_attention_weights",
        [True] * 3 + [False] * 2 + [True] + [False] * 6,
        [(False, shape((8 * unit, width))), (False, shape((8 * unit + 32, width))),
         (False, shape((8 * unit, width))), (False, shape((8 * unit, width)))],
        [vmem((tokens, width)), line, line, vmem((own, width)), dma((5,))],
        (x, first_gain, first_shift, dpk, mg, context, out_far, f1, f2, f3, f4, vectors), (info,), after=(a_send,),
    )
    c1 = hop(c_send, "x")
    d1 = hop(d_send, "y")

    images, used, _ = patches.shape
    flat = jnp.transpose(patches, (1, 0, 2)).reshape(used * images, width)
    padded = 64
    four = 2 * width // 3
    token_out = (False, shape((8, 128), F32))
    n1, context, token = kernel(
        partial(vision_attend_one, images=images, slots=padded), "vision_attention", [True] * 5,
        [(False, shape(flat.shape)), (False, shape((used * images, four))), token_out],
        [vmem(flat.shape), vmem((width, 3 * four)), line, line, vmem(vision_inward_bias.shape),
         vmem((3 * four // 128, padded * images, 128), F32), vmem((four // 128, padded * images, 128), F32), dma((7,))],
        (flat, vision_first_gain, vision_first_shift, vision_project_in, vision_inward_bias), after=(c0,),
    )
    a_send, b_send = fold(
        fold_a_zh_b_x, (a0, a1, a2, b0, b1), [shape((quarter, width)), shape((4 * unit, units_own))], (token,),
    )
    a3, b2 = hop(a_send, "zh"), hop(b_send, "x")
    two = width - four
    vision_middle, token = kernel(
        partial(vision_attend_two, images=images, slots=padded), "vision_attention_rest", [False] * 2 + [True] * 5,
        [(False, shape(flat.shape, F32)), token_out],
        [vmem(flat.shape), vmem((width, 3 * two)), vmem(vision_project_out.shape), vmem(vision_inward_bias.shape), line,
         vmem((3 * two // 128, padded * images, 128), F32), vmem((two // 128, padded * images, 128), F32), dma((7,))],
        (n1, context, flat, vision_project_in, vision_inward_bias, vision_project_out, vision_outward_bias),
        after=(a_send,),
    )

    def vision_second(begin, size, before, after):
        return kernel(
            partial(vision_expand, begin=begin * images), "vision_mlp",
            [True] * 5 + [False] * 2 + [True] * len(before),
            [(True, shape((used, images, width))), (False, shape((8, 128), F32))],
            [vmem((size * images, width), F32), line, line, vmem((hidden,)), line,
             vmem((size * images, width)), vmem((size * images, hidden)), vmem((size, images, width)), dma((6,))],
            (vision_middle, vision_second_gain, vision_second_shift, vision_expand_bias,
             vision_reduce_bias, vision_expand_weight, vision_reduce_weight) + before,
            aliases={7: 0} if before else None, after=after,
        )

    c_send, d_send, vectors = fold(
        fold_c, (c0, c1, d0, d1, vectors),
        [shape((4 * unit + 32, width)), shape((4 * unit, width)), shape((16, width), F32)], (token,),
    )
    c2, d2 = hop(c_send, "y"), hop(d_send, "x")
    first = (2 * used // 5 + 1) // 2 * 2
    vision_output, token = vision_second(0, first, (), (d_send,))

    a4, b_send = fold(
        fold_a_y_b_zl, (a0, a1, a2, a3, b0, b1, b2), [shape((quarter, width)), shape((2 * unit, units_own))], (token,),
    )
    a5, b3 = hop(a4, "y", lambda k, y: k != y), hop(b_send, "zl")
    second = (used - first) // 2
    vision_output, token = vision_second(first, second, (vision_output,), (a4,))

    a_own, b_send, e_send, vectors = fold(
        fold_a_b_zh_c_zl, (a4, a5, b0, b1, b2, b3, c0, c1, c2, d0, d1, d2, vectors),
        [shape((quarter, width)), shape((unit, units_own)), shape((2 * unit + 16, 2 * width)), shape((16, width), F32)],
        (token,),
    )
    b4, e3 = hop(b_send, "zh"), hop(e_send, "zl")
    vision_output, token = vision_second(first + second, used - first - second, (vision_output,), (a_own,))

    b_own, e_send, vectors = fold(
        fold_b_c_zh, (b0, b1, b2, b3, b4, c0, c1, c2, d0, d1, d2, e3, vectors),
        [shape((unit, units_own)), shape((unit + 16, 2 * width)), shape((16, width), F32)], (token,),
    )
    e4 = hop(e_send, "zh")
    (final,) = fold(
        fold_last, (b_own, c0, c1, c2, d0, d1, d2, e3, e4, vectors), [shape((2 * unit + 16, units_own))], (),
    )
    if low:
        groups = [list(range(i, i + (1 << low))) for i in range(0, ranks, 1 << low)]

        def scattered(value):
            return lax.psum_scatter(value, "dp", scatter_dimension=0, tiled=True, axis_index_groups=groups)

        a_own = scattered(a_own)
        total = final[2 * unit :].astype(F32)
        total = lax.psum(total[:, :width] + total[:, width:], "dp", axis_index_groups=groups)
        final = jnp.concatenate(
            [scattered(final[:unit]), scattered(final[unit : 2 * unit]), jnp.concatenate(high_low(total), axis=1)]
        )
    a_away = swap(a_own)
    away = swap(final)
    share = width // ranks
    sizes = [share] * 6 + [2 * share, 4 * share]
    reduce_grad, expand_grad, in_grad, out_grad, *shares, captions_gradient = kernel(
        partial(assemble, ranks=ranks), "assemble", [False] * 5 + [True],
        [(False, shape((4 * share, width), F32)), (False, shape((share, hidden), F32)),
         (False, shape((share, 3 * width), F32)), (False, shape((share, width), F32))]
        + [(False, shape((n,), F32)) for n in sizes] + [(True, shape((tokens, half)))],
        [dma((1,))], (a_own, a_away, final, away, cg_far, cg_half), (info,), aliases={6: 12},
    )
    return (
        jnp.transpose(vision_output, (1, 0, 2)), caption_output.reshape(count, slots, half),
        captions_gradient.reshape(count, slots, half),
        shares[0], shares[1], in_grad, shares[6], out_grad, shares[4],
        shares[2], shares[3], expand_grad, shares[7], reduce_grad, shares[5],
    )


def solution(mesh):
    spread_all = P(("section", "dp"), None, None)
    placed = (P("dp", None, None), P("dp"), P("dp", None, None)) + (P(),) * 12 + (spread_all,) + (P(),) * 12
    features = P("dp", None, "section")
    return jax.shard_map(
        on_device,
        mesh=mesh,
        in_specs=placed,
        out_specs=(
            spread_all, features, features,
            P("dp"), P("dp"), P("dp", None), P("dp"), P("dp", None), P("dp"),
            P("dp"), P("dp"), P("dp", None), P("dp"), P("dp", None), P("dp"),
        ),
        check_vma=False,
    )
```

```python
from functools import partial

import jax
import jax.experimental.pallas as pl
import jax.numpy as jnp
from jax import lax
from jax.experimental.pallas import tpu as pltpu
from jax.sharding import PartitionSpec as P

HEAD_DIM = 64
GROUP = 128
EPSILON = 1e-06
MASKED = -1000000000.0
ROOT = 0.7978845608028654
CUBIC = 0.044715
F32 = jnp.float32
BF16 = jnp.bfloat16
MIB = 1024 * 1024
COST = 1000000
LIMITS = {
    "caption_attention": 14,
    "caption_mlp_forward": 22,
    "caption_mlp_backward": 14,
    "caption_mlp_weights": 16,
    "caption_attention_backward": 16,
    "caption_input_backward": 14,
    "caption_attention_weights": 14,
    "vision_attention": 26,
    "vision_attention_rest": 20,
    "vision_mlp": 16,
}


def nn(a, b):
    return lax.dot_general(a, b, (((1,), (0,)), ((), ())), preferred_element_type=F32)


def nt(a, b):
    return lax.dot_general(a, b, (((1,), (1,)), ((), ())), preferred_element_type=F32)


def tn(a, b):
    return lax.dot_general(a, b, (((0,), (0,)), ((), ())), preferred_element_type=F32)


def row(ref):
    return ref[...].astype(F32).reshape(1, -1)


def units(x):
    average = jnp.mean(x, axis=-1, keepdims=True)
    centred = x - average
    variance = jnp.mean(centred * centred, axis=-1, keepdims=True)
    inverse = lax.rsqrt(variance + EPSILON)
    return centred * inverse, inverse


def norm_back(unit, inverse, gain, dy):
    du = dy * gain
    first = jnp.mean(du, axis=-1, keepdims=True)
    second = jnp.mean(du * unit, axis=-1, keepdims=True)
    return (du - first - unit * second) * inverse


def lane_block(slots, rows):
    return lax.broadcasted_iota(jnp.int32, (rows, GROUP), 1) // slots


def two_heads(a):
    lanes = lax.broadcasted_iota(jnp.int32, a.shape, 1)
    low = (lanes < HEAD_DIM).astype(F32).astype(BF16)
    high = (lanes >= HEAD_DIM).astype(F32).astype(BF16)
    return jnp.concatenate([a * low, a * high], axis=0)


def compact(full, slots):
    block = lane_block(slots, slots)
    out = full[:slots]
    for b in range(1, GROUP // slots):
        out = jnp.where(block == b, full[b * slots : (b + 1) * slots], out)
    return out


def spread(part, slots):
    block = lane_block(slots, slots)
    return jnp.concatenate(
        [part * (block == b).astype(F32).astype(BF16) for b in range(GROUP // slots)], axis=0
    )


def attention(q, k, v, allowed, slots):
    scores = nt(two_heads(k), q)
    probs = []
    for a in range(2):
        s = compact(scores[a * GROUP : (a + 1) * GROUP], slots) * (HEAD_DIM**-0.5)
        s = jnp.where(allowed, s, MASKED)
        powered = jnp.exp(s - jnp.max(s, axis=0, keepdims=True))
        probs.append(powered / jnp.sum(powered, axis=0, keepdims=True))
    wide = jnp.concatenate([spread(p.astype(BF16), slots) for p in probs], axis=0)
    return tn(wide, two_heads(v)), probs


def attention_back(q, k, v, probs, dc, slots):
    vv, kk, qq, dd = two_heads(v), two_heads(k), two_heads(q), two_heads(dc)
    dprobs = nt(vv, dc)
    wide_p, wide_s = [], []
    for a in range(2):
        dp = compact(dprobs[a * GROUP : (a + 1) * GROUP], slots)
        p = probs[a]
        ds = p * (dp - jnp.sum(p * dp, axis=0, keepdims=True))
        wide_p.append(spread(p.astype(BF16), slots))
        wide_s.append(spread(ds.astype(BF16), slots))
    dv = nn(jnp.concatenate(wide_p, axis=1), dd)
    dk = nn(jnp.concatenate(wide_s, axis=1), qq)
    dq = tn(jnp.concatenate(wide_s, axis=0), kk)
    scale = HEAD_DIM**-0.5
    return (dq * scale).astype(BF16), (dk * scale).astype(BF16), dv.astype(BF16)


def fetch(pairs, sems, first=0):
    copies = [pltpu.make_async_copy(a, b, sems.at[first + i]) for i, (a, b) in enumerate(pairs)]
    for copy in copies:
        copy.start()
    return copies


def wait(copies):
    for copy in copies:
        copy.wait()


def part(number, size):
    return pl.ds(pl.multiple_of(number * size, size), size)


def thirds(win, held, width):
    return [(win.at[:, t * width : (t + 1) * width], held.at[:, t * width : (t + 1) * width]) for t in range(3)]


def choose(flag, a, b):
    return jnp.where(flag == 0, a, b)


def inward(n1, t, win, bias):
    width = n1.shape[1]
    out = nn(n1, win[:, t * width : (t + 1) * width])
    if t != 1:
        out = out + bias[:, t // 2 * width : (t // 2 + 1) * width]
    return out.astype(BF16)


def attend_forward(
    info, lens_hbm, x_hbm, cot_hbm, win_hbm, wo_hbm, we_hbm, wr_hbm, *refs, slots,
):
    small, refs = refs[:8], refs[8:]
    mid_ref, x, cot, win, wo, we, wr, vec, pk, pc, ctx_hbm, n1_hbm, *refs = refs
    lens, lines, ctx, n1, sems = refs[0], refs[1:9], *refs[9:]
    rows, width = x.shape
    first = fetch([(lens_hbm, lens), *zip(small, lines)], sems)
    copies = fetch([(x_hbm.at[part(info[0], rows)], x), *thirds(win_hbm, win, width), (wo_hbm, wo)], sems, 9)
    into, out_of = unit_parts(info, we_hbm, wr_hbm, we, wr)
    resident = fetch([*into, *out_of, (cot_hbm, cot)], sems, 14)
    wait(first)
    at = 0
    for line in lines:
        for k in range(line.shape[0] // width):
            vec[at : at + 1] = line[k * width : (k + 1) * width].astype(F32).reshape(1, width)
            at += 1
    copies[0].wait()
    unit, _ = units(x[...].astype(F32))
    n1[...] = (unit * vec[0:1] + vec[1:2]).astype(BF16)
    leaving = fetch([(n1, n1_hbm)], sems, 23)
    for t in range(3):
        copies[1 + t].wait()
        out = nn(n1[...], win[:, t * width : (t + 1) * width])
        if t != 1:
            out = out + vec[2 + t // 2 : 3 + t // 2]
        pk[:, t * width : (t + 1) * width] = out.astype(BF16)
    block = lane_block(slots, 1)
    slot = lax.broadcasted_iota(jnp.int32, (slots, GROUP), 0)
    per = GROUP // slots
    start = info[0] * (rows // slots)
    for n in range(rows // GROUP):
        used = jnp.zeros((1, GROUP), jnp.int32)
        for b in range(per):
            used = jnp.where(block == b, lens[start + n * per + b], used)
        allowed = slot < used
        tokens = slice(n * GROUP, (n + 1) * GROUP)
        for p in range(width // 128):
            q, k, v = (pk[tokens, t * width + p * 128 : t * width + (p + 1) * 128] for t in range(3))
            out, probs = attention(q, k, v, allowed, slots)
            ctx[tokens, p * 128 : (p + 1) * 128] = out.astype(BF16)
            for a in range(2):
                pc[(2 * p + a) * slots : (2 * p + a + 1) * slots, tokens] = probs[a]
    leaving += fetch([(ctx, ctx_hbm)], sems, 24)
    copies[4].wait()
    mid_ref[...] = (x[...].astype(F32) + (nn(ctx[...], wo[...]) + vec[4:5])).astype(BF16)
    wait(leaving + resident)


def unit_parts(info, we_hbm, wr_hbm, we, wr):
    piece = we.shape[1] // 4
    first, second = [], []
    for z in range(4):
        held = slice(z * piece, (z + 1) * piece)
        begin = part(2 * z + info[0], piece)
        first.append((we_hbm.at[:, begin], we.at[:, held]))
        second.append((wr_hbm.at[begin], wr.at[held]))
    return first, second


def expand_forward(
    info, own_ref, oth_ref, cot, we, wr, vec, ctx_hbm, n1_hbm,
    n2_ref, slope_ref, keep_ref, send_ref, outk_ref, outs_ref, mid, act, sems, *, chunk,
):
    tokens, width = mid.shape
    count, half = own_ref.shape[0], width // 2
    c = info[0]
    across = []
    for k, (source, at) in enumerate(((ctx_hbm, 0), (ctx_hbm, half), (n1_hbm, 0), (n1_hbm, half))):
        held = outs_ref.at[tokens + k * count : tokens + (k + 1) * count]
        across += fetch([(source.at[:, at : at + half], held)], sems, k)
    mid[part(c, count)] = own_ref[...]
    mid[part(1 - c, count)] = oth_ref[...]
    bias = jnp.concatenate([choose(c, vec[z : z + 1, :half], vec[z : z + 1, half:]) for z in range(7, 11)], axis=1)
    over = choose(c, vec[11:12, :half], vec[11:12, half:])
    for t in range(0, tokens, chunk):
        old = mid[t : t + chunk].astype(F32)
        unit, _ = units(old)
        n2 = (unit * vec[5:6] + vec[6:7]).astype(BF16)
        n2_ref[t : t + chunk] = n2
        h = nn(n2, we[...]) + bias
        square = h * h
        gate = 0.5 + 0.5 * jnp.tanh(h * (ROOT + (ROOT * CUBIC) * square))
        active = h * gate
        slope = gate + active * (1.0 - gate) * (2.0 * ROOT + (6.0 * CUBIC * ROOT) * square)
        act[t : t + chunk] = active.astype(BF16)
        slope_ref[t : t + chunk] = slope.astype(BF16)
        out = nn(act[t : t + chunk], wr[...])
        outk_ref[t : t + chunk] = choose(c, old[:, :half], old[:, half:]) + (choose(c, out[:, :half], out[:, half:]) + over)
        outs_ref[t : t + chunk] = choose(c, out[:, half:], out[:, :half]).astype(BF16)
    piece = act.shape[1] // 4
    short = piece // 2
    for z in range(4):
        grad = tn(act[:, z * piece : (z + 1) * piece], cot[...])
        held = slice(z * short, (z + 1) * short)
        keep_ref[held] = choose(info[1], grad[:short], grad[short:]).astype(BF16)
        send_ref[held] = choose(info[1], grad[short:], grad[:short]).astype(BF16)
    wait(across)


def expand_backward(
    info, slope_ref, cot, we, wr, dh_ref, db_ref, dk_ref, ds_one, ds_two, acc, *, chunk,
):
    tokens, width = cot.shape
    count = dk_ref.shape[0]
    c = info[0]
    total = jnp.zeros((1, slope_ref.shape[1]), F32)
    for t in range(0, tokens, chunk):
        da = nt(cot[t : t + chunk], wr[...])
        dh = (da * slope_ref[t : t + chunk].astype(F32)).astype(BF16)
        dh_ref[t : t + chunk] = dh
        total = total + jnp.sum(dh.astype(F32), axis=0, keepdims=True)
        acc[t : t + chunk] = nt(dh_ref[t : t + chunk], we[...])
    db_ref[...] = total
    dk_ref[...] = acc[part(c, count)]
    ds_one[...] = acc[part(2 * (1 - c), count // 2)].astype(BF16)
    ds_two[...] = acc[part(2 * (1 - c) + 1, count // 2)].astype(BF16)


def split_rows(grad, first, second, bit, cols, short):
    for n in range(grad.shape[0] // (2 * short)):
        low = grad[2 * n * short : (2 * n + 1) * short]
        high = grad[(2 * n + 1) * short : (2 * n + 2) * short]
        first[n * short : (n + 1) * short, cols] = choose(bit, low, high).astype(BF16)
        second[n * short : (n + 1) * short, cols] = choose(bit, high, low).astype(BF16)


def expand_weights(info, n2_ref, dh_ref, outk_ref, far_ref, keep_ref, send_ref, out_ref):
    span = dh_ref.shape[1] // 2
    for j in range(2):
        cols = slice(j * span, (j + 1) * span)
        grad = tn(n2_ref[...], dh_ref[:, cols])
        split_rows(grad, keep_ref, send_ref, info[2], cols, grad.shape[0] // 8)
    out_ref[...] = (outk_ref[...] + far_ref[: out_ref.shape[0]].astype(F32)).astype(BF16)


def attend_backward(
    info, dn_ref, da_one, da_two, mid_ref, cot, vec, wo, pk, pc,
    dpk, mg_ref, s1, s2, s3, s4, sums_ref, dctx, *, slots,
):
    rows, width = mid_ref.shape
    half, wide = width // 2, 3 * width // 2
    c = info[0]
    cotf = cot[part(c, rows)].astype(F32)
    unit, inverse = units(mid_ref[...].astype(F32))
    dn = dn_ref[...] + jnp.concatenate([da_one[...], da_two[...]], axis=0).astype(F32)
    mf = (cotf + norm_back(unit, inverse, vec[5:6], dn)).astype(BF16)
    mg_ref[...] = mf

    def total(a):
        return jnp.sum(a, axis=0, keepdims=True)

    sums = [total(dn * unit), total(dn), total(mf.astype(F32)), total(cotf)]
    dctx[...] = nt(mf, wo[...]).astype(BF16)
    def one(n, carry):
        for tokens in (part(2 * n, GROUP), part(2 * n + 1, GROUP)):
            for p in range(width // 128):
                q, k, v = (pk[tokens, t * width + p * 128 : t * width + (p + 1) * 128] for t in range(3))
                probs = [pc[(2 * p + a) * slots : (2 * p + a + 1) * slots, tokens] for a in range(2)]
                grads = attention_back(q, k, v, probs, dctx[tokens, p * 128 : (p + 1) * 128], slots)
                for t in range(3):
                    dpk[tokens, t * width + p * 128 : t * width + (p + 1) * 128] = grads[t]
        return carry

    lax.fori_loop(0, rows // (2 * GROUP), one, 0)
    sums += [total(dpk[:, :width].astype(F32)), total(dpk[:, 2 * width :].astype(F32))]
    sums_ref[...] = jnp.concatenate(sums + [jnp.zeros((2, width), F32)], axis=0)

    def store(mine):
        s1[...] = dpk[:, mine : mine + half]
        s2[...] = dpk[:, mine + half : mine + width]
        s3[...] = dpk[:, mine + width : mine + wide]
        s4[...] = mg_ref[:, mine // 3 : mine // 3 + half]

    @pl.when(c == 0)
    def _():
        store(wide)

    @pl.when(c == 1)
    def _():
        store(0)


def high_low(v):
    high = v.astype(BF16)
    return high, (v - high.astype(F32)).astype(BF16)


def attend_weights(
    info, dpk, mg, n1_hbm, ctx_hbm, far, f1, f2, f3, f4, vec, k1, t1, k2, t2, n1, ctx, sems,
):
    rows, half = dpk.shape[0], mg.shape[1] // 2
    c = info[0]
    copies = fetch([(n1_hbm, n1), (ctx_hbm, ctx)], sems)
    short = k1.shape[0] // 8

    def other(k):
        return jnp.concatenate([far[k * rows : (k + 1) * rows], far[(k + 1) * rows : (k + 2) * rows]], axis=1)

    for j, given in enumerate((f1, f2, f3, f4)):
        if j < 3:
            mine, at = dpk[:, pl.ds(pl.multiple_of(c * 3 * half + j * half, 128), half)], 4
        else:
            mine, at = mg[:, pl.ds(pl.multiple_of(c * half, 128), half)], 2
        grad = tn(other(at), given[...])
        if j in (0, 3):
            copies[j // 3].wait()
        grad = grad + tn((n1 if j < 3 else ctx)[...], mine)
        cols = slice((j % 2) * half, (j % 2 + 1) * half)
        if j < 2:
            split_rows(grad, k1, t1, info[1], cols, short)
        else:
            split_rows(grad, k2, t2, info[2], cols, 2 * short)
    high, low = high_low(vec[...])
    t1[8 * short : 8 * short + 16] = high
    t1[8 * short + 16 :] = low


def input_backward(
    info, x, vec, win, dpk, mg, sums_ref, db_ref, cg_hbm, cgs_ref, vec_ref, cgk, sems,
):
    rows, width = x.shape
    half = width // 2
    c = info[0]
    unit, inverse = units(x[...].astype(F32))
    dn = nt(dpk[...], win[...])
    out = norm_back(unit, inverse, vec[0:1], dn) + mg[...].astype(F32)
    cgk[...] = choose(c, out[:, :half], out[:, half:]).astype(BF16)
    leaving = fetch([(cgk, cg_hbm.at[part(c, rows)])], sems)
    cgs_ref[...] = choose(c, out[:, half:], out[:, :half]).astype(BF16)
    vec_ref[0:1] = jnp.sum(dn * unit, axis=0, keepdims=True)
    vec_ref[1:2] = jnp.sum(dn, axis=0, keepdims=True)
    vec_ref[2:8] = sums_ref[:6]
    flag = c.astype(F32)
    for z in range(4):
        one = db_ref[:, z * half : (z + 1) * half]
        vec_ref[8 + z : 9 + z, :half] = one * (1.0 - flag)
        vec_ref[8 + z : 9 + z, half:] = one * flag
    vec_ref[12:] = jnp.zeros((4, width), F32)
    wait(leaving)


def vision_heads(n1, win, bias, pk, ctx, images, slots):
    rows = n1.shape[0]
    some = win.shape[1] // 3
    across = some // 128
    pk[:, rows:] = jnp.zeros((pk.shape[0], pk.shape[1] - rows, 128), F32)
    for t in range(3):
        out = nn(n1[...], win[:, t * some : (t + 1) * some])
        if bias[t] is not None:
            out = out + bias[t]
        out = out.astype(BF16).astype(F32)
        for p in range(across):
            pk[t * across + p, :rows] = out[:, p * 128 : (p + 1) * 128]
    allowed = lax.broadcasted_iota(jnp.int32, (slots, GROUP), 0) < rows // images
    per = GROUP // slots
    for i in range(0, images, per):
        for p in range(across):

            def load(t):
                parts = [pk[t * across + p, pl.ds(i + b, slots, stride=images)] for b in range(per)]
                return jnp.concatenate(parts, axis=0).astype(BF16)

            out, _ = attention(load(0), load(1), load(2), allowed, slots)
            for b in range(per):
                ctx[p, pl.ds(i + b, slots, stride=images)] = out[b * slots : (b + 1) * slots]
    return jnp.concatenate([ctx[p, :rows].astype(BF16) for p in range(across)], axis=1)


def some_columns(win_hbm, win, begin, width):
    some = win.shape[1] // 3
    return [(win_hbm.at[:, t * width + begin : t * width + begin + some], win.at[:, t * some : (t + 1) * some]) for t in range(3)]


def vision_attend_one(
    x_hbm, win_hbm, *refs, images, slots,
):
    small, refs = refs[:8], refs[8:]
    n1_ref, ctx_ref, win_ref, vec, token, x, win, *refs = refs
    lines, (pk, ctx, sems) = refs[:8], refs[8:]
    rows, width = x.shape
    copies = fetch([(x_hbm, x), *zip(small, lines)], sems)
    later = fetch(some_columns(win_hbm, win, 0, width), sems, 9)
    last = fetch(some_columns(win_hbm, win_ref, win.shape[1] // 3, width), sems, 12)
    wait(copies)
    at = 0
    for line in lines:
        for k in range(line.shape[0] // width):
            vec[at : at + 1] = line[k * width : (k + 1) * width].astype(F32).reshape(1, width)
            at += 1
    unit, _ = units(x[...].astype(F32))
    n1_ref[...] = (unit * vec[0:1] + vec[1:2]).astype(BF16)
    wait(later)
    some = win.shape[1] // 3
    ctx_ref[...] = vision_heads(n1_ref, win, (vec[2:3, :some], None, vec[3:4, :some]), pk, ctx, images, slots)
    token[...] = jnp.zeros(token.shape, F32)
    wait(last)


def vision_attend_two(
    n1_ref, ctx_ref, win, vec, x_hbm, wo_hbm, mid_ref, token, x, wo, pk, ctx, sems, *, images, slots,
):
    width = x.shape[1]
    some = win.shape[1] // 3
    copies = fetch([(x_hbm, x), (wo_hbm, wo)], sems)
    bias = (vec[2:3, width - some :], None, vec[3:4, width - some :])
    context = vision_heads(n1_ref, win, bias, pk, ctx, images, slots)
    context = jnp.concatenate([ctx_ref[...], context], axis=1)
    wait(copies)
    mid_ref[...] = x[...].astype(F32) + (nn(context, wo[...]) + vec[4:5])
    token[...] = jnp.zeros(token.shape, F32)


def vision_expand(mid_ref, vec, we, wr, *refs, begin):
    out_hbm, token, n2, act, out, sems = refs[-6:]
    rows, width = n2.shape
    images = out.shape[1]
    mid = mid_ref[begin : begin + rows]
    unit, _ = units(mid)
    n2[...] = (unit * vec[5:6] + vec[6:7]).astype(BF16)
    for f in range(we.shape[1] // width):
        cols = slice(f * width, (f + 1) * width)
        h = nn(n2[...], we[:, cols]) + vec[7 + f : 8 + f]
        gate = 0.5 + 0.5 * jnp.tanh(h * (ROOT + (ROOT * CUBIC) * (h * h)))
        act[:, cols] = (h * gate).astype(BF16)
    result = mid + (nn(act[...], wr[...]) + vec[11:12])
    out[...] = result.astype(BF16).reshape(out.shape)
    token[...] = jnp.zeros(token.shape, F32)
    wait(fetch([(out, out_hbm.at[begin // images : (begin + rows) // images])], sems))


def summed(parts, size, cols=slice(None)):
    total = None
    for ref, begin in parts:
        if not isinstance(begin, int):
            begin = pl.multiple_of(begin, 16)
        one = ref[pl.ds(begin, size), cols].astype(F32)
        total = one if total is None else total + one
    return total


def places(info):
    return info[1], info[2], info[3], info[4]


def fold_a_zl(info, a0, a1, a_out):
    x, y, zl, zh = places(info)
    size = a_out.shape[0] // 2
    for h in range(2):
        at = (2 * h + 1 - zl) * size
        a_out[h * size : (h + 1) * size] = summed([(a0, at), (a1, at)], size).astype(BF16)


def fold_a_zh_b_x(info, a0, a1, a2, b0, b1, a_out, b_out):
    x, y, zl, zh = places(info)
    size, unit = a_out.shape[0], b_out.shape[0] // 4
    at = (2 * (1 - zh) + zl) * size
    a_out[...] = summed([(a0, at), (a1, at), (a2, (1 - zh) * size)], size).astype(BF16)
    for z in range(4):
        at = (2 * z + 1 - x) * unit
        b_out[z * unit : (z + 1) * unit] = summed([(b0, at), (b1, at)], unit).astype(BF16)


def fold_c(info, c0, c1, d0, d1, vec, c_out, d_out, v_out):
    x, y, zl, zh = places(info)
    unit = d_out.shape[0] // 4
    for q in range(4):
        held = slice(q * unit, (q + 1) * unit)
        at = (2 * q + 1 - y) * unit
        c_out[held] = summed([(c0, at), (c1, at)], unit).astype(BF16)
        at = (2 * q + 1 - x) * unit
        d_out[held] = summed([(d0, at), (d1, at)], unit).astype(BF16)
    v = vec[...] + (c1[8 * unit : 8 * unit + 16].astype(F32) + c1[8 * unit + 16 :].astype(F32))
    v_out[...] = v
    c_out[4 * unit : 4 * unit + 16], c_out[4 * unit + 16 :] = high_low(v)


def fold_a_y_b_zl(info, a0, a1, a2, a3, b0, b1, b2, a_out, b_out):
    x, y, zl, zh = places(info)
    size, unit = a_out.shape[0], b_out.shape[0] // 2
    at = (2 * zh + zl) * size
    a_out[...] = summed([(a0, at), (a1, at), (a2, zh * size), (a3, 0)], size).astype(BF16)
    for h in range(2):
        z = 2 * h + 1 - zl
        at = (2 * z + x) * unit
        b_out[h * unit : (h + 1) * unit] = summed([(b0, at), (b1, at), (b2, z * unit)], unit).astype(BF16)


def fold_a_b_zh_c_zl(
    info, a4, a5, b0, b1, b2, b3, c0, c1, c2, d0, d1, d2, vec, a_out, b_out, e_out, v_out
):
    x, y, zl, zh = places(info)
    unit, width = b_out.shape[0], a_out.shape[1]
    a_out[...] = (a4[...].astype(F32) + a5[...].astype(F32)).astype(BF16)
    z = 2 * (1 - zh) + zl
    at = (2 * z + x) * unit
    b_out[...] = summed([(b0, at), (b1, at), (b2, z * unit), (b3, (1 - zh) * unit)], unit).astype(BF16)
    for h in range(2):
        held = slice(h * unit, (h + 1) * unit)
        q = 2 * h + 1 - zl
        at = (2 * q + y) * unit
        e_out[held, :width] = summed([(c0, at), (c1, at), (c2, q * unit)], unit).astype(BF16)
        at = (2 * q + x) * unit
        e_out[held, width:] = summed([(d0, at), (d1, at), (d2, q * unit)], unit).astype(BF16)
    v = vec[...] + (c2[4 * unit : 4 * unit + 16].astype(F32) + c2[4 * unit + 16 :].astype(F32))
    v_out[...] = v
    e_out[2 * unit :, :width], e_out[2 * unit :, width:] = high_low(v)


def fold_b_c_zh(info, b0, b1, b2, b3, b4, c0, c1, c2, d0, d1, d2, e3, vec, b_out, e_out, v_out):
    x, y, zl, zh = places(info)
    unit, width = b_out.shape[0], vec.shape[1]
    z = 2 * zh + zl
    at = (2 * z + x) * unit
    parts = [(b0, at), (b1, at), (b2, z * unit), (b3, zh * unit), (b4, 0)]
    b_out[...] = summed(parts, unit).astype(BF16)
    settle(info, 1 - zh, c0, c1, c2, d0, d1, d2, [(e3, (1 - zh) * unit)], e_out, 0, unit)
    v = vec[...] + (e3[2 * unit :, :width].astype(F32) + e3[2 * unit :, width:].astype(F32))
    v_out[...] = v
    e_out[unit:, :width], e_out[unit:, width:] = high_low(v)


def settle(info, zh, c0, c1, c2, d0, d1, d2, more, out, begin, unit):
    x, y, zl, _ = places(info)
    width = out.shape[1] // 2
    q = 2 * zh + zl
    at = (2 * q + y) * unit
    first = summed([(c0, at), (c1, at), (c2, q * unit)], unit) + summed(more, unit, slice(0, width))
    at = (2 * q + x) * unit
    second = summed([(d0, at), (d1, at), (d2, q * unit)], unit) + summed(more, unit, slice(width, 2 * width))
    out[begin : begin + unit, :width] = first.astype(BF16)
    out[begin : begin + unit, width:] = second.astype(BF16)


def fold_last(info, b_own, c0, c1, c2, d0, d1, d2, e3, e4, vec, out):
    x, y, zl, zh = places(info)
    unit, width = b_own.shape[0], vec.shape[1]
    out[:unit] = b_own[...]
    settle(info, zh, c0, c1, c2, d0, d1, d2, [(e3, zh * unit), (e4, 0)], out, unit, unit)
    v = vec[...] + (e4[unit:, :width].astype(F32) + e4[unit:, width:].astype(F32))
    out[2 * unit :, :width], out[2 * unit :, width:] = high_low(v)


def assemble(
    info, a_own, a_far, f_own, f_far, cg_far, cg_in, a_ref, b_ref, in_ref, out_ref, *refs, ranks
):
    vectors, (cg_hbm, sems) = refs[:8], refs[8:]
    c = info[0]
    rows = cg_far.shape[0]
    leaving = fetch([(cg_far, cg_hbm.at[part(1 - c, rows)])], sems)
    a_ref[...] = choose(c ^ info[2], a_own[...].astype(F32), a_far[...].astype(F32))
    share, hidden = b_ref.shape
    piece = hidden // 8
    wide, half = in_ref.shape[1] // 2, out_ref.shape[1] // 2
    mine, far = f_own[...].astype(F32), f_far[...].astype(F32)
    low, high = choose(c, mine, far), choose(c, far, mine)
    for z in range(4):
        held = slice(z * piece, (z + 1) * piece)
        b_ref[:, 2 * z * piece : (2 * z + 1) * piece] = low[:share, held]
        b_ref[:, (2 * z + 1) * piece : (2 * z + 2) * piece] = high[:share, held]
    in_ref[:, :wide] = low[share : 2 * share, :wide]
    in_ref[:, wide:] = high[share : 2 * share, :wide]
    out_ref[:, :half] = low[share : 2 * share, wide:]
    out_ref[:, half:] = high[share : 2 * share, wide:]
    width = out_ref.shape[1]
    one, two = f_own[2 * share :].astype(F32), f_far[2 * share :].astype(F32)
    total = (one[:, :width] + one[:, width:]) + (two[:, :width] + two[:, width:])
    place = info[5]
    first = 0
    for ref, number in zip(vectors, (1, 1, 1, 1, 1, 1, 2, 4)):
        size = number * width // ranks
        offset = place * size
        which = offset // width
        taken = total[first : first + 1]
        for k in range(1, number):
            taken = jnp.where(which == k, total[first + k : first + k + 1], taken)
        turn = lax.rem(width - lax.rem(offset, width), width)
        turned = pltpu.roll(jnp.concatenate([taken] * 8, axis=0), turn, 1)
        ref[...] = turned[:1, :size].reshape(size)
        first += number
    wait(leaving)


def shape(dims, dtype=BF16):
    return jax.ShapeDtypeStruct(dims, dtype)


def whole(dims):
    return pl.BlockSpec(dims, lambda *_: (0,) * len(dims))


HBM = pl.BlockSpec(memory_space=pltpu.HBM)
NEAR = "near"
PLACES = {True: pltpu.HBM, NEAR: pltpu.VMEM}
FAR = pl.BlockSpec(memory_space=pl.ANY)


def kernel(body, name, ins, outs, scratch, args, scalars=(), aliases=None, after=()):
    first, extra = len(scalars) + len(args), len(after)

    def run(*refs):
        return body(*refs[:first], *refs[first + extra :])

    specs = pltpu.PrefetchScalarGridSpec(
        num_scalar_prefetch=len(scalars),
        grid=(1,),
        in_specs=[HBM if far is True else whole(a.shape) for far, a in zip(ins, args, strict=True)] + [FAR] * extra,
        out_specs=[HBM if far is True else whole(s.shape) for far, s in outs],
        scratch_shapes=scratch,
    )
    return pl.pallas_call(
        run,
        name=name,
        grid_spec=specs,
        out_shape=[PLACES[far](s.shape, s.dtype) if far else s for far, s in outs],
        compiler_params=pltpu.CompilerParams(
            vmem_limit_bytes=LIMITS.get(name, 16) * MIB, dimension_semantics=("arbitrary",)
        ),
        cost_estimate=pl.CostEstimate(flops=COST, bytes_accessed=1000, transcendentals=0),
        input_output_aliases=aliases or {},
    )(*scalars, *(pltpu.with_memory_space_constraint(a, PLACES[far]) if far else a for far, a in zip(ins, args)), *after)


BITS = {"x": 0, "y": 1, "zl": 2, "zh": 3}


def on_device(
    captions, caption_lengths, caption_cotangent,
    first_gain, first_shift, project_in, inward_bias, project_out, outward_bias,
    second_gain, second_shift, expand_weight, expand_bias, reduce_weight, reduce_bias,
    patches,
    vision_first_gain, vision_first_shift, vision_project_in, vision_inward_bias, vision_project_out, vision_outward_bias,
    vision_second_gain, vision_second_shift, vision_expand_weight, vision_expand_bias, vision_reduce_weight, vision_reduce_bias,
):
    count, slots, width = captions.shape
    hidden = expand_weight.shape[1]
    tokens = count * slots
    own = tokens // 2
    half = width // 2
    units_own = hidden // 2
    heads = width // HEAD_DIM
    unit = width // 16
    quarter = hidden // 16
    ranks = lax.axis_size("dp")
    low = (ranks // 16).bit_length() - 1
    core = lax.axis_index("section")
    place = lax.axis_index("dp")
    info = jnp.stack([core] + [(place >> (low + b)) & 1 for b in range(4)] + [place]).astype(jnp.int32)
    x = captions.reshape(tokens, width)
    cot = caption_cotangent.reshape(tokens, width)
    dma = pltpu.SemaphoreType.DMA

    def hop(value, bit, only=None):
        step = 1 << (low + BITS[bit])
        pairs = []
        for k in range(2):
            for d in range(ranks):
                if only is None or only(k, (d >> (low + 1)) & 1):
                    pairs.append((k * ranks + d, k * ranks + (d ^ step)))
        return lax.ppermute(value, ("section", "dp"), pairs)

    def swap(value):
        return lax.ppermute(value, "section", [(0, 1), (1, 0)])

    def vmem(dims, dtype=BF16):
        return pltpu.VMEM(dims, dtype)

    line = vmem((width,))

    def fold(body, args, outs, after):
        return kernel(body, body.__name__, [False] * len(args), [(False, s) for s in outs], [], args, (info,), after=after)

    lines = (first_gain, first_shift, inward_bias, outward_bias, second_gain, second_shift, expand_bias, reduce_bias)
    near = [(own, width), (tokens, width), project_in.shape, project_out.shape, (width, units_own), (units_own, width)]
    middle, x_own, cot_near, win, wo, we, wr, vec, packed, probs, context, normed = kernel(
        partial(attend_forward, slots=slots), "caption_attention",
        [True] * 15,
        [(False, shape((own, width)))] + [(NEAR, shape(d)) for d in near] + [(NEAR, shape((16, width), F32))]
        + [(NEAR, shape((own, 3 * width))), (NEAR, shape((heads * slots, own), F32)),
           (True, shape((own, width))), (True, shape((own, width)))],
        [pltpu.SMEM(caption_lengths.shape, jnp.int32), *[vmem(v.shape) for v in lines], vmem((own, width)), vmem((own, width)), dma((25,))],
        (caption_lengths, x, cot, project_in, project_out, expand_weight, reduce_weight, *lines), (info,),
    )
    middle_far = swap(middle)

    n2, slope, a0, a_send, out_keep, out_send = kernel(
        partial(expand_forward, chunk=256), "caption_mlp_forward",
        [False] * 2 + [NEAR] * 4 + [True] * 2,
        [(False, shape((tokens, width))), (False, shape((tokens, units_own))),
         (False, shape((4 * quarter, width))), (False, shape((4 * quarter, width))),
         (False, shape((tokens, half), F32)), (False, shape((3 * tokens, half)))],
        [vmem((tokens, width)), vmem((tokens, units_own)), dma((4,))],
        (middle, middle_far, cot_near, we, wr, vec, context, normed), (info,),
    )
    a1 = hop(a_send, "x")
    out_far = swap(out_send)

    dh, db, dn_keep, dn_one, dn_two = kernel(
        partial(expand_backward, chunk=256), "caption_mlp_backward",
        [False] + [NEAR] * 3,
        [(False, shape((tokens, units_own))), (False, shape((1, units_own), F32)),
         (False, shape((own, width), F32)), (False, shape((own // 2, width))), (False, shape((own // 2, width)))],
        [vmem((tokens, width), F32)],
        (slope, cot_near, we, wr), (info,),
    )
    dn_one, dn_two = swap(dn_one), swap(dn_two)
    b0, b_send, caption_output = kernel(
        expand_weights, "caption_mlp_weights", [False] * 4,
        [(False, shape((8 * unit, units_own)))] * 2 + [(False, shape((tokens, half)))],
        [], (n2, dh, out_keep, out_far), (info,), after=(dn_keep,),
    )
    b1 = hop(b_send, "y")

    dpk, mg, p1, p2, p3, p4, sums = kernel(
        partial(attend_backward, slots=slots), "caption_attention_backward",
        [False] * 4 + [NEAR] * 5,
        [(False, shape((own, 3 * width))), (False, shape((own, width)))]
        + [(False, shape((own, half)))] * 4 + [(False, shape((8, width), F32))],
        [vmem((own, width))],
        (dn_keep, dn_one, dn_two, middle, cot_near, vec, wo, packed, probs),
        (info,), after=(b0,),
    )
    f1, f2, f3, f4 = swap(p1), swap(p2), swap(p3), swap(p4)

    cg_half, cg_send, vectors = kernel(
        input_backward, "caption_input_backward",
        [NEAR] * 3 + [False] * 4,
        [(True, shape((tokens, half))), (False, shape((own, half))), (False, shape((16, width), F32))],
        [vmem((own, half)), dma((1,))],
        (x_own, vec, win, dpk, mg, sums, db), (info,),
    )
    cg_far = swap(cg_send)
    (a_send,) = fold(fold_a_zl, (a0, a1), [shape((2 * quarter, width))], (vectors,))
    a2 = hop(a_send, "zl")

    c0, c_send, d0, d_send = kernel(
        attend_weights, "caption_attention_weights",
        [False] * 2 + [True] * 2 + [False] * 6,
        [(False, shape((8 * unit, width))), (False, shape((8 * unit + 32, width))),
         (False, shape((8 * unit, width))), (False, shape((8 * unit, width)))],
        [vmem((own, width)), vmem((own, width)), dma((2,))],
        (dpk, mg, normed, context, out_far, f1, f2, f3, f4, vectors), (info,), after=(a_send,),
    )
    c1 = hop(c_send, "x")
    d1 = hop(d_send, "y")

    images, used, _ = patches.shape
    flat = jnp.transpose(patches, (1, 0, 2)).reshape(used * images, width)
    padded = 64
    four = 2 * width // 3
    token_out = (False, shape((8, 128), F32))
    two = width - four
    lines = (vision_first_gain, vision_first_shift, vision_inward_bias, vision_outward_bias,
             vision_second_gain, vision_second_shift, vision_expand_bias, vision_reduce_bias)
    n1, context, win, vec, token = kernel(
        partial(vision_attend_one, images=images, slots=padded), "vision_attention", [True] * 10,
        [(False, shape(flat.shape)), (False, shape((used * images, four))), (False, shape((width, 3 * two))),
         (False, shape((16, width), F32)), token_out],
        [vmem(flat.shape), vmem((width, 3 * four)), *[vmem(v.shape) for v in lines],
         vmem((3 * four // 128, padded * images, 128), F32), vmem((four // 128, padded * images, 128), F32), dma((15,))],
        (flat, vision_project_in, *lines), after=(c0,),
    )
    a_send, b_send = fold(
        fold_a_zh_b_x, (a0, a1, a2, b0, b1), [shape((quarter, width)), shape((4 * unit, units_own))], (token,),
    )
    a3, b2 = hop(a_send, "zh"), hop(b_send, "x")
    vision_middle, token = kernel(
        partial(vision_attend_two, images=images, slots=padded), "vision_attention_rest", [False] * 4 + [True] * 2,
        [(False, shape(flat.shape, F32)), token_out],
        [vmem(flat.shape), vmem(vision_project_out.shape),
         vmem((3 * two // 128, padded * images, 128), F32), vmem((two // 128, padded * images, 128), F32), dma((2,))],
        (n1, context, win, vec, flat, vision_project_out), after=(a_send,),
    )

    def vision_second(begin, size, before, after):
        return kernel(
            partial(vision_expand, begin=begin * images), "vision_mlp",
            [False] * 4 + [True] * len(before),
            [(True, shape((used, images, width))), token_out],
            [vmem((size * images, width)), vmem((size * images, hidden)), vmem((size, images, width)), dma((1,))],
            (vision_middle, vec, vision_expand_weight, vision_reduce_weight) + before,
            aliases={4: 0} if before else None, after=after,
        )

    c_send, d_send, vectors = fold(
        fold_c, (c0, c1, d0, d1, vectors),
        [shape((4 * unit + 32, width)), shape((4 * unit, width)), shape((16, width), F32)], (token,),
    )
    c2, d2 = hop(c_send, "y"), hop(d_send, "x")
    first = (2 * used // 5 + 1) // 2 * 2
    vision_output, token = vision_second(0, first, (), (d_send,))

    a4, b_send = fold(
        fold_a_y_b_zl, (a0, a1, a2, a3, b0, b1, b2), [shape((quarter, width)), shape((2 * unit, units_own))], (token,),
    )
    a5, b3 = hop(a4, "y", lambda k, y: k != y), hop(b_send, "zl")
    second = (used - first) // 2
    vision_output, token = vision_second(first, second, (vision_output,), (a4,))

    a_own, b_send, e_send, vectors = fold(
        fold_a_b_zh_c_zl, (a4, a5, b0, b1, b2, b3, c0, c1, c2, d0, d1, d2, vectors),
        [shape((quarter, width)), shape((unit, units_own)), shape((2 * unit + 16, 2 * width)), shape((16, width), F32)],
        (token,),
    )
    b4, e3 = hop(b_send, "zh"), hop(e_send, "zl")
    vision_output, token = vision_second(first + second, used - first - second, (vision_output,), (a_own,))

    b_own, e_send, vectors = fold(
        fold_b_c_zh, (b0, b1, b2, b3, b4, c0, c1, c2, d0, d1, d2, e3, vectors),
        [shape((unit, units_own)), shape((unit + 16, 2 * width)), shape((16, width), F32)], (token,),
    )
    e4 = hop(e_send, "zh")
    (final,) = fold(
        fold_last, (b_own, c0, c1, c2, d0, d1, d2, e3, e4, vectors), [shape((2 * unit + 16, units_own))], (),
    )
    if low:
        groups = [list(range(i, i + (1 << low))) for i in range(0, ranks, 1 << low)]

        def scattered(value):
            return lax.psum_scatter(value, "dp", scatter_dimension=0, tiled=True, axis_index_groups=groups)

        a_own = scattered(a_own)
        total = final[2 * unit :].astype(F32)
        total = lax.psum(total[:, :width] + total[:, width:], "dp", axis_index_groups=groups)
        final = jnp.concatenate(
            [scattered(final[:unit]), scattered(final[unit : 2 * unit]), jnp.concatenate(high_low(total), axis=1)]
        )
    a_away = swap(a_own)
    away = swap(final)
    share = width // ranks
    sizes = [share] * 6 + [2 * share, 4 * share]
    reduce_grad, expand_grad, in_grad, out_grad, *shares, captions_gradient = kernel(
        partial(assemble, ranks=ranks), "assemble", [False] * 5 + [True],
        [(False, shape((4 * share, width), F32)), (False, shape((share, hidden), F32)),
         (False, shape((share, 3 * width), F32)), (False, shape((share, width), F32))]
        + [(False, shape((n,), F32)) for n in sizes] + [(True, shape((tokens, half)))],
        [dma((1,))], (a_own, a_away, final, away, cg_far, cg_half), (info,), aliases={6: 12},
    )
    return (
        jnp.transpose(vision_output, (1, 0, 2)), caption_output.reshape(count, slots, half),
        captions_gradient.reshape(count, slots, half),
        shares[0], shares[1], in_grad, shares[6], out_grad, shares[4],
        shares[2], shares[3], expand_grad, shares[7], reduce_grad, shares[5],
    )


def solution(mesh):
    spread_all = P(("section", "dp"), None, None)
    placed = (P("dp", None, None), P("dp"), P("dp", None, None)) + (P(),) * 12 + (spread_all,) + (P(),) * 12
    features = P("dp", None, "section")
    return jax.shard_map(
        on_device,
        mesh=mesh,
        in_specs=placed,
        out_specs=(
            spread_all, features, features,
            P("dp"), P("dp"), P("dp", None), P("dp"), P("dp", None), P("dp"),
            P("dp"), P("dp"), P("dp", None), P("dp"), P("dp", None), P("dp"),
        ),
        check_vma=False,
    )
```

```python
from functools import partial

import jax
import jax.experimental.pallas as pl
import jax.numpy as jnp
from jax import lax
from jax.experimental.pallas import tpu as pltpu
from jax.sharding import PartitionSpec as P

HEAD_DIM = 64
GROUP = 128
EPSILON = 1e-06
MASKED = -1000000000.0
ROOT = 0.7978845608028654
CUBIC = 0.044715
F32 = jnp.float32
BF16 = jnp.bfloat16
MIB = 1024 * 1024
COST = 1000000
COSTS = {
    "caption_attention": 8,
    "caption_mlp_forward": 11,
    "caption_mlp_backward": 6,
    "caption_mlp_weights": 4,
    "caption_attention_backward": 8,
    "caption_input_backward": 4,
    "caption_attention_weights": 5,
    "vision_attention": 7,
    "vision_attention_rest": 6,
    "vision_mlp": 4,
}
LIMITS = {
    "caption_attention": 14,
    "caption_mlp_forward": 18,
    "caption_mlp_backward": 14,
    "caption_mlp_weights": 16,
    "caption_attention_backward": 16,
    "caption_input_backward": 14,
    "caption_attention_weights": 14,
    "vision_attention": 26,
    "vision_attention_rest": 20,
    "vision_mlp": 16,
}


def nn(a, b):
    return lax.dot_general(a, b, (((1,), (0,)), ((), ())), preferred_element_type=F32)


def nt(a, b):
    return lax.dot_general(a, b, (((1,), (1,)), ((), ())), preferred_element_type=F32)


def tn(a, b):
    return lax.dot_general(a, b, (((0,), (0,)), ((), ())), preferred_element_type=F32)


def row(ref):
    return ref[...].astype(F32).reshape(1, -1)


def units(x):
    average = jnp.mean(x, axis=-1, keepdims=True)
    centred = x - average
    variance = jnp.mean(centred * centred, axis=-1, keepdims=True)
    inverse = lax.rsqrt(variance + EPSILON)
    return centred * inverse, inverse


def norm_back(unit, inverse, gain, dy):
    du = dy * gain
    first = jnp.mean(du, axis=-1, keepdims=True)
    second = jnp.mean(du * unit, axis=-1, keepdims=True)
    return (du - first - unit * second) * inverse


def lane_block(slots, rows):
    return lax.broadcasted_iota(jnp.int32, (rows, GROUP), 1) // slots


def two_heads(a):
    lanes = lax.broadcasted_iota(jnp.int32, a.shape, 1)
    low = (lanes < HEAD_DIM).astype(F32).astype(BF16)
    high = (lanes >= HEAD_DIM).astype(F32).astype(BF16)
    return jnp.concatenate([a * low, a * high], axis=0)


def compact(full, slots):
    block = lane_block(slots, slots)
    out = full[:slots]
    for b in range(1, GROUP // slots):
        out = jnp.where(block == b, full[b * slots : (b + 1) * slots], out)
    return out


def spread(part, slots):
    block = lane_block(slots, slots)
    return jnp.concatenate(
        [part * (block == b).astype(F32).astype(BF16) for b in range(GROUP // slots)], axis=0
    )


def attention(q, k, v, allowed, slots):
    scores = nt(two_heads(k), q)
    probs = []
    for a in range(2):
        s = compact(scores[a * GROUP : (a + 1) * GROUP], slots) * (HEAD_DIM**-0.5)
        s = jnp.where(allowed, s, MASKED)
        powered = jnp.exp(s - jnp.max(s, axis=0, keepdims=True))
        probs.append(powered / jnp.sum(powered, axis=0, keepdims=True))
    wide = jnp.concatenate([spread(p.astype(BF16), slots) for p in probs], axis=0)
    return tn(wide, two_heads(v)), probs


def attention_back(q, k, v, probs, dc, slots):
    vv, kk, qq, dd = two_heads(v), two_heads(k), two_heads(q), two_heads(dc)
    dprobs = nt(vv, dc)
    wide_p, wide_s = [], []
    for a in range(2):
        dp = compact(dprobs[a * GROUP : (a + 1) * GROUP], slots)
        p = probs[a]
        ds = p * (dp - jnp.sum(p * dp, axis=0, keepdims=True))
        wide_p.append(spread(p.astype(BF16), slots))
        wide_s.append(spread(ds.astype(BF16), slots))
    dv = nn(jnp.concatenate(wide_p, axis=1), dd)
    dk = nn(jnp.concatenate(wide_s, axis=1), qq)
    dq = tn(jnp.concatenate(wide_s, axis=0), kk)
    scale = HEAD_DIM**-0.5
    return (dq * scale).astype(BF16), (dk * scale).astype(BF16), dv.astype(BF16)


def fetch(pairs, sems, first=0):
    copies = [pltpu.make_async_copy(a, b, sems.at[first + i]) for i, (a, b) in enumerate(pairs)]
    for copy in copies:
        copy.start()
    return copies


def wait(copies):
    for copy in copies:
        copy.wait()


def part(number, size):
    return pl.ds(pl.multiple_of(number * size, size), size)


def thirds(win, held, width):
    return [(win.at[:, t * width : (t + 1) * width], held.at[:, t * width : (t + 1) * width]) for t in range(3)]


def choose(flag, a, b):
    return jnp.where(flag == 0, a, b)


def inward(n1, t, win, bias):
    width = n1.shape[1]
    out = nn(n1, win[:, t * width : (t + 1) * width])
    if t != 1:
        out = out + bias[:, t // 2 * width : (t // 2 + 1) * width]
    return out.astype(BF16)


def attend_forward(
    info, lens_hbm, x_hbm, cot_hbm, win_hbm, wo_hbm, we_hbm, wr_hbm, *refs, slots,
):
    small, refs = refs[:8], refs[8:]
    mid_ref, x, cot, win, wo, we, wr, vec, pk, pc, ctx_hbm, n1_hbm, *refs = refs
    lens, lines, ctx, n1, sems = refs[0], refs[1:9], *refs[9:]
    rows, width = x.shape
    first = fetch([(lens_hbm, lens), *zip(small, lines)], sems)
    copies = fetch([(x_hbm.at[part(info[0], rows)], x), *thirds(win_hbm, win, width), (wo_hbm, wo)], sems, 9)
    into, out_of = unit_parts(info, we_hbm, wr_hbm, we, wr)
    resident = fetch([*into, *out_of, (cot_hbm, cot)], sems, 14)
    wait(first)
    at = 0
    for line in lines:
        for k in range(line.shape[0] // width):
            vec[at : at + 1] = line[k * width : (k + 1) * width].astype(F32).reshape(1, width)
            at += 1
    copies[0].wait()
    unit, _ = units(x[...].astype(F32))
    n1[...] = (unit * vec[0:1] + vec[1:2]).astype(BF16)
    leaving = fetch([(n1, n1_hbm)], sems, 23)

    def project(held, wait_for):
        for t in range(3):
            if wait_for:
                copies[1 + t].wait()
            out = nn(n1[held], win[:, t * width : (t + 1) * width])
            if t != 1:
                out = out + vec[2 + t // 2 : 3 + t // 2]
            pk[held, t * width : (t + 1) * width] = out.astype(BF16)

    project(slice(0, rows // 2), True)
    block = lane_block(slots, 1)
    slot = lax.broadcasted_iota(jnp.int32, (slots, GROUP), 0)
    per = GROUP // slots
    start = info[0] * (rows // slots)
    for n in range(rows // GROUP):
        if n == rows // GROUP // 2:
            project(slice(rows // 2, rows), False)
        used = jnp.zeros((1, GROUP), jnp.int32)
        for b in range(per):
            used = jnp.where(block == b, lens[start + n * per + b], used)
        allowed = slot < used
        tokens = slice(n * GROUP, (n + 1) * GROUP)
        for p in range(width // 128):
            q, k, v = (pk[tokens, t * width + p * 128 : t * width + (p + 1) * 128] for t in range(3))
            out, probs = attention(q, k, v, allowed, slots)
            ctx[tokens, p * 128 : (p + 1) * 128] = out.astype(BF16)
            for a in range(2):
                pc[(2 * p + a) * slots : (2 * p + a + 1) * slots, tokens] = probs[a]
    leaving += fetch([(ctx, ctx_hbm)], sems, 24)
    copies[4].wait()
    mid_ref[...] = (x[...].astype(F32) + (nn(ctx[...], wo[...]) + vec[4:5])).astype(BF16)
    wait(leaving + resident)


def unit_parts(info, we_hbm, wr_hbm, we, wr):
    piece = we.shape[1] // 4
    first, second = [], []
    for z in range(4):
        held = slice(z * piece, (z + 1) * piece)
        begin = part(2 * z + info[0], piece)
        first.append((we_hbm.at[:, begin], we.at[:, held]))
        second.append((wr_hbm.at[begin], wr.at[held]))
    return first, second


def expand_forward(
    info, own_ref, oth_ref, cot, we, wr, vec, ctx_hbm, n1_hbm,
    n2_ref, slope_ref, keep_ref, send_ref, outk_ref, outs_ref, mid, act, sems, *, chunk,
):
    tokens, width = mid.shape
    count, half = own_ref.shape[0], width // 2
    c = info[0]
    across = []
    for k, (source, at) in enumerate(((ctx_hbm, 0), (ctx_hbm, half), (n1_hbm, 0), (n1_hbm, half))):
        held = outs_ref.at[tokens + k * count : tokens + (k + 1) * count]
        across += fetch([(source.at[:, at : at + half], held)], sems, k)
    mid[part(c, count)] = own_ref[...]
    mid[part(1 - c, count)] = oth_ref[...]
    bias = jnp.concatenate([choose(c, vec[z : z + 1, :half], vec[z : z + 1, half:]) for z in range(7, 11)], axis=1)
    over = choose(c, vec[11:12, :half], vec[11:12, half:])
    for t in range(0, tokens, chunk):
        old = mid[t : t + chunk].astype(F32)
        unit, _ = units(old)
        n2 = (unit * vec[5:6] + vec[6:7]).astype(BF16)
        n2_ref[t : t + chunk] = n2
        h = nn(n2, we[...]) + bias
        square = h * h
        gate = 0.5 + 0.5 * jnp.tanh(h * (ROOT + (ROOT * CUBIC) * square))
        active = h * gate
        slope = gate + active * (1.0 - gate) * (2.0 * ROOT + (6.0 * CUBIC * ROOT) * square)
        act[t : t + chunk] = active.astype(BF16)
        slope_ref[t : t + chunk] = slope.astype(BF16)
        out = nn(act[t : t + chunk], wr[...])
        outk_ref[t : t + chunk] = choose(c, old[:, :half], old[:, half:]) + (choose(c, out[:, :half], out[:, half:]) + over)
        outs_ref[t : t + chunk] = choose(c, out[:, half:], out[:, :half]).astype(BF16)
    piece = act.shape[1] // 4
    short = piece // 2
    for z in range(4):
        grad = tn(act[:, z * piece : (z + 1) * piece], cot[...])
        held = slice(z * short, (z + 1) * short)
        keep_ref[held] = choose(info[1], grad[:short], grad[short:]).astype(BF16)
        send_ref[held] = choose(info[1], grad[short:], grad[:short]).astype(BF16)
    wait(across)


def expand_backward(
    info, slope_ref, cot, we, wr, dh_ref, db_ref, dk_ref, ds_one, ds_two, acc, *, chunk,
):
    tokens, width = cot.shape
    count = dk_ref.shape[0]
    c = info[0]
    total = jnp.zeros((1, slope_ref.shape[1]), F32)
    for t in range(0, tokens, chunk):
        da = nt(cot[t : t + chunk], wr[...])
        dh = (da * slope_ref[t : t + chunk].astype(F32)).astype(BF16)
        dh_ref[t : t + chunk] = dh
        total = total + jnp.sum(dh.astype(F32), axis=0, keepdims=True)
        acc[t : t + chunk] = nt(dh_ref[t : t + chunk], we[...])
    db_ref[...] = total
    dk_ref[...] = acc[part(c, count)]
    ds_one[...] = acc[part(2 * (1 - c), count // 2)].astype(BF16)
    ds_two[...] = acc[part(2 * (1 - c) + 1, count // 2)].astype(BF16)


def split_rows(grad, first, second, bit, cols, short):
    for n in range(grad.shape[0] // (2 * short)):
        low = grad[2 * n * short : (2 * n + 1) * short]
        high = grad[(2 * n + 1) * short : (2 * n + 2) * short]
        first[n * short : (n + 1) * short, cols] = choose(bit, low, high).astype(BF16)
        second[n * short : (n + 1) * short, cols] = choose(bit, high, low).astype(BF16)


def expand_weights(info, n2_ref, dh_ref, outk_ref, far_ref, keep_ref, send_ref, out_ref):
    span = dh_ref.shape[1] // 2
    for j in range(2):
        cols = slice(j * span, (j + 1) * span)
        grad = tn(n2_ref[...], dh_ref[:, cols])
        split_rows(grad, keep_ref, send_ref, info[2], cols, grad.shape[0] // 8)
    out_ref[...] = (outk_ref[...] + far_ref[: out_ref.shape[0]].astype(F32)).astype(BF16)


def attend_backward(
    info, dn_ref, da_one, da_two, mid_ref, cot, vec, wo, pk, pc,
    dpk, mg_ref, s0, s1, sums_ref, dctx, *, slots,
):
    rows, width = mid_ref.shape
    half, wide = width // 2, 3 * width // 2
    c = info[0]
    cotf = cot[part(c, rows)].astype(F32)
    unit, inverse = units(mid_ref[...].astype(F32))
    dn = dn_ref[...] + jnp.concatenate([da_one[...], da_two[...]], axis=0).astype(F32)
    mf = (cotf + norm_back(unit, inverse, vec[5:6], dn)).astype(BF16)
    mg_ref[...] = mf

    def total(a):
        return jnp.sum(a, axis=0, keepdims=True)

    sums = [total(dn * unit), total(dn), total(mf.astype(F32)), total(cotf)]
    dctx[...] = nt(mf, wo[...]).astype(BF16)
    def one(n, carry):
        for tokens in (part(2 * n, GROUP), part(2 * n + 1, GROUP)):
            for p in range(width // 128):
                q, k, v = (pk[tokens, t * width + p * 128 : t * width + (p + 1) * 128] for t in range(3))
                probs = [pc[(2 * p + a) * slots : (2 * p + a + 1) * slots, tokens] for a in range(2)]
                grads = attention_back(q, k, v, probs, dctx[tokens, p * 128 : (p + 1) * 128], slots)
                for t in range(3):
                    dpk[tokens, t * width + p * 128 : t * width + (p + 1) * 128] = grads[t]
        return carry

    lax.fori_loop(0, rows // (2 * GROUP), one, 0)
    sums += [total(dpk[:, :width].astype(F32)), total(dpk[:, 2 * width :].astype(F32))]
    sums_ref[...] = jnp.concatenate(sums + [jnp.zeros((2, width), F32)], axis=0)

    def store(mine):
        s0[0 * rows : 1 * rows] = dpk[:, mine : mine + half]
        s0[1 * rows : 2 * rows] = dpk[:, mine + half : mine + width]
        s1[0 * rows : 1 * rows] = dpk[:, mine + width : mine + wide]
        s1[1 * rows : 2 * rows] = mg_ref[:, mine // 3 : mine // 3 + half]

    @pl.when(c == 0)
    def _():
        store(wide)

    @pl.when(c == 1)
    def _():
        store(0)


def high_low(v):
    high = v.astype(BF16)
    return high, (v - high.astype(F32)).astype(BF16)


def attend_weights(
    info, dpk, mg, n1_hbm, ctx_hbm, far, f0, f1, vec, k1, t1, k2, t2, n1, ctx, sems,
):
    rows, half = dpk.shape[0], mg.shape[1] // 2
    c = info[0]
    copies = fetch([(n1_hbm, n1), (ctx_hbm, ctx)], sems)
    short = k1.shape[0] // 8

    def other(k):
        return jnp.concatenate([far[k * rows : (k + 1) * rows], far[(k + 1) * rows : (k + 2) * rows]], axis=1)

    for j, given in enumerate((f0.at[0 * rows : 1 * rows], f0.at[1 * rows : 2 * rows], f1.at[0 * rows : 1 * rows], f1.at[1 * rows : 2 * rows])):
        if j < 3:
            mine, at = dpk[:, pl.ds(pl.multiple_of(c * 3 * half + j * half, 128), half)], 4
        else:
            mine, at = mg[:, pl.ds(pl.multiple_of(c * half, 128), half)], 2
        grad = tn(other(at), given[...])
        if j in (0, 3):
            copies[j // 3].wait()
        grad = grad + tn((n1 if j < 3 else ctx)[...], mine)
        cols = slice((j % 2) * half, (j % 2 + 1) * half)
        if j < 2:
            split_rows(grad, k1, t1, info[1], cols, short)
        else:
            split_rows(grad, k2, t2, info[2], cols, 2 * short)
    high, low = high_low(vec[...])
    t1[8 * short : 8 * short + 16] = high
    t1[8 * short + 16 :] = low


def input_backward(
    info, x, vec, win, dpk, mg, sums_ref, db_ref, cg_hbm, cgs_ref, vec_ref, cgk, sems,
):
    rows, width = x.shape
    half = width // 2
    c = info[0]
    unit, inverse = units(x[...].astype(F32))
    dn = nt(dpk[...], win[...])
    out = norm_back(unit, inverse, vec[0:1], dn) + mg[...].astype(F32)
    cgk[...] = choose(c, out[:, :half], out[:, half:]).astype(BF16)
    leaving = fetch([(cgk, cg_hbm.at[part(c, rows)])], sems)
    cgs_ref[...] = choose(c, out[:, half:], out[:, :half]).astype(BF16)
    vec_ref[0:1] = jnp.sum(dn * unit, axis=0, keepdims=True)
    vec_ref[1:2] = jnp.sum(dn, axis=0, keepdims=True)
    vec_ref[2:8] = sums_ref[:6]
    flag = c.astype(F32)
    for z in range(4):
        one = db_ref[:, z * half : (z + 1) * half]
        vec_ref[8 + z : 9 + z, :half] = one * (1.0 - flag)
        vec_ref[8 + z : 9 + z, half:] = one * flag
    vec_ref[12:] = jnp.zeros((4, width), F32)
    wait(leaving)


def vision_heads(n1, win, bias, pk, ctx, images, slots):
    rows = n1.shape[0]
    some = win.shape[1] // 3
    across = some // 128
    pk[:, rows:] = jnp.zeros((pk.shape[0], pk.shape[1] - rows, 128), F32)
    for t in range(3):
        out = nn(n1[...], win[:, t * some : (t + 1) * some])
        if bias[t] is not None:
            out = out + bias[t]
        out = out.astype(BF16).astype(F32)
        for p in range(across):
            pk[t * across + p, :rows] = out[:, p * 128 : (p + 1) * 128]
    allowed = lax.broadcasted_iota(jnp.int32, (slots, GROUP), 0) < rows // images
    per = GROUP // slots
    for i in range(0, images, per):
        for p in range(across):

            def load(t):
                parts = [pk[t * across + p, pl.ds(i + b, slots, stride=images)] for b in range(per)]
                return jnp.concatenate(parts, axis=0).astype(BF16)

            out, _ = attention(load(0), load(1), load(2), allowed, slots)
            for b in range(per):
                ctx[p, pl.ds(i + b, slots, stride=images)] = out[b * slots : (b + 1) * slots]
    return jnp.concatenate([ctx[p, :rows].astype(BF16) for p in range(across)], axis=1)


def some_columns(win_hbm, win, begin, width):
    some = win.shape[1] // 3
    return [(win_hbm.at[:, t * width + begin : t * width + begin + some], win.at[:, t * some : (t + 1) * some]) for t in range(3)]


def vision_attend_one(
    x_hbm, win_hbm, *refs, images, slots,
):
    small, refs = refs[:8], refs[8:]
    n1_ref, ctx_ref, win_ref, vec, token, x, win, *refs = refs
    lines, (pk, ctx, sems) = refs[:8], refs[8:]
    rows, width = x.shape
    copies = fetch([(x_hbm, x), *zip(small, lines)], sems)
    later = fetch(some_columns(win_hbm, win, 0, width), sems, 9)
    last = fetch(some_columns(win_hbm, win_ref, win.shape[1] // 3, width), sems, 12)
    wait(copies)
    at = 0
    for line in lines:
        for k in range(line.shape[0] // width):
            vec[at : at + 1] = line[k * width : (k + 1) * width].astype(F32).reshape(1, width)
            at += 1
    unit, _ = units(x[...].astype(F32))
    n1_ref[...] = (unit * vec[0:1] + vec[1:2]).astype(BF16)
    wait(later)
    some = win.shape[1] // 3
    ctx_ref[...] = vision_heads(n1_ref, win, (vec[2:3, :some], None, vec[3:4, :some]), pk, ctx, images, slots)
    token[...] = jnp.zeros(token.shape, F32)
    wait(last)


def vision_attend_two(
    n1_ref, ctx_ref, win, vec, x_hbm, wo_hbm, mid_ref, token, x, wo, pk, ctx, sems, *, images, slots,
):
    width = x.shape[1]
    some = win.shape[1] // 3
    copies = fetch([(x_hbm, x), (wo_hbm, wo)], sems)
    bias = (vec[2:3, width - some :], None, vec[3:4, width - some :])
    context = vision_heads(n1_ref, win, bias, pk, ctx, images, slots)
    context = jnp.concatenate([ctx_ref[...], context], axis=1)
    wait(copies)
    mid_ref[...] = x[...].astype(F32) + (nn(context, wo[...]) + vec[4:5])
    token[...] = jnp.zeros(token.shape, F32)


def vision_expand(mid_ref, vec, we, wr, *refs, begin):
    out_hbm, token, n2, act, out, sems = refs[-6:]
    rows, width = n2.shape
    images = out.shape[1]
    mid = mid_ref[begin : begin + rows]
    unit, _ = units(mid)
    n2[...] = (unit * vec[5:6] + vec[6:7]).astype(BF16)
    for f in range(we.shape[1] // width):
        cols = slice(f * width, (f + 1) * width)
        h = nn(n2[...], we[:, cols]) + vec[7 + f : 8 + f]
        gate = 0.5 + 0.5 * jnp.tanh(h * (ROOT + (ROOT * CUBIC) * (h * h)))
        act[:, cols] = (h * gate).astype(BF16)
    result = mid + (nn(act[...], wr[...]) + vec[11:12])
    out[...] = result.astype(BF16).reshape(out.shape)
    token[...] = jnp.zeros(token.shape, F32)
    wait(fetch([(out, out_hbm.at[begin // images : (begin + rows) // images])], sems))


def summed(parts, size, cols=slice(None)):
    total = None
    for ref, begin in parts:
        if not isinstance(begin, int):
            begin = pl.multiple_of(begin, 16)
        one = ref[pl.ds(begin, size), cols].astype(F32)
        total = one if total is None else total + one
    return total


def places(info):
    return info[1], info[2], info[3], info[4]


def fold_a_zl(info, a0, a1, a_out):
    x, y, zl, zh = places(info)
    size = a_out.shape[0] // 2
    for h in range(2):
        at = (2 * h + 1 - zl) * size
        a_out[h * size : (h + 1) * size] = summed([(a0, at), (a1, at)], size).astype(BF16)


def fold_a_zh_b_x(info, a0, a1, a2, b0, b1, a_out, b_out):
    x, y, zl, zh = places(info)
    size, unit = a_out.shape[0], b_out.shape[0] // 4
    at = (2 * (1 - zh) + zl) * size
    a_out[...] = summed([(a0, at), (a1, at), (a2, (1 - zh) * size)], size).astype(BF16)
    for z in range(4):
        at = (2 * z + 1 - x) * unit
        b_out[z * unit : (z + 1) * unit] = summed([(b0, at), (b1, at)], unit).astype(BF16)


def fold_c(info, c0, c1, d0, d1, vec, c_out, d_out, v_out):
    x, y, zl, zh = places(info)
    unit = d_out.shape[0] // 4
    for q in range(4):
        held = slice(q * unit, (q + 1) * unit)
        at = (2 * q + 1 - y) * unit
        c_out[held] = summed([(c0, at), (c1, at)], unit).astype(BF16)
        at = (2 * q + 1 - x) * unit
        d_out[held] = summed([(d0, at), (d1, at)], unit).astype(BF16)
    v = vec[...] + (c1[8 * unit : 8 * unit + 16].astype(F32) + c1[8 * unit + 16 :].astype(F32))
    v_out[...] = v
    c_out[4 * unit : 4 * unit + 16], c_out[4 * unit + 16 :] = high_low(v)


def fold_a_y_b_zl(info, a0, a1, a2, a3, b0, b1, b2, a_out, b_out):
    x, y, zl, zh = places(info)
    size, unit = a_out.shape[0], b_out.shape[0] // 2
    at = (2 * zh + zl) * size
    a_out[...] = summed([(a0, at), (a1, at), (a2, zh * size), (a3, 0)], size).astype(BF16)
    for h in range(2):
        z = 2 * h + 1 - zl
        at = (2 * z + x) * unit
        b_out[h * unit : (h + 1) * unit] = summed([(b0, at), (b1, at), (b2, z * unit)], unit).astype(BF16)


def fold_a_b_zh_c_zl(
    info, a4, a5, b0, b1, b2, b3, c0, c1, c2, d0, d1, d2, vec, a_out, b_out, e_out, v_out
):
    x, y, zl, zh = places(info)
    unit, width = b_out.shape[0], a_out.shape[1]
    a_out[...] = (a4[...].astype(F32) + a5[...].astype(F32)).astype(BF16)
    z = 2 * (1 - zh) + zl
    at = (2 * z + x) * unit
    b_out[...] = summed([(b0, at), (b1, at), (b2, z * unit), (b3, (1 - zh) * unit)], unit).astype(BF16)
    for h in range(2):
        held = slice(h * unit, (h + 1) * unit)
        q = 2 * h + 1 - zl
        at = (2 * q + y) * unit
        e_out[held, :width] = summed([(c0, at), (c1, at), (c2, q * unit)], unit).astype(BF16)
        at = (2 * q + x) * unit
        e_out[held, width:] = summed([(d0, at), (d1, at), (d2, q * unit)], unit).astype(BF16)
    v = vec[...] + (c2[4 * unit : 4 * unit + 16].astype(F32) + c2[4 * unit + 16 :].astype(F32))
    v_out[...] = v
    e_out[2 * unit :, :width], e_out[2 * unit :, width:] = high_low(v)


def fold_b_c_zh(info, b0, b1, b2, b3, b4, c0, c1, c2, d0, d1, d2, e3, vec, b_out, e_out, v_out):
    x, y, zl, zh = places(info)
    unit, width = b_out.shape[0], vec.shape[1]
    z = 2 * zh + zl
    at = (2 * z + x) * unit
    parts = [(b0, at), (b1, at), (b2, z * unit), (b3, zh * unit), (b4, 0)]
    b_out[...] = summed(parts, unit).astype(BF16)
    settle(info, 1 - zh, c0, c1, c2, d0, d1, d2, [(e3, (1 - zh) * unit)], e_out, 0, unit)
    v = vec[...] + (e3[2 * unit :, :width].astype(F32) + e3[2 * unit :, width:].astype(F32))
    v_out[...] = v
    e_out[unit:, :width], e_out[unit:, width:] = high_low(v)


def settle(info, zh, c0, c1, c2, d0, d1, d2, more, out, begin, unit):
    x, y, zl, _ = places(info)
    width = out.shape[1] // 2
    q = 2 * zh + zl
    at = (2 * q + y) * unit
    first = summed([(c0, at), (c1, at), (c2, q * unit)], unit) + summed(more, unit, slice(0, width))
    at = (2 * q + x) * unit
    second = summed([(d0, at), (d1, at), (d2, q * unit)], unit) + summed(more, unit, slice(width, 2 * width))
    out[begin : begin + unit, :width] = first.astype(BF16)
    out[begin : begin + unit, width:] = second.astype(BF16)


def fold_last(info, b_own, c0, c1, c2, d0, d1, d2, e3, e4, vec, out):
    x, y, zl, zh = places(info)
    unit, width = b_own.shape[0], vec.shape[1]
    out[:unit] = b_own[...]
    settle(info, zh, c0, c1, c2, d0, d1, d2, [(e3, zh * unit), (e4, 0)], out, unit, unit)
    v = vec[...] + (e4[unit:, :width].astype(F32) + e4[unit:, width:].astype(F32))
    out[2 * unit :, :width], out[2 * unit :, width:] = high_low(v)


def assemble(
    info, a_own, a_far, f_own, f_far, cg_far, cg_in, a_ref, b_ref, in_ref, out_ref, *refs, ranks
):
    vectors, (cg_hbm, sems) = refs[:8], refs[8:]
    c = info[0]
    rows = cg_far.shape[0]
    leaving = fetch([(cg_far, cg_hbm.at[part(1 - c, rows)])], sems)
    a_ref[...] = choose(c ^ info[2], a_own[...].astype(F32), a_far[...].astype(F32))
    share, hidden = b_ref.shape
    piece = hidden // 8
    wide, half = in_ref.shape[1] // 2, out_ref.shape[1] // 2
    mine, far = f_own[...].astype(F32), f_far[...].astype(F32)
    low, high = choose(c, mine, far), choose(c, far, mine)
    for z in range(4):
        held = slice(z * piece, (z + 1) * piece)
        b_ref[:, 2 * z * piece : (2 * z + 1) * piece] = low[:share, held]
        b_ref[:, (2 * z + 1) * piece : (2 * z + 2) * piece] = high[:share, held]
    in_ref[:, :wide] = low[share : 2 * share, :wide]
    in_ref[:, wide:] = high[share : 2 * share, :wide]
    out_ref[:, :half] = low[share : 2 * share, wide:]
    out_ref[:, half:] = high[share : 2 * share, wide:]
    width = out_ref.shape[1]
    one, two = f_own[2 * share :].astype(F32), f_far[2 * share :].astype(F32)
    total = (one[:, :width] + one[:, width:]) + (two[:, :width] + two[:, width:])
    place = info[5]
    first = 0
    for ref, number in zip(vectors, (1, 1, 1, 1, 1, 1, 2, 4)):
        size = number * width // ranks
        offset = place * size
        which = offset // width
        taken = total[first : first + 1]
        for k in range(1, number):
            taken = jnp.where(which == k, total[first + k : first + k + 1], taken)
        turn = lax.rem(width - lax.rem(offset, width), width)
        turned = pltpu.roll(jnp.concatenate([taken] * 8, axis=0), turn, 1)
        ref[...] = turned[:1, :size].reshape(size)
        first += number
    wait(leaving)


def shape(dims, dtype=BF16):
    return jax.ShapeDtypeStruct(dims, dtype)


def whole(dims):
    return pl.BlockSpec(dims, lambda *_: (0,) * len(dims))


HBM = pl.BlockSpec(memory_space=pltpu.HBM)
NEAR = "near"
PLACES = {True: pltpu.HBM, NEAR: pltpu.VMEM}
FAR = pl.BlockSpec(memory_space=pl.ANY)


def kernel(body, name, ins, outs, scratch, args, scalars=(), aliases=None, after=()):
    first, extra = len(scalars) + len(args), len(after)

    def run(*refs):
        return body(*refs[:first], *refs[first + extra :])

    specs = pltpu.PrefetchScalarGridSpec(
        num_scalar_prefetch=len(scalars),
        grid=(1,),
        in_specs=[HBM if far is True else whole(a.shape) for far, a in zip(ins, args, strict=True)] + [FAR] * extra,
        out_specs=[HBM if far is True else whole(s.shape) for far, s in outs],
        scratch_shapes=scratch,
    )
    return pl.pallas_call(
        run,
        name=name,
        grid_spec=specs,
        out_shape=[PLACES[far](s.shape, s.dtype) if far else s for far, s in outs],
        compiler_params=pltpu.CompilerParams(
            vmem_limit_bytes=LIMITS.get(name, 16) * MIB, dimension_semantics=("arbitrary",)
        ),
        cost_estimate=pl.CostEstimate(flops=COSTS.get(name, 1) * COST, bytes_accessed=1000, transcendentals=0),
        input_output_aliases=aliases or {},
    )(*scalars, *(pltpu.with_memory_space_constraint(a, PLACES[far]) if far else a for far, a in zip(ins, args)), *after)


BITS = {"x": 0, "y": 1, "zl": 2, "zh": 3}


def on_device(
    captions, caption_lengths, caption_cotangent,
    first_gain, first_shift, project_in, inward_bias, project_out, outward_bias,
    second_gain, second_shift, expand_weight, expand_bias, reduce_weight, reduce_bias,
    patches,
    vision_first_gain, vision_first_shift, vision_project_in, vision_inward_bias, vision_project_out, vision_outward_bias,
    vision_second_gain, vision_second_shift, vision_expand_weight, vision_expand_bias, vision_reduce_weight, vision_reduce_bias,
):
    count, slots, width = captions.shape
    hidden = expand_weight.shape[1]
    tokens = count * slots
    own = tokens // 2
    half = width // 2
    units_own = hidden // 2
    heads = width // HEAD_DIM
    unit = width // 16
    quarter = hidden // 16
    ranks = lax.axis_size("dp")
    low = (ranks // 16).bit_length() - 1
    core = lax.axis_index("section")
    place = lax.axis_index("dp")
    info = jnp.stack([core] + [(place >> (low + b)) & 1 for b in range(4)] + [place]).astype(jnp.int32)
    x = captions.reshape(tokens, width)
    cot = caption_cotangent.reshape(tokens, width)
    dma = pltpu.SemaphoreType.DMA

    def hop(value, bit, only=None):
        step = 1 << (low + BITS[bit])
        pairs = []
        for k in range(2):
            for d in range(ranks):
                if only is None or only(k, (d >> (low + 1)) & 1):
                    pairs.append((k * ranks + d, k * ranks + (d ^ step)))
        return lax.ppermute(value, ("section", "dp"), pairs)

    def swap(value):
        return lax.ppermute(value, "section", [(0, 1), (1, 0)])

    def vmem(dims, dtype=BF16):
        return pltpu.VMEM(dims, dtype)

    line = vmem((width,))

    def fold(body, args, outs, after):
        return kernel(body, body.__name__, [False] * len(args), [(False, s) for s in outs], [], args, (info,), after=after)

    lines = (first_gain, first_shift, inward_bias, outward_bias, second_gain, second_shift, expand_bias, reduce_bias)
    near = [(own, width), (tokens, width), project_in.shape, project_out.shape, (width, units_own), (units_own, width)]
    middle, x_own, cot_near, win, wo, we, wr, vec, packed, probs, context, normed = kernel(
        partial(attend_forward, slots=slots), "caption_attention",
        [True] * 15,
        [(False, shape((own, width)))] + [(NEAR, shape(d)) for d in near] + [(NEAR, shape((16, width), F32))]
        + [(NEAR, shape((own, 3 * width))), (NEAR, shape((heads * slots, own), F32)),
           (True, shape((own, width))), (True, shape((own, width)))],
        [pltpu.SMEM(caption_lengths.shape, jnp.int32), *[vmem(v.shape) for v in lines], vmem((own, width)), vmem((own, width)), dma((25,))],
        (caption_lengths, x, cot, project_in, project_out, expand_weight, reduce_weight, *lines), (info,),
    )
    middle_far = swap(middle)

    n2, slope, a0, a_send, out_keep, out_send = kernel(
        partial(expand_forward, chunk=256), "caption_mlp_forward",
        [False] * 2 + [NEAR] * 4 + [True] * 2,
        [(False, shape((tokens, width))), (False, shape((tokens, units_own))),
         (False, shape((4 * quarter, width))), (False, shape((4 * quarter, width))),
         (False, shape((tokens, half), F32)), (False, shape((3 * tokens, half)))],
        [vmem((tokens, width)), vmem((tokens, units_own)), dma((4,))],
        (middle, middle_far, cot_near, we, wr, vec, context, normed), (info,),
    )
    a1 = hop(a_send, "x")
    out_far = swap(out_send)

    dh, db, dn_keep, dn_one, dn_two = kernel(
        partial(expand_backward, chunk=256), "caption_mlp_backward",
        [False] + [NEAR] * 3,
        [(False, shape((tokens, units_own))), (False, shape((1, units_own), F32)),
         (False, shape((own, width), F32)), (False, shape((own // 2, width))), (False, shape((own // 2, width)))],
        [vmem((tokens, width), F32)],
        (slope, cot_near, we, wr), (info,),
    )
    dn_one, dn_two = swap(dn_one), swap(dn_two)
    b0, b_send, caption_output = kernel(
        expand_weights, "caption_mlp_weights", [False] * 4,
        [(False, shape((8 * unit, units_own)))] * 2 + [(False, shape((tokens, half)))],
        [], (n2, dh, out_keep, out_far), (info,), after=(dn_keep,),
    )
    b1 = hop(b_send, "y")

    dpk, mg, *pieces, sums = kernel(
        partial(attend_backward, slots=slots), "caption_attention_backward",
        [False] * 4 + [NEAR] * 5,
        [(False, shape((own, 3 * width))), (False, shape((own, width)))]
        + [(False, shape((k * own, half))) for k in (2, 2)] + [(False, shape((8, width), F32))],
        [vmem((own, width))],
        (dn_keep, dn_one, dn_two, middle, cot_near, vec, wo, packed, probs),
        (info,), after=(b0,),
    )
    fars = [swap(p) for p in pieces]

    cg_half, cg_send, vectors = kernel(
        input_backward, "caption_input_backward",
        [NEAR] * 3 + [False] * 4,
        [(True, shape((tokens, half))), (False, shape((own, half))), (False, shape((16, width), F32))],
        [vmem((own, half)), dma((1,))],
        (x_own, vec, win, dpk, mg, sums, db), (info,),
    )
    cg_far = swap(cg_send)
    (a_send,) = fold(fold_a_zl, (a0, a1), [shape((2 * quarter, width))], (vectors,))
    a2 = hop(a_send, "zl")

    c0, c_send, d0, d_send = kernel(
        attend_weights, "caption_attention_weights",
        [False] * 2 + [True] * 2 + [False] * 4,
        [(False, shape((8 * unit, width))), (False, shape((8 * unit + 32, width))),
         (False, shape((8 * unit, width))), (False, shape((8 * unit, width)))],
        [vmem((own, width)), vmem((own, width)), dma((2,))],
        (dpk, mg, normed, context, out_far, *fars, vectors), (info,), after=(a_send,),
    )
    c1 = hop(c_send, "x")
    d1 = hop(d_send, "y")

    images, used, _ = patches.shape
    flat = jnp.transpose(patches, (1, 0, 2)).reshape(used * images, width)
    padded = 64
    four = 2 * width // 3
    token_out = (False, shape((8, 128), F32))
    two = width - four
    lines = (vision_first_gain, vision_first_shift, vision_inward_bias, vision_outward_bias,
             vision_second_gain, vision_second_shift, vision_expand_bias, vision_reduce_bias)
    n1, context, win, vec, token = kernel(
        partial(vision_attend_one, images=images, slots=padded), "vision_attention", [True] * 10,
        [(False, shape(flat.shape)), (False, shape((used * images, four))), (False, shape((width, 3 * two))),
         (False, shape((16, width), F32)), token_out],
        [vmem(flat.shape), vmem((width, 3 * four)), *[vmem(v.shape) for v in lines],
         vmem((3 * four // 128, padded * images, 128), F32), vmem((four // 128, padded * images, 128), F32), dma((15,))],
        (flat, vision_project_in, *lines), after=(c0,),
    )
    a_send, b_send = fold(
        fold_a_zh_b_x, (a0, a1, a2, b0, b1), [shape((quarter, width)), shape((4 * unit, units_own))], (token,),
    )
    a3, b2 = hop(a_send, "zh"), hop(b_send, "x")
    vision_middle, token = kernel(
        partial(vision_attend_two, images=images, slots=padded), "vision_attention_rest", [False] * 4 + [True] * 2,
        [(False, shape(flat.shape, F32)), token_out],
        [vmem(flat.shape), vmem(vision_project_out.shape),
         vmem((3 * two // 128, padded * images, 128), F32), vmem((two // 128, padded * images, 128), F32), dma((2,))],
        (n1, context, win, vec, flat, vision_project_out), after=(a_send,),
    )

    def vision_second(begin, size, before, after):
        return kernel(
            partial(vision_expand, begin=begin * images), "vision_mlp",
            [False] * 4 + [True] * len(before),
            [(True, shape((used, images, width))), token_out],
            [vmem((size * images, width)), vmem((size * images, hidden)), vmem((size, images, width)), dma((1,))],
            (vision_middle, vec, vision_expand_weight, vision_reduce_weight) + before,
            aliases={4: 0} if before else None, after=after,
        )

    c_send, d_send, vectors = fold(
        fold_c, (c0, c1, d0, d1, vectors),
        [shape((4 * unit + 32, width)), shape((4 * unit, width)), shape((16, width), F32)], (token,),
    )
    c2, d2 = hop(c_send, "y"), hop(d_send, "x")
    first = (2 * used // 5 + 1) // 2 * 2
    vision_output, token = vision_second(0, first, (), (d_send,))

    a4, b_send = fold(
        fold_a_y_b_zl, (a0, a1, a2, a3, b0, b1, b2), [shape((quarter, width)), shape((2 * unit, units_own))], (token,),
    )
    a5, b3 = hop(a4, "y", lambda k, y: k != y), hop(b_send, "zl")
    second = (used - first) // 2
    vision_output, token = vision_second(first, second, (vision_output,), (a4,))

    a_own, b_send, e_send, vectors = fold(
        fold_a_b_zh_c_zl, (a4, a5, b0, b1, b2, b3, c0, c1, c2, d0, d1, d2, vectors),
        [shape((quarter, width)), shape((unit, units_own)), shape((2 * unit + 16, 2 * width)), shape((16, width), F32)],
        (token,),
    )
    b4, e3 = hop(b_send, "zh"), hop(e_send, "zl")
    vision_output, token = vision_second(first + second, used - first - second, (vision_output,), (a_own,))

    b_own, e_send, vectors = fold(
        fold_b_c_zh, (b0, b1, b2, b3, b4, c0, c1, c2, d0, d1, d2, e3, vectors),
        [shape((unit, units_own)), shape((unit + 16, 2 * width)), shape((16, width), F32)], (token,),
    )
    e4 = hop(e_send, "zh")
    (final,) = fold(
        fold_last, (b_own, c0, c1, c2, d0, d1, d2, e3, e4, vectors), [shape((2 * unit + 16, units_own))], (),
    )
    if low:
        groups = [list(range(i, i + (1 << low))) for i in range(0, ranks, 1 << low)]

        def scattered(value):
            return lax.psum_scatter(value, "dp", scatter_dimension=0, tiled=True, axis_index_groups=groups)

        a_own = scattered(a_own)
        total = final[2 * unit :].astype(F32)
        total = lax.psum(total[:, :width] + total[:, width:], "dp", axis_index_groups=groups)
        final = jnp.concatenate(
            [scattered(final[:unit]), scattered(final[unit : 2 * unit]), jnp.concatenate(high_low(total), axis=1)]
        )
    a_away = swap(a_own)
    away = swap(final)
    share = width // ranks
    sizes = [share] * 6 + [2 * share, 4 * share]
    reduce_grad, expand_grad, in_grad, out_grad, *shares, captions_gradient = kernel(
        partial(assemble, ranks=ranks), "assemble", [False] * 5 + [True],
        [(False, shape((4 * share, width), F32)), (False, shape((share, hidden), F32)),
         (False, shape((share, 3 * width), F32)), (False, shape((share, width), F32))]
        + [(False, shape((n,), F32)) for n in sizes] + [(True, shape((tokens, half)))],
        [dma((1,))], (a_own, a_away, final, away, cg_far, cg_half), (info,), aliases={6: 12},
    )
    return (
        jnp.transpose(vision_output, (1, 0, 2)), caption_output.reshape(count, slots, half),
        captions_gradient.reshape(count, slots, half),
        shares[0], shares[1], in_grad, shares[6], out_grad, shares[4],
        shares[2], shares[3], expand_grad, shares[7], reduce_grad, shares[5],
    )


def solution(mesh):
    spread_all = P(("section", "dp"), None, None)
    placed = (P("dp", None, None), P("dp"), P("dp", None, None)) + (P(),) * 12 + (spread_all,) + (P(),) * 12
    features = P("dp", None, "section")
    return jax.shard_map(
        on_device,
        mesh=mesh,
        in_specs=placed,
        out_specs=(
            spread_all, features, features,
            P("dp"), P("dp"), P("dp", None), P("dp"), P("dp", None), P("dp"),
            P("dp"), P("dp"), P("dp", None), P("dp"), P("dp", None), P("dp"),
        ),
        check_vma=False,
    )
```

```python
from functools import partial

import jax
import jax.experimental.pallas as pl
import jax.numpy as jnp
from jax import lax
from jax.experimental.pallas import tpu as pltpu
from jax.sharding import PartitionSpec as P

HEAD_DIM = 64
GROUP = 128
EPSILON = 1e-06
MASKED = -1000000000.0
ROOT = 0.7978845608028654
CUBIC = 0.044715
F32 = jnp.float32
BF16 = jnp.bfloat16
MIB = 1024 * 1024
COST = 1000000
COSTS = {
    "caption_attention": 8,
    "caption_mlp_forward": 11,
    "caption_mlp_backward": 6,
    "caption_mlp_weights": 4,
    "caption_attention_backward": 8,
    "caption_input_backward": 4,
    "caption_attention_weights": 5,
    "vision_attention": 7,
    "vision_attention_rest": 6,
    "vision_mlp": 4,
}
LIMITS = {
    "caption_attention": 14,
    "caption_mlp_forward": 18,
    "caption_mlp_backward": 14,
    "caption_mlp_weights": 16,
    "caption_attention_backward": 16,
    "caption_input_backward": 14,
    "caption_attention_weights": 14,
    "vision_attention": 26,
    "vision_attention_rest": 20,
    "vision_mlp": 16,
}


def nn(a, b):
    return lax.dot_general(a, b, (((1,), (0,)), ((), ())), preferred_element_type=F32)


def nt(a, b):
    return lax.dot_general(a, b, (((1,), (1,)), ((), ())), preferred_element_type=F32)


def tn(a, b):
    return lax.dot_general(a, b, (((0,), (0,)), ((), ())), preferred_element_type=F32)


def row(ref):
    return ref[...].astype(F32).reshape(1, -1)


def units(x):
    average = jnp.mean(x, axis=-1, keepdims=True)
    centred = x - average
    variance = jnp.mean(centred * centred, axis=-1, keepdims=True)
    inverse = lax.rsqrt(variance + EPSILON)
    return centred * inverse, inverse


def norm_back(unit, inverse, gain, dy):
    du = dy * gain
    first = jnp.mean(du, axis=-1, keepdims=True)
    second = jnp.mean(du * unit, axis=-1, keepdims=True)
    return (du - first - unit * second) * inverse


def lane_block(slots, rows):
    return lax.broadcasted_iota(jnp.int32, (rows, GROUP), 1) // slots


def two_heads(a):
    lanes = lax.broadcasted_iota(jnp.int32, a.shape, 1)
    low = (lanes < HEAD_DIM).astype(F32).astype(BF16)
    high = (lanes >= HEAD_DIM).astype(F32).astype(BF16)
    return jnp.concatenate([a * low, a * high], axis=0)


def compact(full, slots):
    block = lane_block(slots, slots)
    out = full[:slots]
    for b in range(1, GROUP // slots):
        out = jnp.where(block == b, full[b * slots : (b + 1) * slots], out)
    return out


def spread(part, slots):
    block = lane_block(slots, slots)
    return jnp.concatenate(
        [part * (block == b).astype(F32).astype(BF16) for b in range(GROUP // slots)], axis=0
    )


def attention(q, k, v, allowed, slots):
    scores = nt(two_heads(k), q)
    probs = []
    for a in range(2):
        s = compact(scores[a * GROUP : (a + 1) * GROUP], slots) * (HEAD_DIM**-0.5)
        s = jnp.where(allowed, s, MASKED)
        powered = jnp.exp(s - jnp.max(s, axis=0, keepdims=True))
        probs.append(powered / jnp.sum(powered, axis=0, keepdims=True))
    wide = jnp.concatenate([spread(p.astype(BF16), slots) for p in probs], axis=0)
    return tn(wide, two_heads(v)), probs


def attention_back(q, k, v, probs, dc, slots):
    vv, kk, qq, dd = two_heads(v), two_heads(k), two_heads(q), two_heads(dc)
    dprobs = nt(vv, dc)
    wide_p, wide_s = [], []
    for a in range(2):
        dp = compact(dprobs[a * GROUP : (a + 1) * GROUP], slots)
        p = probs[a]
        ds = p * (dp - jnp.sum(p * dp, axis=0, keepdims=True))
        wide_p.append(spread(p.astype(BF16), slots))
        wide_s.append(spread(ds.astype(BF16), slots))
    dv = nn(jnp.concatenate(wide_p, axis=1), dd)
    dk = nn(jnp.concatenate(wide_s, axis=1), qq)
    dq = tn(jnp.concatenate(wide_s, axis=0), kk)
    scale = HEAD_DIM**-0.5
    return (dq * scale).astype(BF16), (dk * scale).astype(BF16), dv.astype(BF16)


def fetch(pairs, sems, first=0):
    copies = [pltpu.make_async_copy(a, b, sems.at[first + i]) for i, (a, b) in enumerate(pairs)]
    for copy in copies:
        copy.start()
    return copies


def wait(copies):
    for copy in copies:
        copy.wait()


def part(number, size):
    return pl.ds(pl.multiple_of(number * size, size), size)


def thirds(win, held, width):
    return [(win.at[:, t * width : (t + 1) * width], held.at[:, t * width : (t + 1) * width]) for t in range(3)]


def choose(flag, a, b):
    return jnp.where(flag == 0, a, b)


def inward(n1, t, win, bias):
    width = n1.shape[1]
    out = nn(n1, win[:, t * width : (t + 1) * width])
    if t != 1:
        out = out + bias[:, t // 2 * width : (t // 2 + 1) * width]
    return out.astype(BF16)


def put_rows(lines, rows):
    width, at = rows.shape[1], 0
    for line in lines:
        for k in range(line.shape[0] // width):
            rows[at : at + 1] = line[k * width : (k + 1) * width].astype(F32).reshape(1, width)
            at += 1


def attend_forward(
    info, lens_hbm, x_hbm, cot_hbm, win_hbm, wo_hbm, we_hbm, wr_hbm, *refs, slots,
):
    small, refs = refs[:8], refs[8:]
    mid_ref, x, cot, win, wo, we, wr, vec, pk, pc, ctx_hbm, n1_hbm, *refs = refs
    lens, lines, ctx, n1, sems = refs[0], refs[1:9], *refs[9:]
    rows, width = x.shape
    first = fetch([(lens_hbm, lens), *zip(small, lines)], sems)
    copies = fetch([(x_hbm.at[part(info[0], rows)], x), *thirds(win_hbm, win, width), (wo_hbm, wo)], sems, 9)
    into, out_of = unit_parts(info, we_hbm, wr_hbm, we, wr)
    resident = fetch([*into, *out_of, (cot_hbm, cot)], sems, 14)
    wait(first)
    put_rows(lines, vec)
    copies[0].wait()
    unit, _ = units(x[...].astype(F32))
    n1[...] = (unit * vec[0:1] + vec[1:2]).astype(BF16)
    leaving = fetch([(n1, n1_hbm)], sems, 23)

    def project(held, wait_for):
        for t in range(3):
            if wait_for:
                copies[1 + t].wait()
            out = nn(n1[held], win[:, t * width : (t + 1) * width])
            if t != 1:
                out = out + vec[2 + t // 2 : 3 + t // 2]
            pk[held, t * width : (t + 1) * width] = out.astype(BF16)

    project(slice(0, rows // 2), True)
    block = lane_block(slots, 1)
    slot = lax.broadcasted_iota(jnp.int32, (slots, GROUP), 0)
    per = GROUP // slots
    start = info[0] * (rows // slots)
    for n in range(rows // GROUP):
        if n == rows // GROUP // 2:
            project(slice(rows // 2, rows), False)
        used = jnp.zeros((1, GROUP), jnp.int32)
        for b in range(per):
            used = jnp.where(block == b, lens[start + n * per + b], used)
        allowed = slot < used
        tokens = slice(n * GROUP, (n + 1) * GROUP)
        for p in range(width // 128):
            q, k, v = (pk[tokens, t * width + p * 128 : t * width + (p + 1) * 128] for t in range(3))
            out, probs = attention(q, k, v, allowed, slots)
            ctx[tokens, p * 128 : (p + 1) * 128] = out.astype(BF16)
            for a in range(2):
                pc[(2 * p + a) * slots : (2 * p + a + 1) * slots, tokens] = probs[a]
    leaving += fetch([(ctx, ctx_hbm)], sems, 24)
    copies[4].wait()
    mid_ref[...] = (x[...].astype(F32) + (nn(ctx[...], wo[...]) + vec[4:5])).astype(BF16)
    wait(leaving + resident)


def unit_parts(info, we_hbm, wr_hbm, we, wr):
    piece = we.shape[1] // 4
    first, second = [], []
    for z in range(4):
        held = slice(z * piece, (z + 1) * piece)
        begin = part(2 * z + info[0], piece)
        first.append((we_hbm.at[:, begin], we.at[:, held]))
        second.append((wr_hbm.at[begin], wr.at[held]))
    return first, second


def expand_forward(
    info, own_ref, oth_ref, cot, we, wr, vec, ctx_hbm, n1_hbm,
    n2_ref, slope_ref, keep_ref, send_ref, outk_ref, outs_ref, mid, act, sems, *, chunk,
):
    tokens, width = mid.shape
    count, half = own_ref.shape[0], width // 2
    c = info[0]
    across = []
    for k, (source, at) in enumerate(((ctx_hbm, 0), (ctx_hbm, half), (n1_hbm, 0), (n1_hbm, half))):
        held = outs_ref.at[tokens + k * count : tokens + (k + 1) * count]
        across += fetch([(source.at[:, at : at + half], held)], sems, k)
    mid[part(c, count)] = own_ref[...]
    mid[part(1 - c, count)] = oth_ref[...]
    bias = jnp.concatenate([choose(c, vec[z : z + 1, :half], vec[z : z + 1, half:]) for z in range(7, 11)], axis=1)
    over = choose(c, vec[11:12, :half], vec[11:12, half:])
    for t in range(0, tokens, chunk):
        old = mid[t : t + chunk].astype(F32)
        unit, _ = units(old)
        n2 = (unit * vec[5:6] + vec[6:7]).astype(BF16)
        n2_ref[t : t + chunk] = n2
        h = nn(n2, we[...]) + bias
        square = h * h
        gate = 0.5 + 0.5 * jnp.tanh(h * (ROOT + (ROOT * CUBIC) * square))
        active = h * gate
        slope = gate + active * (1.0 - gate) * (2.0 * ROOT + (6.0 * CUBIC * ROOT) * square)
        act[t : t + chunk] = active.astype(BF16)
        slope_ref[t : t + chunk] = slope.astype(BF16)
        out = nn(act[t : t + chunk], wr[...])
        outk_ref[t : t + chunk] = choose(c, old[:, :half], old[:, half:]) + (choose(c, out[:, :half], out[:, half:]) + over)
        outs_ref[t : t + chunk] = choose(c, out[:, half:], out[:, :half]).astype(BF16)
    piece = act.shape[1] // 4
    short = piece // 2
    for z in range(4):
        grad = tn(act[:, z * piece : (z + 1) * piece], cot[...])
        held = slice(z * short, (z + 1) * short)
        keep_ref[held] = choose(info[1], grad[:short], grad[short:]).astype(BF16)
        send_ref[held] = choose(info[1], grad[short:], grad[:short]).astype(BF16)
    wait(across)


def expand_backward(
    info, slope_ref, cot, we, wr, dh_ref, db_ref, dk_ref, ds_one, ds_two, acc, *, chunk,
):
    tokens, width = cot.shape
    count = dk_ref.shape[0]
    c = info[0]
    total = jnp.zeros((1, slope_ref.shape[1]), F32)
    for t in range(0, tokens, chunk):
        da = nt(cot[t : t + chunk], wr[...])
        dh = (da * slope_ref[t : t + chunk].astype(F32)).astype(BF16)
        dh_ref[t : t + chunk] = dh
        total = total + jnp.sum(dh.astype(F32), axis=0, keepdims=True)
        acc[t : t + chunk] = nt(dh_ref[t : t + chunk], we[...])
    db_ref[...] = total
    dk_ref[...] = acc[part(c, count)]
    ds_one[...] = acc[part(2 * (1 - c), count // 2)].astype(BF16)
    ds_two[...] = acc[part(2 * (1 - c) + 1, count // 2)].astype(BF16)


def split_rows(grad, first, second, bit, cols, short):
    for n in range(grad.shape[0] // (2 * short)):
        low = grad[2 * n * short : (2 * n + 1) * short]
        high = grad[(2 * n + 1) * short : (2 * n + 2) * short]
        first[n * short : (n + 1) * short, cols] = choose(bit, low, high).astype(BF16)
        second[n * short : (n + 1) * short, cols] = choose(bit, high, low).astype(BF16)


def expand_weights(info, n2_ref, dh_ref, outk_ref, far_ref, keep_ref, send_ref, out_ref):
    span = dh_ref.shape[1] // 2
    for j in range(2):
        cols = slice(j * span, (j + 1) * span)
        grad = tn(n2_ref[...], dh_ref[:, cols])
        split_rows(grad, keep_ref, send_ref, info[2], cols, grad.shape[0] // 8)
    out_ref[...] = (outk_ref[...] + far_ref[: out_ref.shape[0]].astype(F32)).astype(BF16)


def attend_backward(
    info, dn_ref, da_one, da_two, mid_ref, cot, vec, wo, pk, pc,
    dpk, mg_ref, s0, s1, sums_ref, dctx, *, slots,
):
    rows, width = mid_ref.shape
    half, wide = width // 2, 3 * width // 2
    c = info[0]
    cotf = cot[part(c, rows)].astype(F32)
    unit, inverse = units(mid_ref[...].astype(F32))
    dn = dn_ref[...] + jnp.concatenate([da_one[...], da_two[...]], axis=0).astype(F32)
    mf = (cotf + norm_back(unit, inverse, vec[5:6], dn)).astype(BF16)
    mg_ref[...] = mf

    def total(a):
        return jnp.sum(a, axis=0, keepdims=True)

    sums = [total(dn * unit), total(dn), total(mf.astype(F32)), total(cotf)]
    dctx[...] = nt(mf, wo[...]).astype(BF16)
    def one(n, carry):
        for tokens in (part(2 * n, GROUP), part(2 * n + 1, GROUP)):
            for p in range(width // 128):
                q, k, v = (pk[tokens, t * width + p * 128 : t * width + (p + 1) * 128] for t in range(3))
                probs = [pc[(2 * p + a) * slots : (2 * p + a + 1) * slots, tokens] for a in range(2)]
                grads = attention_back(q, k, v, probs, dctx[tokens, p * 128 : (p + 1) * 128], slots)
                for t in range(3):
                    dpk[tokens, t * width + p * 128 : t * width + (p + 1) * 128] = grads[t]
        return carry

    lax.fori_loop(0, rows // (2 * GROUP), one, 0)
    sums += [total(dpk[:, :width].astype(F32)), total(dpk[:, 2 * width :].astype(F32))]
    sums_ref[...] = jnp.concatenate(sums + [jnp.zeros((2, width), F32)], axis=0)

    def store(mine):
        s0[0 * rows : 1 * rows] = dpk[:, mine : mine + half]
        s0[1 * rows : 2 * rows] = dpk[:, mine + half : mine + width]
        s1[0 * rows : 1 * rows] = dpk[:, mine + width : mine + wide]
        s1[1 * rows : 2 * rows] = mg_ref[:, mine // 3 : mine // 3 + half]

    @pl.when(c == 0)
    def _():
        store(wide)

    @pl.when(c == 1)
    def _():
        store(0)


def high_low(v):
    high = v.astype(BF16)
    return high, (v - high.astype(F32)).astype(BF16)


def far_rows(far, k, rows):
    return jnp.concatenate([far[k * rows : (k + 1) * rows], far[(k + 1) * rows : (k + 2) * rows]], axis=1)


def attend_weights_one(info, dpk, n1_hbm, far, f0, vec, k1, t1, n1, sems):
    rows, half = dpk.shape[0], k1.shape[1] // 2
    copies = fetch([(n1_hbm, n1)], sems)
    short = k1.shape[0] // 8
    other = far_rows(far, 4, rows)
    for j in range(2):
        mine = dpk[:, pl.ds(pl.multiple_of(info[0] * 3 * half + j * half, 128), half)]
        grad = tn(other, f0[j * rows : (j + 1) * rows])
        if j == 0:
            wait(copies)
        grad = grad + tn(n1[...], mine)
        split_rows(grad, k1, t1, info[1], slice(j * half, (j + 1) * half), short)
    high, low = high_low(vec[...])
    t1[8 * short : 8 * short + 16] = high
    t1[8 * short + 16 :] = low


def attend_weights_two(
    info, dpk, mg, n1_hbm, ctx_hbm, far, f1, x_hbm, win_hbm, *refs,
):
    small, (k2, t2, x, win_one, win_two, lines_out, n1, ctx), refs = refs[:8], refs[8:16], refs[16:]
    lines, sems = refs[:8], refs[8]
    rows, half = dpk.shape[0], mg.shape[1] // 2
    c = info[0]
    copies = fetch([(n1_hbm, n1), (ctx_hbm, ctx)], sems)
    width = n1.shape[1]
    near = fetch([(x_hbm, x), *zip(small, lines)], sems, 2)
    near += fetch(some_columns(win_hbm, win_one, 0, width), sems, 11)
    near += fetch(some_columns(win_hbm, win_two, win_one.shape[1] // 3, width), sems, 14)
    short = k2.shape[0] // 4
    mine = dpk[:, pl.ds(pl.multiple_of(c * 3 * half + 2 * half, 128), half)]
    grad = tn(far_rows(far, 4, rows), f1[:rows])
    copies[0].wait()
    split_rows(grad + tn(n1[...], mine), k2, t2, info[2], slice(0, half), short)
    mine = mg[:, pl.ds(pl.multiple_of(c * half, 128), half)]
    grad = tn(far_rows(far, 2, rows), f1[rows:])
    copies[1].wait()
    split_rows(grad + tn(ctx[...], mine), k2, t2, info[2], slice(half, 2 * half), short)
    wait(near)
    put_rows(lines, lines_out)


def input_backward(
    info, x, vec, win, dpk, mg, sums_ref, db_ref, cg_hbm, cgs_ref, vec_ref, cgk, sems,
):
    rows, width = x.shape
    half = width // 2
    c = info[0]
    unit, inverse = units(x[...].astype(F32))
    dn = nt(dpk[...], win[...])
    out = norm_back(unit, inverse, vec[0:1], dn) + mg[...].astype(F32)
    cgk[...] = choose(c, out[:, :half], out[:, half:]).astype(BF16)
    leaving = fetch([(cgk, cg_hbm.at[part(c, rows)])], sems)
    cgs_ref[...] = choose(c, out[:, half:], out[:, :half]).astype(BF16)
    vec_ref[0:1] = jnp.sum(dn * unit, axis=0, keepdims=True)
    vec_ref[1:2] = jnp.sum(dn, axis=0, keepdims=True)
    vec_ref[2:8] = sums_ref[:6]
    flag = c.astype(F32)
    for z in range(4):
        one = db_ref[:, z * half : (z + 1) * half]
        vec_ref[8 + z : 9 + z, :half] = one * (1.0 - flag)
        vec_ref[8 + z : 9 + z, half:] = one * flag
    vec_ref[12:] = jnp.zeros((4, width), F32)
    wait(leaving)


def vision_heads(n1, win, bias, pk, ctx, images, slots):
    rows = n1.shape[0]
    some = win.shape[1] // 3
    across = some // 128
    pk[:, rows:] = jnp.zeros((pk.shape[0], pk.shape[1] - rows, 128), F32)
    for t in range(3):
        out = nn(n1[...], win[:, t * some : (t + 1) * some])
        if bias[t] is not None:
            out = out + bias[t]
        for p in range(across):
            pk[t * across + p, :rows] = out[:, p * 128 : (p + 1) * 128]
    allowed = lax.broadcasted_iota(jnp.int32, (slots, GROUP), 0) < rows // images
    per = GROUP // slots
    for i in range(0, images, per):
        for p in range(across):

            def load(t):
                parts = [pk[t * across + p, pl.ds(i + b, slots, stride=images)] for b in range(per)]
                return jnp.concatenate(parts, axis=0).astype(BF16)

            out, _ = attention(load(0), load(1), load(2), allowed, slots)
            for b in range(per):
                ctx[p, pl.ds(i + b, slots, stride=images)] = out[b * slots : (b + 1) * slots]
    return jnp.concatenate([ctx[p, :rows].astype(BF16) for p in range(across)], axis=1)


def some_columns(win_hbm, win, begin, width):
    some = win.shape[1] // 3
    return [(win_hbm.at[:, t * width + begin : t * width + begin + some], win.at[:, t * some : (t + 1) * some]) for t in range(3)]


def vision_attend_one(x, win, vec, n1_ref, ctx_ref, token, pk, ctx, *, images, slots):
    unit, _ = units(x[...].astype(F32))
    n1_ref[...] = (unit * vec[0:1] + vec[1:2]).astype(BF16)
    some = win.shape[1] // 3
    ctx_ref[...] = vision_heads(n1_ref, win, (vec[2:3, :some], None, vec[3:4, :some]), pk, ctx, images, slots)
    token[...] = jnp.zeros(token.shape, F32)


def vision_attend_two(
    n1_ref, ctx_ref, win, vec, x_hbm, wo_hbm, mid_ref, token, x, wo, pk, ctx, sems, *, images, slots,
):
    width = x.shape[1]
    some = win.shape[1] // 3
    copies = fetch([(x_hbm, x), (wo_hbm, wo)], sems)
    bias = (vec[2:3, width - some :], None, vec[3:4, width - some :])
    context = vision_heads(n1_ref, win, bias, pk, ctx, images, slots)
    context = jnp.concatenate([ctx_ref[...], context], axis=1)
    wait(copies)
    mid_ref[...] = x[...].astype(F32) + (nn(context, wo[...]) + vec[4:5])
    token[...] = jnp.zeros(token.shape, F32)


def vision_expand(mid_ref, vec, we, wr, *refs, begin):
    out_hbm, token, n2, act, out, sems = refs[-6:]
    rows, width = n2.shape
    images = out.shape[1]
    mid = mid_ref[begin : begin + rows]
    unit, _ = units(mid)
    n2[...] = (unit * vec[5:6] + vec[6:7]).astype(BF16)
    for f in range(we.shape[1] // width):
        cols = slice(f * width, (f + 1) * width)
        h = nn(n2[...], we[:, cols]) + vec[7 + f : 8 + f]
        gate = 0.5 + 0.5 * jnp.tanh(h * (ROOT + (ROOT * CUBIC) * (h * h)))
        act[:, cols] = (h * gate).astype(BF16)
    result = mid + (nn(act[...], wr[...]) + vec[11:12])
    out[...] = result.astype(BF16).reshape(out.shape)
    token[...] = jnp.zeros(token.shape, F32)
    wait(fetch([(out, out_hbm.at[begin // images : (begin + rows) // images])], sems))


def summed(parts, size, cols=slice(None)):
    total = None
    for ref, begin in parts:
        if not isinstance(begin, int):
            begin = pl.multiple_of(begin, 16)
        one = ref[pl.ds(begin, size), cols].astype(F32)
        total = one if total is None else total + one
    return total


def places(info):
    return info[1], info[2], info[3], info[4]


def fold_a_zl(info, a0, a1, a_out):
    x, y, zl, zh = places(info)
    size = a_out.shape[0] // 2
    for h in range(2):
        at = (2 * h + 1 - zl) * size
        a_out[h * size : (h + 1) * size] = summed([(a0, at), (a1, at)], size).astype(BF16)


def fold_a_zh_b_x(info, a0, a1, a2, b0, b1, a_out, b_out):
    x, y, zl, zh = places(info)
    size, unit = a_out.shape[0], b_out.shape[0] // 4
    at = (2 * (1 - zh) + zl) * size
    a_out[...] = summed([(a0, at), (a1, at), (a2, (1 - zh) * size)], size).astype(BF16)
    for z in range(4):
        at = (2 * z + 1 - x) * unit
        b_out[z * unit : (z + 1) * unit] = summed([(b0, at), (b1, at)], unit).astype(BF16)


def fold_c(info, c0, c1, d0, d1, vec, c_out, d_out, v_out):
    x, y, zl, zh = places(info)
    unit = d_out.shape[0] // 4
    for q in range(4):
        held = slice(q * unit, (q + 1) * unit)
        at = (2 * q + 1 - y) * unit
        c_out[held] = summed([(c0, at), (c1, at)], unit).astype(BF16)
        at = (2 * q + 1 - x) * unit
        d_out[held] = summed([(d0, at), (d1, at)], unit).astype(BF16)
    v = vec[...] + (c1[8 * unit : 8 * unit + 16].astype(F32) + c1[8 * unit + 16 :].astype(F32))
    v_out[...] = v
    c_out[4 * unit : 4 * unit + 16], c_out[4 * unit + 16 :] = high_low(v)


def fold_a_y_b_zl(info, a0, a1, a2, a3, b0, b1, b2, a_out, b_out):
    x, y, zl, zh = places(info)
    size, unit = a_out.shape[0], b_out.shape[0] // 2
    at = (2 * zh + zl) * size
    a_out[...] = summed([(a0, at), (a1, at), (a2, zh * size), (a3, 0)], size).astype(BF16)
    for h in range(2):
        z = 2 * h + 1 - zl
        at = (2 * z + x) * unit
        b_out[h * unit : (h + 1) * unit] = summed([(b0, at), (b1, at), (b2, z * unit)], unit).astype(BF16)


def fold_a_b_zh_c_zl(
    info, a4, a5, b0, b1, b2, b3, c0, c1, c2, d0, d1, d2, vec, a_out, b_out, e_out, v_out
):
    x, y, zl, zh = places(info)
    unit, width = b_out.shape[0], a_out.shape[1]
    a_out[...] = (a4[...].astype(F32) + a5[...].astype(F32)).astype(BF16)
    z = 2 * (1 - zh) + zl
    at = (2 * z + x) * unit
    b_out[...] = summed([(b0, at), (b1, at), (b2, z * unit), (b3, (1 - zh) * unit)], unit).astype(BF16)
    for h in range(2):
        held = slice(h * unit, (h + 1) * unit)
        q = 2 * h + 1 - zl
        at = (2 * q + y) * unit
        e_out[held, :width] = summed([(c0, at), (c1, at), (c2, q * unit)], unit).astype(BF16)
        at = (2 * q + x) * unit
        e_out[held, width:] = summed([(d0, at), (d1, at), (d2, q * unit)], unit).astype(BF16)
    v = vec[...] + (c2[4 * unit : 4 * unit + 16].astype(F32) + c2[4 * unit + 16 :].astype(F32))
    v_out[...] = v
    e_out[2 * unit :, :width], e_out[2 * unit :, width:] = high_low(v)


def fold_b_c_zh(info, b0, b1, b2, b3, b4, c0, c1, c2, d0, d1, d2, e3, vec, kept, e_out):
    x, y, zl, zh = places(info)
    unit, width = b4.shape[0], vec.shape[1]
    z = 2 * zh + zl
    at = (2 * z + x) * unit
    parts = [(b0, at), (b1, at), (b2, z * unit), (b3, zh * unit), (b4, 0)]
    kept[:unit] = summed(parts, unit).astype(BF16)
    settle(info, zh, c0, c1, c2, d0, d1, d2, [(e3, zh * unit)], kept, unit, unit)
    settle(info, 1 - zh, c0, c1, c2, d0, d1, d2, [(e3, (1 - zh) * unit)], e_out, 0, unit)
    v = vec[...] + (e3[2 * unit :, :width].astype(F32) + e3[2 * unit :, width:].astype(F32))
    high, low = high_low(v)
    kept[2 * unit :, :width], kept[2 * unit :, width:] = high, low
    e_out[unit:, :width], e_out[unit:, width:] = high, low


def settle(info, zh, c0, c1, c2, d0, d1, d2, more, out, begin, unit):
    x, y, zl, _ = places(info)
    width = out.shape[1] // 2
    q = 2 * zh + zl
    at = (2 * q + y) * unit
    first = summed([(c0, at), (c1, at), (c2, q * unit)], unit) + summed(more, unit, slice(0, width))
    at = (2 * q + x) * unit
    second = summed([(d0, at), (d1, at), (d2, q * unit)], unit) + summed(more, unit, slice(width, 2 * width))
    out[begin : begin + unit, :width] = first.astype(BF16)
    out[begin : begin + unit, width:] = second.astype(BF16)


def assemble(
    info, a_own, a_far, k_own, k_far, e_own, e_far, cg_far, cg_in, a_ref, b_ref, in_ref, out_ref, *refs, ranks
):
    vectors, (cg_hbm, sems) = refs[:8], refs[8:]
    c = info[0]
    rows = cg_far.shape[0]
    leaving = fetch([(cg_far, cg_hbm.at[part(1 - c, rows)])], sems)
    a_ref[...] = choose(c ^ info[2], a_own[...].astype(F32), a_far[...].astype(F32))
    share, hidden = b_ref.shape
    piece = hidden // 8
    wide, half = in_ref.shape[1] // 2, out_ref.shape[1] // 2
    mine, far = k_own[:share].astype(F32), k_far[:share].astype(F32)
    low, high = choose(c, mine, far), choose(c, far, mine)
    for z in range(4):
        held = slice(z * piece, (z + 1) * piece)
        b_ref[:, 2 * z * piece : (2 * z + 1) * piece] = low[:share, held]
        b_ref[:, (2 * z + 1) * piece : (2 * z + 2) * piece] = high[:share, held]
    mine = k_own[share : 2 * share].astype(F32) + e_own[:share].astype(F32)
    far = k_far[share : 2 * share].astype(F32) + e_far[:share].astype(F32)
    low, high = choose(c, mine, far), choose(c, far, mine)
    in_ref[:, :wide] = low[:, :wide]
    in_ref[:, wide:] = high[:, :wide]
    out_ref[:, :half] = low[:, wide:]
    out_ref[:, half:] = high[:, wide:]
    width = out_ref.shape[1]

    def both_halves(kept, last):
        kept, last = kept[2 * share :].astype(F32), last[share:].astype(F32)
        return (kept[:, :width] + kept[:, width:]) + (last[:, :width] + last[:, width:])

    total = both_halves(k_own, e_own) + both_halves(k_far, e_far)
    place = info[5]
    first = 0
    for ref, number in zip(vectors, (1, 1, 1, 1, 1, 1, 2, 4)):
        size = number * width // ranks
        offset = place * size
        which = offset // width
        taken = total[first : first + 1]
        for k in range(1, number):
            taken = jnp.where(which == k, total[first + k : first + k + 1], taken)
        turn = lax.rem(width - lax.rem(offset, width), width)
        turned = pltpu.roll(jnp.concatenate([taken] * 8, axis=0), turn, 1)
        ref[...] = turned[:1, :size].reshape(size)
        first += number
    wait(leaving)


def shape(dims, dtype=BF16):
    return jax.ShapeDtypeStruct(dims, dtype)


def whole(dims):
    return pl.BlockSpec(dims, lambda *_: (0,) * len(dims))


HBM = pl.BlockSpec(memory_space=pltpu.HBM)
NEAR = "near"
PLACES = {True: pltpu.HBM, NEAR: pltpu.VMEM}
FAR = pl.BlockSpec(memory_space=pl.ANY)


def kernel(body, name, ins, outs, scratch, args, scalars=(), aliases=None, after=()):
    first, extra = len(scalars) + len(args), len(after)

    def run(*refs):
        return body(*refs[:first], *refs[first + extra :])

    specs = pltpu.PrefetchScalarGridSpec(
        num_scalar_prefetch=len(scalars),
        grid=(1,),
        in_specs=[HBM if far is True else whole(a.shape) for far, a in zip(ins, args, strict=True)] + [FAR] * extra,
        out_specs=[HBM if far is True else whole(s.shape) for far, s in outs],
        scratch_shapes=scratch,
    )
    return pl.pallas_call(
        run,
        name=name,
        grid_spec=specs,
        out_shape=[PLACES[far](s.shape, s.dtype) if far else s for far, s in outs],
        compiler_params=pltpu.CompilerParams(
            vmem_limit_bytes=LIMITS.get(name, 16) * MIB, dimension_semantics=("arbitrary",)
        ),
        cost_estimate=pl.CostEstimate(flops=COSTS.get(name, 1) * COST, bytes_accessed=1000, transcendentals=0),
        input_output_aliases=aliases or {},
    )(*scalars, *(pltpu.with_memory_space_constraint(a, PLACES[far]) if far else a for far, a in zip(ins, args)), *after)


BITS = {"x": 0, "y": 1, "zl": 2, "zh": 3}


def on_device(
    captions, caption_lengths, caption_cotangent,
    first_gain, first_shift, project_in, inward_bias, project_out, outward_bias,
    second_gain, second_shift, expand_weight, expand_bias, reduce_weight, reduce_bias,
    patches,
    vision_first_gain, vision_first_shift, vision_project_in, vision_inward_bias, vision_project_out, vision_outward_bias,
    vision_second_gain, vision_second_shift, vision_expand_weight, vision_expand_bias, vision_reduce_weight, vision_reduce_bias,
):
    count, slots, width = captions.shape
    hidden = expand_weight.shape[1]
    tokens = count * slots
    own = tokens // 2
    half = width // 2
    units_own = hidden // 2
    heads = width // HEAD_DIM
    unit = width // 16
    quarter = hidden // 16
    ranks = lax.axis_size("dp")
    low = (ranks // 16).bit_length() - 1
    core = lax.axis_index("section")
    place = lax.axis_index("dp")
    info = jnp.stack([core] + [(place >> (low + b)) & 1 for b in range(4)] + [place]).astype(jnp.int32)
    x = captions.reshape(tokens, width)
    cot = caption_cotangent.reshape(tokens, width)
    dma = pltpu.SemaphoreType.DMA

    def hop(value, bit, only=None):
        step = 1 << (low + BITS[bit])
        pairs = []
        for k in range(2):
            for d in range(ranks):
                if only is None or only(k, (d >> (low + 1)) & 1):
                    pairs.append((k * ranks + d, k * ranks + (d ^ step)))
        return lax.ppermute(value, ("section", "dp"), pairs)

    def swap(value):
        return lax.ppermute(value, "section", [(0, 1), (1, 0)])

    def vmem(dims, dtype=BF16):
        return pltpu.VMEM(dims, dtype)

    line = vmem((width,))

    def fold(body, args, outs, after):
        return kernel(body, body.__name__, [False] * len(args), [(False, s) for s in outs], [], args, (info,), after=after)

    lines = (first_gain, first_shift, inward_bias, outward_bias, second_gain, second_shift, expand_bias, reduce_bias)
    near = [(own, width), (tokens, width), project_in.shape, project_out.shape, (width, units_own), (units_own, width)]
    middle, x_own, cot_near, win, wo, we, wr, vec, packed, probs, context, normed = kernel(
        partial(attend_forward, slots=slots), "caption_attention",
        [True] * 15,
        [(False, shape((own, width)))] + [(NEAR, shape(d)) for d in near] + [(NEAR, shape((16, width), F32))]
        + [(NEAR, shape((own, 3 * width))), (NEAR, shape((heads * slots, own), F32)),
           (True, shape((own, width))), (True, shape((own, width)))],
        [pltpu.SMEM(caption_lengths.shape, jnp.int32), *[vmem(v.shape) for v in lines], vmem((own, width)), vmem((own, width)), dma((25,))],
        (caption_lengths, x, cot, project_in, project_out, expand_weight, reduce_weight, *lines), (info,),
    )
    middle_far = swap(middle)

    n2, slope, a0, a_send, out_keep, out_send = kernel(
        partial(expand_forward, chunk=256), "caption_mlp_forward",
        [False] * 2 + [NEAR] * 4 + [True] * 2,
        [(False, shape((tokens, width))), (False, shape((tokens, units_own))),
         (False, shape((4 * quarter, width))), (False, shape((4 * quarter, width))),
         (False, shape((tokens, half), F32)), (False, shape((3 * tokens, half)))],
        [vmem((tokens, width)), vmem((tokens, units_own)), dma((4,))],
        (middle, middle_far, cot_near, we, wr, vec, context, normed), (info,),
    )
    a1 = hop(a_send, "x")
    out_far = swap(out_send)

    dh, db, dn_keep, dn_one, dn_two = kernel(
        partial(expand_backward, chunk=256), "caption_mlp_backward",
        [False] + [NEAR] * 3,
        [(False, shape((tokens, units_own))), (False, shape((1, units_own), F32)),
         (False, shape((own, width), F32)), (False, shape((own // 2, width))), (False, shape((own // 2, width)))],
        [vmem((tokens, width), F32)],
        (slope, cot_near, we, wr), (info,),
    )
    dn_one, dn_two = swap(dn_one), swap(dn_two)
    b0, b_send, caption_output = kernel(
        expand_weights, "caption_mlp_weights", [False] * 4,
        [(False, shape((8 * unit, units_own)))] * 2 + [(False, shape((tokens, half)))],
        [], (n2, dh, out_keep, out_far), (info,), after=(dn_keep,),
    )
    b1 = hop(b_send, "y")

    dpk, mg, *pieces, sums = kernel(
        partial(attend_backward, slots=slots), "caption_attention_backward",
        [False] * 4 + [NEAR] * 5,
        [(False, shape((own, 3 * width))), (False, shape((own, width)))]
        + [(False, shape((k * own, half))) for k in (2, 2)] + [(False, shape((8, width), F32))],
        [vmem((own, width))],
        (dn_keep, dn_one, dn_two, middle, cot_near, vec, wo, packed, probs),
        (info,), after=(b0,),
    )
    fars = [swap(p) for p in pieces]

    cg_half, cg_send, vectors = kernel(
        input_backward, "caption_input_backward",
        [NEAR] * 3 + [False] * 4,
        [(True, shape((tokens, half))), (False, shape((own, half))), (False, shape((16, width), F32))],
        [vmem((own, half)), dma((1,))],
        (x_own, vec, win, dpk, mg, sums, db), (info,),
    )
    cg_far = swap(cg_send)
    (a_send,) = fold(fold_a_zl, (a0, a1), [shape((2 * quarter, width))], (vectors,))
    a2 = hop(a_send, "zl")

    images, used, _ = patches.shape
    flat = jnp.transpose(patches, (1, 0, 2)).reshape(used * images, width)
    four = 2 * width // 3
    two = width - four
    lines = (vision_first_gain, vision_first_shift, vision_inward_bias, vision_outward_bias,
             vision_second_gain, vision_second_shift, vision_expand_bias, vision_reduce_bias)
    c0, c_send = kernel(
        attend_weights_one, "caption_attention_weights", [False, True, False, False, False],
        [(False, shape((8 * unit, width))), (False, shape((8 * unit + 32, width)))],
        [vmem((own, width)), dma((1,))],
        (dpk, normed, out_far, fars[0], vectors), (info,), after=(a_send,),
    )
    c1 = hop(c_send, "x")
    d0, d_send, flat_near, win_one, win, vec = kernel(
        attend_weights_two, "caption_attention_weights", [False] * 2 + [True] * 2 + [False] * 2 + [True] * 10,
        [(False, shape((8 * unit, width))), (False, shape((8 * unit, width))),
         (False, shape(flat.shape)), (False, shape((width, 3 * four))), (False, shape((width, 3 * two))), (False, shape((16, width), F32))],
        [vmem((own, width)), vmem((own, width)), *[vmem(v.shape) for v in lines], dma((17,))],
        (dpk, mg, normed, context, out_far, fars[1], flat, vision_project_in, *lines), (info,), after=(c0,),
    )
    d1 = hop(d_send, "y")

    padded = 64
    token_out = (False, shape((8, 128), F32))
    n1, context, token = kernel(
        partial(vision_attend_one, images=images, slots=padded), "vision_attention", [False] * 3,
        [(False, shape(flat.shape)), (False, shape((used * images, four))), token_out],
        [vmem((3 * four // 128, padded * images, 128), F32), vmem((four // 128, padded * images, 128), F32)],
        (flat_near, win_one, vec), after=(d0,),
    )
    a_send, b_send = fold(
        fold_a_zh_b_x, (a0, a1, a2, b0, b1), [shape((quarter, width)), shape((4 * unit, units_own))], (token,),
    )
    a3, b2 = hop(a_send, "zh"), hop(b_send, "x")
    vision_middle, token = kernel(
        partial(vision_attend_two, images=images, slots=padded), "vision_attention_rest", [False] * 4 + [True] * 2,
        [(False, shape(flat.shape, F32)), token_out],
        [vmem(flat.shape), vmem(vision_project_out.shape),
         vmem((3 * two // 128, padded * images, 128), F32), vmem((two // 128, padded * images, 128), F32), dma((2,))],
        (n1, context, win, vec, flat, vision_project_out), after=(a_send,),
    )

    def vision_second(begin, size, before, after):
        return kernel(
            partial(vision_expand, begin=begin * images), "vision_mlp",
            [False] * 4 + [True] * len(before),
            [(True, shape((used, images, width))), token_out],
            [vmem((size * images, width)), vmem((size * images, hidden)), vmem((size, images, width)), dma((1,))],
            (vision_middle, vec, vision_expand_weight, vision_reduce_weight) + before,
            aliases={4: 0} if before else None, after=after,
        )

    c_send, d_send, vectors = fold(
        fold_c, (c0, c1, d0, d1, vectors),
        [shape((4 * unit + 32, width)), shape((4 * unit, width)), shape((16, width), F32)], (token,),
    )
    c2, d2 = hop(c_send, "y"), hop(d_send, "x")
    first = (2 * used // 5 + 1) // 2 * 2
    vision_output, token = vision_second(0, first, (), (d_send,))

    a4, b_send = fold(
        fold_a_y_b_zl, (a0, a1, a2, a3, b0, b1, b2), [shape((quarter, width)), shape((2 * unit, units_own))], (token,),
    )
    a5, b3 = hop(a4, "y", lambda k, y: k != y), hop(b_send, "zl")
    second = (used - first) // 2
    vision_output, token = vision_second(first, second, (vision_output,), (a4,))

    a_own, b_send, e_send, vectors = fold(
        fold_a_b_zh_c_zl, (a4, a5, b0, b1, b2, b3, c0, c1, c2, d0, d1, d2, vectors),
        [shape((quarter, width)), shape((unit, units_own)), shape((2 * unit + 16, 2 * width)), shape((16, width), F32)],
        (token,),
    )
    b4, e3 = hop(b_send, "zh"), hop(e_send, "zl")
    vision_output, token = vision_second(first + second, used - first - second, (vision_output,), (a_own,))

    kept, e_send = fold(
        fold_b_c_zh, (b0, b1, b2, b3, b4, c0, c1, c2, d0, d1, d2, e3, vectors),
        [shape((2 * unit + 16, units_own)), shape((unit + 16, 2 * width))], (token,),
    )
    e4 = hop(e_send, "zh")
    if low:
        groups = [list(range(i, i + (1 << low))) for i in range(0, ranks, 1 << low)]

        def scattered(value):
            return lax.psum_scatter(value, "dp", scatter_dimension=0, tiled=True, axis_index_groups=groups)

        def reduced(value):
            total = value.astype(F32)
            total = lax.psum(total[:, :width] + total[:, width:], "dp", axis_index_groups=groups)
            return jnp.concatenate(high_low(total), axis=1)

        a_own = scattered(a_own)
        kept = jnp.concatenate([scattered(kept[:unit]), scattered(kept[unit : 2 * unit]), reduced(kept[2 * unit :])])
        e4 = jnp.concatenate([scattered(e4[:unit]), reduced(e4[unit:])])
    a_away, kept_away, away = swap(a_own), swap(kept), swap(e4)
    share = width // ranks
    sizes = [share] * 6 + [2 * share, 4 * share]
    reduce_grad, expand_grad, in_grad, out_grad, *shares, captions_gradient = kernel(
        partial(assemble, ranks=ranks), "assemble", [False] * 7 + [True],
        [(False, shape((4 * share, width), F32)), (False, shape((share, hidden), F32)),
         (False, shape((share, 3 * width), F32)), (False, shape((share, width), F32))]
        + [(False, shape((n,), F32)) for n in sizes] + [(True, shape((tokens, half)))],
        [dma((1,))], (a_own, a_away, kept, kept_away, e4, away, cg_far, cg_half), (info,), aliases={8: 12},
    )
    return (
        jnp.transpose(vision_output, (1, 0, 2)), caption_output.reshape(count, slots, half),
        captions_gradient.reshape(count, slots, half),
        shares[0], shares[1], in_grad, shares[6], out_grad, shares[4],
        shares[2], shares[3], expand_grad, shares[7], reduce_grad, shares[5],
    )


def solution(mesh):
    spread_all = P(("section", "dp"), None, None)
    placed = (P("dp", None, None), P("dp"), P("dp", None, None)) + (P(),) * 12 + (spread_all,) + (P(),) * 12
    features = P("dp", None, "section")
    return jax.shard_map(
        on_device,
        mesh=mesh,
        in_specs=placed,
        out_specs=(
            spread_all, features, features,
            P("dp"), P("dp"), P("dp", None), P("dp"), P("dp", None), P("dp"),
            P("dp"), P("dp"), P("dp", None), P("dp"), P("dp", None), P("dp"),
        ),
        check_vma=False,
    )
```

```python
from functools import partial

import jax
import jax.experimental.pallas as pl
import jax.numpy as jnp
from jax import lax
from jax.experimental.pallas import tpu as pltpu
from jax.sharding import PartitionSpec as P

HEAD_DIM = 64
GROUP = 128
EPSILON = 1e-06
MASKED = -1000000000.0
ROOT = 0.7978845608028654
CUBIC = 0.044715
F32 = jnp.float32
BF16 = jnp.bfloat16
MIB = 1024 * 1024
COST = 1000000
COSTS = {
    "caption_attention": 8,
    "caption_mlp_forward": 11,
    "caption_mlp_backward": 6,
    "caption_mlp_weights": 4,
    "caption_attention_backward": 8,
    "caption_input_backward": 4,
    "caption_attention_weights": 5,
    "vision_attention": 7,
    "vision_attention_rest": 6,
    "vision_mlp": 4,
}
LIMITS = {
    "caption_attention": 14,
    "caption_mlp_forward": 18,
    "caption_mlp_backward": 14,
    "caption_mlp_weights": 16,
    "caption_attention_backward": 16,
    "caption_input_backward": 14,
    "caption_attention_weights": 14,
    "vision_attention": 26,
    "vision_attention_rest": 20,
    "vision_mlp": 16,
}


def nn(a, b):
    return lax.dot_general(a, b, (((1,), (0,)), ((), ())), preferred_element_type=F32)


def nt(a, b):
    return lax.dot_general(a, b, (((1,), (1,)), ((), ())), preferred_element_type=F32)


def tn(a, b):
    return lax.dot_general(a, b, (((0,), (0,)), ((), ())), preferred_element_type=F32)


def row(ref):
    return ref[...].astype(F32).reshape(1, -1)


def units(x):
    average = jnp.mean(x, axis=-1, keepdims=True)
    centred = x - average
    variance = jnp.mean(centred * centred, axis=-1, keepdims=True)
    inverse = lax.rsqrt(variance + EPSILON)
    return centred * inverse, inverse


def norm_back(unit, inverse, gain, dy):
    du = dy * gain
    first = jnp.mean(du, axis=-1, keepdims=True)
    second = jnp.mean(du * unit, axis=-1, keepdims=True)
    return (du - first - unit * second) * inverse


def lane_block(slots, rows):
    return lax.broadcasted_iota(jnp.int32, (rows, GROUP), 1) // slots


def two_heads(a):
    lanes = lax.broadcasted_iota(jnp.int32, a.shape, 1)
    low = (lanes < HEAD_DIM).astype(F32).astype(BF16)
    high = (lanes >= HEAD_DIM).astype(F32).astype(BF16)
    return jnp.concatenate([a * low, a * high], axis=0)


def compact(full, slots):
    block = lane_block(slots, slots)
    out = full[:slots]
    for b in range(1, GROUP // slots):
        out = jnp.where(block == b, full[b * slots : (b + 1) * slots], out)
    return out


def spread(part, slots):
    block = lane_block(slots, slots)
    return jnp.concatenate(
        [part * (block == b).astype(F32).astype(BF16) for b in range(GROUP // slots)], axis=0
    )


def attention(q, k, v, allowed, slots):
    scores = nt(two_heads(k), q)
    probs = []
    for a in range(2):
        s = compact(scores[a * GROUP : (a + 1) * GROUP], slots) * (HEAD_DIM**-0.5)
        s = jnp.where(allowed, s, MASKED)
        powered = jnp.exp(s - jnp.max(s, axis=0, keepdims=True))
        probs.append(powered / jnp.sum(powered, axis=0, keepdims=True))
    wide = jnp.concatenate([spread(p.astype(BF16), slots) for p in probs], axis=0)
    return tn(wide, two_heads(v)), probs


def attention_back(q, k, v, probs, dc, slots):
    vv, kk, qq, dd = two_heads(v), two_heads(k), two_heads(q), two_heads(dc)
    dprobs = nt(vv, dc)
    wide_p, wide_s = [], []
    for a in range(2):
        dp = compact(dprobs[a * GROUP : (a + 1) * GROUP], slots)
        p = probs[a]
        ds = p * (dp - jnp.sum(p * dp, axis=0, keepdims=True))
        wide_p.append(spread(p.astype(BF16), slots))
        wide_s.append(spread(ds.astype(BF16), slots))
    dv = nn(jnp.concatenate(wide_p, axis=1), dd)
    dk = nn(jnp.concatenate(wide_s, axis=1), qq)
    dq = tn(jnp.concatenate(wide_s, axis=0), kk)
    scale = HEAD_DIM**-0.5
    return (dq * scale).astype(BF16), (dk * scale).astype(BF16), dv.astype(BF16)


def fetch(pairs, sems, first=0):
    copies = [pltpu.make_async_copy(a, b, sems.at[first + i]) for i, (a, b) in enumerate(pairs)]
    for copy in copies:
        copy.start()
    return copies


def wait(copies):
    for copy in copies:
        copy.wait()


def part(number, size):
    return pl.ds(pl.multiple_of(number * size, size), size)


def thirds(win, held, width):
    return [(win.at[:, t * width : (t + 1) * width], held.at[:, t * width : (t + 1) * width]) for t in range(3)]


def choose(flag, a, b):
    return jnp.where(flag == 0, a, b)


def inward(n1, t, win, bias):
    width = n1.shape[1]
    out = nn(n1, win[:, t * width : (t + 1) * width])
    if t != 1:
        out = out + bias[:, t // 2 * width : (t // 2 + 1) * width]
    return out.astype(BF16)


def put_rows(lines, rows):
    width, at = rows.shape[1], 0
    for line in lines:
        for k in range(line.shape[0] // width):
            rows[at : at + 1] = line[k * width : (k + 1) * width].astype(F32).reshape(1, width)
            at += 1


def attend_forward(
    info, lens_hbm, x_hbm, cot_hbm, win_hbm, wo_hbm, we_hbm, wr_hbm, *refs, slots,
):
    small, refs = refs[:8], refs[8:]
    mid_ref, x, cot, win, wo, we, wr, vec, pk, pc, ctx_hbm, n1_hbm, *refs = refs
    lens, lines, ctx, n1, sems = refs[0], refs[1:9], *refs[9:]
    rows, width = x.shape
    first = fetch([(lens_hbm, lens), *zip(small, lines)], sems)
    copies = fetch([(x_hbm.at[part(info[0], rows)], x), *thirds(win_hbm, win, width), (wo_hbm, wo)], sems, 9)
    into, out_of = unit_parts(info, we_hbm, wr_hbm, we, wr)
    resident = fetch([*into, *out_of, (cot_hbm, cot)], sems, 14)
    wait(first)
    put_rows(lines, vec)
    copies[0].wait()
    unit, _ = units(x[...].astype(F32))
    n1[...] = (unit * vec[0:1] + vec[1:2]).astype(BF16)
    leaving = fetch([(n1, n1_hbm)], sems, 23)

    def project(held, wait_for):
        for t in range(3):
            if wait_for:
                copies[1 + t].wait()
            out = nn(n1[held], win[:, t * width : (t + 1) * width])
            if t != 1:
                out = out + vec[2 + t // 2 : 3 + t // 2]
            pk[held, t * width : (t + 1) * width] = out.astype(BF16)

    project(slice(0, rows // 2), True)
    block = lane_block(slots, 1)
    slot = lax.broadcasted_iota(jnp.int32, (slots, GROUP), 0)
    per = GROUP // slots
    start = info[0] * (rows // slots)
    for n in range(rows // GROUP):
        if n == rows // GROUP // 2:
            project(slice(rows // 2, rows), False)
        used = jnp.zeros((1, GROUP), jnp.int32)
        for b in range(per):
            used = jnp.where(block == b, lens[start + n * per + b], used)
        allowed = slot < used
        tokens = slice(n * GROUP, (n + 1) * GROUP)
        for p in range(width // 128):
            q, k, v = (pk[tokens, t * width + p * 128 : t * width + (p + 1) * 128] for t in range(3))
            out, probs = attention(q, k, v, allowed, slots)
            ctx[tokens, p * 128 : (p + 1) * 128] = out.astype(BF16)
            for a in range(2):
                pc[(2 * p + a) * slots : (2 * p + a + 1) * slots, tokens] = probs[a]
    leaving += fetch([(ctx, ctx_hbm)], sems, 24)
    copies[4].wait()
    mid_ref[...] = (x[...].astype(F32) + (nn(ctx[...], wo[...]) + vec[4:5])).astype(BF16)
    wait(leaving + resident)


def unit_parts(info, we_hbm, wr_hbm, we, wr):
    piece = we.shape[1] // 4
    first, second = [], []
    for z in range(4):
        held = slice(z * piece, (z + 1) * piece)
        begin = part(2 * z + info[0], piece)
        first.append((we_hbm.at[:, begin], we.at[:, held]))
        second.append((wr_hbm.at[begin], wr.at[held]))
    return first, second


def expand_forward(
    info, own_ref, oth_ref, cot, we, wr, vec, ctx_hbm, n1_hbm,
    n2_ref, slope_ref, keep_ref, send_ref, outk_ref, outs_ref, mid, act, sems, *, chunk,
):
    tokens, width = mid.shape
    count, half = own_ref.shape[0], width // 2
    c = info[0]
    across = []
    for k, (source, at) in enumerate(((ctx_hbm, 0), (ctx_hbm, half), (n1_hbm, 0), (n1_hbm, half))):
        held = outs_ref.at[tokens + k * count : tokens + (k + 1) * count]
        across += fetch([(source.at[:, at : at + half], held)], sems, k)
    mid[part(c, count)] = own_ref[...]
    mid[part(1 - c, count)] = oth_ref[...]
    bias = jnp.concatenate([choose(c, vec[z : z + 1, :half], vec[z : z + 1, half:]) for z in range(7, 11)], axis=1)
    over = choose(c, vec[11:12, :half], vec[11:12, half:])
    for t in range(0, tokens, chunk):
        old = mid[t : t + chunk].astype(F32)
        unit, _ = units(old)
        n2 = (unit * vec[5:6] + vec[6:7]).astype(BF16)
        n2_ref[t : t + chunk] = n2
        h = nn(n2, we[...]) + bias
        square = h * h
        gate = 0.5 + 0.5 * jnp.tanh(h * (ROOT + (ROOT * CUBIC) * square))
        active = h * gate
        slope = gate + active * (1.0 - gate) * (2.0 * ROOT + (6.0 * CUBIC * ROOT) * square)
        act[t : t + chunk] = active.astype(BF16)
        slope_ref[t : t + chunk] = slope.astype(BF16)
        out = nn(act[t : t + chunk], wr[...])
        outk_ref[t : t + chunk] = choose(c, old[:, :half], old[:, half:]) + (choose(c, out[:, :half], out[:, half:]) + over)
        outs_ref[t : t + chunk] = choose(c, out[:, half:], out[:, :half]).astype(BF16)
    piece = act.shape[1] // 4
    short = piece // 2
    for z in range(4):
        grad = tn(act[:, z * piece : (z + 1) * piece], cot[...])
        held = slice(z * short, (z + 1) * short)
        keep_ref[held] = choose(info[1], grad[:short], grad[short:]).astype(BF16)
        send_ref[held] = choose(info[1], grad[short:], grad[:short]).astype(BF16)
    wait(across)


def expand_backward(
    info, slope_ref, cot, we, wr, dh_ref, db_ref, dk_ref, ds_one, ds_two, acc, *, chunk,
):
    tokens, width = cot.shape
    count = dk_ref.shape[0]
    c = info[0]
    total = jnp.zeros((1, slope_ref.shape[1]), F32)
    for t in range(0, tokens, chunk):
        da = nt(cot[t : t + chunk], wr[...])
        dh = (da * slope_ref[t : t + chunk].astype(F32)).astype(BF16)
        dh_ref[t : t + chunk] = dh
        total = total + jnp.sum(dh.astype(F32), axis=0, keepdims=True)
        acc[t : t + chunk] = nt(dh_ref[t : t + chunk], we[...])
    db_ref[...] = total
    dk_ref[...] = acc[part(c, count)]
    ds_one[...] = acc[part(2 * (1 - c), count // 2)].astype(BF16)
    ds_two[...] = acc[part(2 * (1 - c) + 1, count // 2)].astype(BF16)


def split_rows(grad, first, second, bit, cols, short):
    for n in range(grad.shape[0] // (2 * short)):
        low = grad[2 * n * short : (2 * n + 1) * short]
        high = grad[(2 * n + 1) * short : (2 * n + 2) * short]
        first[n * short : (n + 1) * short, cols] = choose(bit, low, high).astype(BF16)
        second[n * short : (n + 1) * short, cols] = choose(bit, high, low).astype(BF16)


def expand_weights(info, n2_ref, dh_ref, outk_ref, far_ref, keep_ref, send_ref, out_ref):
    span = dh_ref.shape[1] // 2
    for j in range(2):
        cols = slice(j * span, (j + 1) * span)
        grad = tn(n2_ref[...], dh_ref[:, cols])
        split_rows(grad, keep_ref, send_ref, info[2], cols, grad.shape[0] // 8)
    out_ref[...] = (outk_ref[...] + far_ref[: out_ref.shape[0]].astype(F32)).astype(BF16)


def attend_backward(
    info, dn_ref, da_one, da_two, mid_ref, cot, vec, wo, pk, pc,
    dpk, mg_ref, s0, s1, sums_ref, dctx, *, slots,
):
    rows, width = mid_ref.shape
    half, wide = width // 2, 3 * width // 2
    c = info[0]
    cotf = cot[part(c, rows)].astype(F32)
    unit, inverse = units(mid_ref[...].astype(F32))
    dn = dn_ref[...] + jnp.concatenate([da_one[...], da_two[...]], axis=0).astype(F32)
    mf = (cotf + norm_back(unit, inverse, vec[5:6], dn)).astype(BF16)
    mg_ref[...] = mf

    def total(a):
        return jnp.sum(a, axis=0, keepdims=True)

    sums = [total(dn * unit), total(dn), total(mf.astype(F32)), total(cotf)]
    dctx[...] = nt(mf, wo[...]).astype(BF16)
    def one(n, carry):
        for tokens in (part(2 * n, GROUP), part(2 * n + 1, GROUP)):
            for p in range(width // 128):
                q, k, v = (pk[tokens, t * width + p * 128 : t * width + (p + 1) * 128] for t in range(3))
                probs = [pc[(2 * p + a) * slots : (2 * p + a + 1) * slots, tokens] for a in range(2)]
                grads = attention_back(q, k, v, probs, dctx[tokens, p * 128 : (p + 1) * 128], slots)
                for t in range(3):
                    dpk[tokens, t * width + p * 128 : t * width + (p + 1) * 128] = grads[t]
        return carry

    lax.fori_loop(0, rows // (2 * GROUP), one, 0)
    sums += [total(dpk[:, :width].astype(F32)), total(dpk[:, 2 * width :].astype(F32))]
    sums_ref[...] = jnp.concatenate(sums + [jnp.zeros((2, width), F32)], axis=0)

    def store(mine):
        s0[0 * rows : 1 * rows] = dpk[:, mine : mine + half]
        s0[1 * rows : 2 * rows] = dpk[:, mine + half : mine + width]
        s1[0 * rows : 1 * rows] = dpk[:, mine + width : mine + wide]
        s1[1 * rows : 2 * rows] = mg_ref[:, mine // 3 : mine // 3 + half]

    @pl.when(c == 0)
    def _():
        store(wide)

    @pl.when(c == 1)
    def _():
        store(0)


def high_low(v):
    high = v.astype(BF16)
    return high, (v - high.astype(F32)).astype(BF16)


def far_rows(far, k, rows):
    return jnp.concatenate([far[k * rows : (k + 1) * rows], far[(k + 1) * rows : (k + 2) * rows]], axis=1)


def attend_weights_one(info, dpk, n1_hbm, far, f0, vec, k1, t1, n1, sems):
    rows, half = dpk.shape[0], k1.shape[1] // 2
    copies = fetch([(n1_hbm, n1)], sems)
    short = k1.shape[0] // 8
    other = far_rows(far, 4, rows)
    for j in range(2):
        mine = dpk[:, pl.ds(pl.multiple_of(info[0] * 3 * half + j * half, 128), half)]
        grad = tn(other, f0[j * rows : (j + 1) * rows])
        if j == 0:
            wait(copies)
        grad = grad + tn(n1[...], mine)
        split_rows(grad, k1, t1, info[1], slice(j * half, (j + 1) * half), short)
    high, low = high_low(vec[...])
    t1[8 * short : 8 * short + 16] = high
    t1[8 * short + 16 :] = low


def attend_weights_two(
    info, dpk, mg, n1_hbm, ctx_hbm, far, f1, x_hbm, win_hbm, *refs,
):
    small, (k2, t2, x, win_one, win_two, lines_out, n1, ctx), refs = refs[:8], refs[8:16], refs[16:]
    lines, sems = refs[:8], refs[8]
    rows, half = dpk.shape[0], mg.shape[1] // 2
    c = info[0]
    copies = fetch([(n1_hbm, n1), (ctx_hbm, ctx)], sems)
    width = n1.shape[1]
    near = fetch([(x_hbm, x), *zip(small, lines)], sems, 2)
    near += fetch(some_columns(win_hbm, win_one, 0, width), sems, 11)
    near += fetch(some_columns(win_hbm, win_two, win_one.shape[1] // 3, width), sems, 14)
    short = k2.shape[0] // 4
    mine = dpk[:, pl.ds(pl.multiple_of(c * 3 * half + 2 * half, 128), half)]
    grad = tn(far_rows(far, 4, rows), f1[:rows])
    copies[0].wait()
    split_rows(grad + tn(n1[...], mine), k2, t2, info[2], slice(0, half), short)
    mine = mg[:, pl.ds(pl.multiple_of(c * half, 128), half)]
    grad = tn(far_rows(far, 2, rows), f1[rows:])
    copies[1].wait()
    split_rows(grad + tn(ctx[...], mine), k2, t2, info[2], slice(half, 2 * half), short)
    wait(near)
    put_rows(lines, lines_out)


def input_backward(
    info, x, vec, win, dpk, mg, sums_ref, db_ref, cg_hbm, cgs_ref, vec_ref, cgk, sems,
):
    rows, width = x.shape
    half = width // 2
    c = info[0]
    unit, inverse = units(x[...].astype(F32))
    dn = nt(dpk[...], win[...])
    out = norm_back(unit, inverse, vec[0:1], dn) + mg[...].astype(F32)
    cgk[...] = choose(c, out[:, :half], out[:, half:]).astype(BF16)
    leaving = fetch([(cgk, cg_hbm.at[part(c, rows)])], sems)
    cgs_ref[...] = choose(c, out[:, half:], out[:, :half]).astype(BF16)
    vec_ref[0:1] = jnp.sum(dn * unit, axis=0, keepdims=True)
    vec_ref[1:2] = jnp.sum(dn, axis=0, keepdims=True)
    vec_ref[2:8] = sums_ref[:6]
    flag = c.astype(F32)
    for z in range(4):
        one = db_ref[:, z * half : (z + 1) * half]
        vec_ref[8 + z : 9 + z, :half] = one * (1.0 - flag)
        vec_ref[8 + z : 9 + z, half:] = one * flag
    vec_ref[12:] = jnp.zeros((4, width), F32)
    wait(leaving)


def vision_heads(n1, win, bias, pk, ctx, images, slots):
    rows = n1.shape[0]
    some = win.shape[1] // 3
    across = some // 128
    pk[:, rows:] = jnp.zeros((pk.shape[0], pk.shape[1] - rows, 128), F32)
    for t in range(3):
        out = nn(n1[...], win[:, t * some : (t + 1) * some])
        if bias[t] is not None:
            out = out + bias[t]
        for p in range(across):
            pk[t * across + p, :rows] = out[:, p * 128 : (p + 1) * 128]
    allowed = lax.broadcasted_iota(jnp.int32, (slots, GROUP), 0) < rows // images
    per = GROUP // slots
    for i in range(0, images, per):
        for p in range(across):

            def load(t):
                parts = [pk[t * across + p, pl.ds(i + b, slots, stride=images)] for b in range(per)]
                return jnp.concatenate(parts, axis=0).astype(BF16)

            out, _ = attention(load(0), load(1), load(2), allowed, slots)
            for b in range(per):
                ctx[p, pl.ds(i + b, slots, stride=images)] = out[b * slots : (b + 1) * slots]
    return jnp.concatenate([ctx[p, :rows].astype(BF16) for p in range(across)], axis=1)


def some_columns(win_hbm, win, begin, width):
    some = win.shape[1] // 3
    return [(win_hbm.at[:, t * width + begin : t * width + begin + some], win.at[:, t * some : (t + 1) * some]) for t in range(3)]


def vision_attend_one(x, win, vec, n1_ref, ctx_ref, token, pk, ctx, *, images, slots):
    unit, _ = units(x[...].astype(F32))
    n1_ref[...] = (unit * vec[0:1] + vec[1:2]).astype(BF16)
    some = win.shape[1] // 3
    ctx_ref[...] = vision_heads(n1_ref, win, (vec[2:3, :some], None, vec[3:4, :some]), pk, ctx, images, slots)
    token[...] = jnp.zeros(token.shape, F32)


def vision_attend_two(
    n1_ref, ctx_ref, win, vec, x_hbm, wo_hbm, mid_ref, token, x, wo, pk, ctx, sems, *, images, slots,
):
    width = x.shape[1]
    some = win.shape[1] // 3
    copies = fetch([(x_hbm, x), (wo_hbm, wo)], sems)
    bias = (vec[2:3, width - some :], None, vec[3:4, width - some :])
    context = vision_heads(n1_ref, win, bias, pk, ctx, images, slots)
    context = jnp.concatenate([ctx_ref[...], context], axis=1)
    wait(copies)
    mid_ref[...] = x[...].astype(F32) + (nn(context, wo[...]) + vec[4:5])
    token[...] = jnp.zeros(token.shape, F32)


def vision_expand(mid_ref, vec, we, wr, *refs, begin):
    out_hbm, token, n2, act, out, sems = refs[-6:]
    rows, width = n2.shape
    images = out.shape[1]
    mid = mid_ref[begin : begin + rows]
    unit, _ = units(mid)
    n2[...] = (unit * vec[5:6] + vec[6:7]).astype(BF16)
    for f in range(we.shape[1] // width):
        cols = slice(f * width, (f + 1) * width)
        h = nn(n2[...], we[:, cols]) + vec[7 + f : 8 + f]
        gate = 0.5 + 0.5 * jnp.tanh(h * (ROOT + (ROOT * CUBIC) * (h * h)))
        act[:, cols] = (h * gate).astype(BF16)
    result = mid + (nn(act[...], wr[...]) + vec[11:12])
    out[...] = result.astype(BF16).reshape(out.shape)
    token[...] = jnp.zeros(token.shape, F32)
    wait(fetch([(out, out_hbm.at[begin // images : (begin + rows) // images])], sems))


def summed(parts, size, cols=slice(None)):
    total = None
    for ref, begin in parts:
        if not isinstance(begin, int):
            begin = pl.multiple_of(begin, 16)
        one = ref[pl.ds(begin, size), cols].astype(F32)
        total = one if total is None else total + one
    return total


def places(info):
    return info[1], info[2], info[3], info[4]


def fold_a_zl(info, a0, a1, a_out):
    x, y, zl, zh = places(info)
    size = a_out.shape[0] // 2
    for h in range(2):
        at = (2 * h + 1 - zl) * size
        a_out[h * size : (h + 1) * size] = summed([(a0, at), (a1, at)], size).astype(BF16)


def fold_a_zh_b_x(info, a0, a1, a2, b0, b1, a_out, b_out):
    x, y, zl, zh = places(info)
    size, unit = a_out.shape[0], b_out.shape[0] // 4
    at = (2 * (1 - zh) + zl) * size
    a_out[...] = summed([(a0, at), (a1, at), (a2, (1 - zh) * size)], size).astype(BF16)
    for z in range(4):
        at = (2 * z + 1 - x) * unit
        b_out[z * unit : (z + 1) * unit] = summed([(b0, at), (b1, at)], unit).astype(BF16)


def fold_c(info, c0, c1, d0, d1, vec, c_out, d_out, v_out):
    x, y, zl, zh = places(info)
    unit = d_out.shape[0] // 4
    for q in range(4):
        held = slice(q * unit, (q + 1) * unit)
        at = (2 * q + 1 - y) * unit
        c_out[held] = summed([(c0, at), (c1, at)], unit).astype(BF16)
        at = (2 * q + 1 - x) * unit
        d_out[held] = summed([(d0, at), (d1, at)], unit).astype(BF16)
    v = vec[...] + (c1[8 * unit : 8 * unit + 16].astype(F32) + c1[8 * unit + 16 :].astype(F32))
    v_out[...] = v
    c_out[4 * unit : 4 * unit + 16], c_out[4 * unit + 16 :] = high_low(v)


def fold_a_y_b_zl(info, a0, a1, a2, a3, b0, b1, b2, a_out, b_out):
    x, y, zl, zh = places(info)
    size, unit = a_out.shape[0], b_out.shape[0] // 2
    at = (2 * zh + zl) * size
    a_out[...] = summed([(a0, at), (a1, at), (a2, zh * size), (a3, 0)], size).astype(BF16)
    for h in range(2):
        z = 2 * h + 1 - zl
        at = (2 * z + x) * unit
        b_out[h * unit : (h + 1) * unit] = summed([(b0, at), (b1, at), (b2, z * unit)], unit).astype(BF16)


def fold_a_b_zh_c_zl(
    info, a4, a5, b0, b1, b2, b3, c0, c1, c2, d0, d1, d2, vec, a_out, b_out, e_out, v_out
):
    x, y, zl, zh = places(info)
    unit, width = b_out.shape[0], a_out.shape[1]
    a_out[...] = (a4[...].astype(F32) + a5[...].astype(F32)).astype(BF16)
    z = 2 * (1 - zh) + zl
    at = (2 * z + x) * unit
    b_out[...] = summed([(b0, at), (b1, at), (b2, z * unit), (b3, (1 - zh) * unit)], unit).astype(BF16)
    for h in range(2):
        held = slice(h * unit, (h + 1) * unit)
        q = 2 * h + 1 - zl
        at = (2 * q + y) * unit
        e_out[held, :width] = summed([(c0, at), (c1, at), (c2, q * unit)], unit).astype(BF16)
        at = (2 * q + x) * unit
        e_out[held, width:] = summed([(d0, at), (d1, at), (d2, q * unit)], unit).astype(BF16)
    v = vec[...] + (c2[4 * unit : 4 * unit + 16].astype(F32) + c2[4 * unit + 16 :].astype(F32))
    v_out[...] = v
    e_out[2 * unit :, :width], e_out[2 * unit :, width:] = high_low(v)


def fold_b_c_zh(info, b0, b1, b2, b3, b4, c0, c1, c2, d0, d1, d2, e3, vec, kept, e_out):
    x, y, zl, zh = places(info)
    unit, width = b4.shape[0], vec.shape[1]
    z = 2 * zh + zl
    at = (2 * z + x) * unit
    parts = [(b0, at), (b1, at), (b2, z * unit), (b3, zh * unit), (b4, 0)]
    kept[:unit] = summed(parts, unit).astype(BF16)
    settle(info, zh, c0, c1, c2, d0, d1, d2, [(e3, zh * unit)], kept, unit, unit)
    settle(info, 1 - zh, c0, c1, c2, d0, d1, d2, [(e3, (1 - zh) * unit)], e_out, 0, unit)
    v = vec[...] + (e3[2 * unit :, :width].astype(F32) + e3[2 * unit :, width:].astype(F32))
    high, low = high_low(v)
    kept[2 * unit :, :width], kept[2 * unit :, width:] = high, low
    e_out[unit:, :width], e_out[unit:, width:] = high, low


def settle(info, zh, c0, c1, c2, d0, d1, d2, more, out, begin, unit):
    x, y, zl, _ = places(info)
    width = out.shape[1] // 2
    q = 2 * zh + zl
    at = (2 * q + y) * unit
    first = summed([(c0, at), (c1, at), (c2, q * unit)], unit) + summed(more, unit, slice(0, width))
    at = (2 * q + x) * unit
    second = summed([(d0, at), (d1, at), (d2, q * unit)], unit) + summed(more, unit, slice(width, 2 * width))
    out[begin : begin + unit, :width] = first.astype(BF16)
    out[begin : begin + unit, width:] = second.astype(BF16)


def assemble(
    info, a_own, a_far, k_own, k_far, e_own, e_far, cg_far, cg_in, a_ref, b_ref, in_ref, out_ref, *refs, ranks
):
    vectors, (cg_hbm, sems) = refs[:8], refs[8:]
    c = info[0]
    rows = cg_far.shape[0]
    leaving = fetch([(cg_far, cg_hbm.at[part(1 - c, rows)])], sems)
    a_ref[...] = choose(c ^ info[2], a_own[...].astype(F32), a_far[...].astype(F32))
    share, hidden = b_ref.shape
    piece = hidden // 8
    wide, half = in_ref.shape[1] // 2, out_ref.shape[1] // 2
    mine, far = k_own[:share].astype(F32), k_far[:share].astype(F32)
    low, high = choose(c, mine, far), choose(c, far, mine)
    for z in range(4):
        held = slice(z * piece, (z + 1) * piece)
        b_ref[:, 2 * z * piece : (2 * z + 1) * piece] = low[:share, held]
        b_ref[:, (2 * z + 1) * piece : (2 * z + 2) * piece] = high[:share, held]
    mine = k_own[share : 2 * share].astype(F32) + e_own[:share].astype(F32)
    far = k_far[share : 2 * share].astype(F32) + e_far[:share].astype(F32)
    low, high = choose(c, mine, far), choose(c, far, mine)
    in_ref[:, :wide] = low[:, :wide]
    in_ref[:, wide:] = high[:, :wide]
    out_ref[:, :half] = low[:, wide:]
    out_ref[:, half:] = high[:, wide:]
    width = out_ref.shape[1]

    def both_halves(kept, last):
        kept, last = kept[2 * share :].astype(F32), last[share:].astype(F32)
        return (kept[:, :width] + kept[:, width:]) + (last[:, :width] + last[:, width:])

    total = both_halves(k_own, e_own) + both_halves(k_far, e_far)
    place = info[5]
    first = 0
    for ref, number in zip(vectors, (1, 1, 1, 1, 1, 1, 2, 4)):
        size = number * width // ranks
        offset = place * size
        which = offset // width
        taken = total[first : first + 1]
        for k in range(1, number):
            taken = jnp.where(which == k, total[first + k : first + k + 1], taken)
        turn = lax.rem(width - lax.rem(offset, width), width)
        turned = pltpu.roll(jnp.concatenate([taken] * 8, axis=0), turn, 1)
        ref[...] = turned[:1, :size].reshape(size)
        first += number
    wait(leaving)


def shape(dims, dtype=BF16):
    return jax.ShapeDtypeStruct(dims, dtype)


def whole(dims):
    return pl.BlockSpec(dims, lambda *_: (0,) * len(dims))


HBM = pl.BlockSpec(memory_space=pltpu.HBM)
NEAR = "near"
PLACES = {True: pltpu.HBM, NEAR: pltpu.VMEM}
FAR = pl.BlockSpec(memory_space=pl.ANY)


def kernel(body, name, ins, outs, scratch, args, scalars=(), aliases=None, after=()):
    first, extra = len(scalars) + len(args), len(after)

    def run(*refs):
        return body(*refs[:first], *refs[first + extra :])

    specs = pltpu.PrefetchScalarGridSpec(
        num_scalar_prefetch=len(scalars),
        grid=(1,),
        in_specs=[HBM if far is True else whole(a.shape) for far, a in zip(ins, args, strict=True)] + [FAR] * extra,
        out_specs=[HBM if far is True else whole(s.shape) for far, s in outs],
        scratch_shapes=scratch,
    )
    return pl.pallas_call(
        run,
        name=name,
        grid_spec=specs,
        out_shape=[PLACES[far](s.shape, s.dtype) if far else s for far, s in outs],
        compiler_params=pltpu.CompilerParams(
            vmem_limit_bytes=LIMITS.get(name, 16) * MIB, dimension_semantics=("arbitrary",)
        ),
        cost_estimate=pl.CostEstimate(flops=COSTS.get(name, 1) * COST, bytes_accessed=1000, transcendentals=0),
        input_output_aliases=aliases or {},
    )(*scalars, *(pltpu.with_memory_space_constraint(a, PLACES[far]) if far else a for far, a in zip(ins, args)), *after)


BITS = {"x": 0, "y": 1, "zl": 2, "zh": 3}


def on_device(
    captions, caption_lengths, caption_cotangent,
    first_gain, first_shift, project_in, inward_bias, project_out, outward_bias,
    second_gain, second_shift, expand_weight, expand_bias, reduce_weight, reduce_bias,
    patches,
    vision_first_gain, vision_first_shift, vision_project_in, vision_inward_bias, vision_project_out, vision_outward_bias,
    vision_second_gain, vision_second_shift, vision_expand_weight, vision_expand_bias, vision_reduce_weight, vision_reduce_bias,
):
    count, slots, width = captions.shape
    hidden = expand_weight.shape[1]
    tokens = count * slots
    own = tokens // 2
    half = width // 2
    units_own = hidden // 2
    heads = width // HEAD_DIM
    unit = width // 16
    quarter = hidden // 16
    ranks = lax.axis_size("dp")
    low = (ranks // 16).bit_length() - 1
    core = lax.axis_index("section")
    place = lax.axis_index("dp")
    info = jnp.stack([core] + [(place >> (low + b)) & 1 for b in range(4)] + [place]).astype(jnp.int32)
    x = captions.reshape(tokens, width)
    cot = caption_cotangent.reshape(tokens, width)
    dma = pltpu.SemaphoreType.DMA

    def hop(value, bit, only=None):
        step = 1 << (low + BITS[bit])
        pairs = []
        for k in range(2):
            for d in range(ranks):
                if only is None or only(k, (d >> (low + 1)) & 1):
                    pairs.append((k * ranks + d, k * ranks + (d ^ step)))
        return lax.ppermute(value, ("section", "dp"), pairs)

    def swap(value):
        return lax.ppermute(value, "section", [(0, 1), (1, 0)])

    def vmem(dims, dtype=BF16):
        return pltpu.VMEM(dims, dtype)

    line = vmem((width,))

    def fold(body, args, outs, after):
        return kernel(body, body.__name__, [False] * len(args), [(False, s) for s in outs], [], args, (info,), after=after)

    lines = (first_gain, first_shift, inward_bias, outward_bias, second_gain, second_shift, expand_bias, reduce_bias)
    near = [(own, width), (tokens, width), project_in.shape, project_out.shape, (width, units_own), (units_own, width)]
    middle, x_own, cot_near, win, wo, we, wr, vec, packed, probs, context, normed = kernel(
        partial(attend_forward, slots=slots), "caption_attention",
        [True] * 15,
        [(False, shape((own, width)))] + [(NEAR, shape(d)) for d in near] + [(NEAR, shape((16, width), F32))]
        + [(NEAR, shape((own, 3 * width))), (NEAR, shape((heads * slots, own), F32)),
           (True, shape((own, width))), (True, shape((own, width)))],
        [pltpu.SMEM(caption_lengths.shape, jnp.int32), *[vmem(v.shape) for v in lines], vmem((own, width)), vmem((own, width)), dma((25,))],
        (caption_lengths, x, cot, project_in, project_out, expand_weight, reduce_weight, *lines), (info,),
    )
    middle_far = swap(middle)

    n2, slope, a0, a_send, out_keep, out_send = kernel(
        partial(expand_forward, chunk=256), "caption_mlp_forward",
        [False] * 2 + [NEAR] * 4 + [True] * 2,
        [(False, shape((tokens, width))), (False, shape((tokens, units_own))),
         (False, shape((4 * quarter, width))), (False, shape((4 * quarter, width))),
         (False, shape((tokens, half), F32)), (False, shape((3 * tokens, half)))],
        [vmem((tokens, width)), vmem((tokens, units_own)), dma((4,))],
        (middle, middle_far, cot_near, we, wr, vec, context, normed), (info,),
    )
    a1 = hop(a_send, "x")
    out_far = swap(out_send)

    dh, db, dn_keep, dn_one, dn_two = kernel(
        partial(expand_backward, chunk=256), "caption_mlp_backward",
        [False] + [NEAR] * 3,
        [(False, shape((tokens, units_own))), (False, shape((1, units_own), F32)),
         (False, shape((own, width), F32)), (False, shape((own // 2, width))), (False, shape((own // 2, width)))],
        [vmem((tokens, width), F32)],
        (slope, cot_near, we, wr), (info,),
    )
    dn_one, dn_two = swap(dn_one), swap(dn_two)
    b0, b_send, caption_output = kernel(
        expand_weights, "caption_mlp_weights", [False] * 4,
        [(False, shape((8 * unit, units_own)))] * 2 + [(False, shape((tokens, half)))],
        [], (n2, dh, out_keep, out_far), (info,), after=(dn_keep,),
    )
    b1 = hop(b_send, "y")

    dpk, mg, *pieces, sums = kernel(
        partial(attend_backward, slots=slots), "caption_attention_backward",
        [False] * 4 + [NEAR] * 5,
        [(False, shape((own, 3 * width))), (False, shape((own, width)))]
        + [(False, shape((k * own, half))) for k in (2, 2)] + [(False, shape((8, width), F32))],
        [vmem((own, width))],
        (dn_keep, dn_one, dn_two, middle, cot_near, vec, wo, packed, probs),
        (info,), after=(b0,),
    )
    fars = [swap(p) for p in pieces]

    cg_half, cg_send, vectors = kernel(
        input_backward, "caption_input_backward",
        [NEAR] * 3 + [False] * 4,
        [(True, shape((tokens, half))), (False, shape((own, half))), (False, shape((16, width), F32))],
        [vmem((own, half)), dma((1,))],
        (x_own, vec, win, dpk, mg, sums, db), (info,),
    )
    cg_far = swap(cg_send)
    (a_send,) = fold(fold_a_zl, (a0, a1), [shape((2 * quarter, width))], (vectors,))
    a2 = hop(a_send, "zl")

    images, used, _ = patches.shape
    flat = jnp.transpose(patches, (1, 0, 2)).reshape(used * images, width)
    four = 2 * width // 3
    two = width - four
    lines = (vision_first_gain, vision_first_shift, vision_inward_bias, vision_outward_bias,
             vision_second_gain, vision_second_shift, vision_expand_bias, vision_reduce_bias)
    c0, c_send = kernel(
        attend_weights_one, "caption_attention_weights", [False, True, False, False, False],
        [(False, shape((8 * unit, width))), (False, shape((8 * unit + 32, width)))],
        [vmem((own, width)), dma((1,))],
        (dpk, normed, out_far, fars[0], vectors), (info,), after=(a_send,),
    )
    c1 = hop(c_send, "x")
    d0, d_send, flat_near, win_one, win, vec = kernel(
        attend_weights_two, "caption_attention_weights", [False] * 2 + [True] * 2 + [False] * 2 + [True] * 10,
        [(False, shape((8 * unit, width))), (False, shape((8 * unit, width))),
         (False, shape(flat.shape)), (False, shape((width, 3 * four))), (False, shape((width, 3 * two))), (False, shape((16, width), F32))],
        [vmem((own, width)), vmem((own, width)), *[vmem(v.shape) for v in lines], dma((17,))],
        (dpk, mg, normed, context, out_far, fars[1], flat, vision_project_in, *lines), (info,), after=(c0,),
    )
    d1 = hop(d_send, "y")

    padded = 64
    token_out = (False, shape((8, 128), F32))
    n1, context, token = kernel(
        partial(vision_attend_one, images=images, slots=padded), "vision_attention", [False] * 3,
        [(False, shape(flat.shape)), (False, shape((used * images, four))), token_out],
        [vmem((3 * four // 128, (padded + 1) * images, 128), F32), vmem((four // 128, (padded + 1) * images, 128), F32)],
        (flat_near, win_one, vec), after=(d0,),
    )
    a_send, b_send = fold(
        fold_a_zh_b_x, (a0, a1, a2, b0, b1), [shape((quarter, width)), shape((4 * unit, units_own))], (token,),
    )
    a3, b2 = hop(a_send, "zh"), hop(b_send, "x")
    vision_middle, token = kernel(
        partial(vision_attend_two, images=images, slots=padded), "vision_attention_rest", [False] * 4 + [True] * 2,
        [(False, shape(flat.shape, F32)), token_out],
        [vmem(flat.shape), vmem(vision_project_out.shape),
         vmem((3 * two // 128, (padded + 1) * images, 128), F32), vmem((two // 128, (padded + 1) * images, 128), F32), dma((2,))],
        (n1, context, win, vec, flat, vision_project_out), after=(a_send,),
    )

    def vision_second(begin, size, before, after):
        return kernel(
            partial(vision_expand, begin=begin * images), "vision_mlp",
            [False] * 4 + [True] * len(before),
            [(True, shape((used, images, width))), token_out],
            [vmem((size * images, width)), vmem((size * images, hidden)), vmem((size, images, width)), dma((1,))],
            (vision_middle, vec, vision_expand_weight, vision_reduce_weight) + before,
            aliases={4: 0} if before else None, after=after,
        )

    c_send, d_send, vectors = fold(
        fold_c, (c0, c1, d0, d1, vectors),
        [shape((4 * unit + 32, width)), shape((4 * unit, width)), shape((16, width), F32)], (token,),
    )
    c2, d2 = hop(c_send, "y"), hop(d_send, "x")
    first = (2 * used // 5 + 1) // 2 * 2
    vision_output, token = vision_second(0, first, (), (d_send,))

    a4, b_send = fold(
        fold_a_y_b_zl, (a0, a1, a2, a3, b0, b1, b2), [shape((quarter, width)), shape((2 * unit, units_own))], (token,),
    )
    a5, b3 = hop(a4, "y", lambda k, y: k != y), hop(b_send, "zl")
    second = (used - first) // 2
    vision_output, token = vision_second(first, second, (vision_output,), (a4,))

    a_own, b_send, e_send, vectors = fold(
        fold_a_b_zh_c_zl, (a4, a5, b0, b1, b2, b3, c0, c1, c2, d0, d1, d2, vectors),
        [shape((quarter, width)), shape((unit, units_own)), shape((2 * unit + 16, 2 * width)), shape((16, width), F32)],
        (token,),
    )
    b4, e3 = hop(b_send, "zh"), hop(e_send, "zl")
    vision_output, token = vision_second(first + second, used - first - second, (vision_output,), (a_own,))

    kept, e_send = fold(
        fold_b_c_zh, (b0, b1, b2, b3, b4, c0, c1, c2, d0, d1, d2, e3, vectors),
        [shape((2 * unit + 16, units_own)), shape((unit + 16, 2 * width))], (token,),
    )
    e4 = hop(e_send, "zh")
    if low:
        groups = [list(range(i, i + (1 << low))) for i in range(0, ranks, 1 << low)]

        def scattered(value):
            return lax.psum_scatter(value, "dp", scatter_dimension=0, tiled=True, axis_index_groups=groups)

        def reduced(value):
            total = value.astype(F32)
            total = lax.psum(total[:, :width] + total[:, width:], "dp", axis_index_groups=groups)
            return jnp.concatenate(high_low(total), axis=1)

        a_own = scattered(a_own)
        kept = jnp.concatenate([scattered(kept[:unit]), scattered(kept[unit : 2 * unit]), reduced(kept[2 * unit :])])
        e4 = jnp.concatenate([scattered(e4[:unit]), reduced(e4[unit:])])
    a_away, kept_away, away = swap(a_own), swap(kept), swap(e4)
    share = width // ranks
    sizes = [share] * 6 + [2 * share, 4 * share]
    reduce_grad, expand_grad, in_grad, out_grad, *shares, captions_gradient = kernel(
        partial(assemble, ranks=ranks), "assemble", [False] * 7 + [True],
        [(False, shape((4 * share, width), F32)), (False, shape((share, hidden), F32)),
         (False, shape((share, 3 * width), F32)), (False, shape((share, width), F32))]
        + [(False, shape((n,), F32)) for n in sizes] + [(True, shape((tokens, half)))],
        [dma((1,))], (a_own, a_away, kept, kept_away, e4, away, cg_far, cg_half), (info,), aliases={8: 12},
    )
    return (
        jnp.transpose(vision_output, (1, 0, 2)), caption_output.reshape(count, slots, half),
        captions_gradient.reshape(count, slots, half),
        shares[0], shares[1], in_grad, shares[6], out_grad, shares[4],
        shares[2], shares[3], expand_grad, shares[7], reduce_grad, shares[5],
    )


def solution(mesh):
    spread_all = P(("section", "dp"), None, None)
    placed = (P("dp", None, None), P("dp"), P("dp", None, None)) + (P(),) * 12 + (spread_all,) + (P(),) * 12
    features = P("dp", None, "section")
    return jax.shard_map(
        on_device,
        mesh=mesh,
        in_specs=placed,
        out_specs=(
            spread_all, features, features,
            P("dp"), P("dp"), P("dp", None), P("dp"), P("dp", None), P("dp"),
            P("dp"), P("dp"), P("dp", None), P("dp"), P("dp", None), P("dp"),
        ),
        check_vma=False,
    )
```
